32 devices in a mesh: dp: 8 (over y, x, core), tp: 4 (over z).
Axes of the slice: x: 2, y: 2, z: 4, core: 2. Of those that a mesh axis runs over, the one named last changes fastest.
Arguments:
- tokens: bfloat16 [4096, 768], P('dp'), may hold values from -6 to 6
- cotangent: bfloat16 [4096, 768], P('dp'), may hold values from -6 to 6
- norm1_gain: float32 [768], replicated, may hold values from 0.1 to 1.9
- w_input: bfloat16 [768, 768], P(None, 'tp'), may hold values from -0.21875 to 0.21875
- w_forget: bfloat16 [768, 384], P(None, 'tp'), may hold values from -0.21875 to 0.21875
- w_outgate: bfloat16 [768, 768], P(None, 'tp'), may hold values from -0.21875 to 0.21875
- forget_gap: float32 [384], P('tp'), may hold values from 0.0001 to 0.05
- phase_angle: float32 [384], P('tp'), may hold values from -3.140625 to 3.140625
- group_gain: float32 [768], P('tp'), may hold values from 0.1 to 1.9
- w_mix: bfloat16 [768, 768], P('tp'), may hold values from -0.21875 to 0.21875
- norm2_gain: float32 [768], replicated, may hold values from 0.1 to 1.9
- w_gate: bfloat16 [768, 1536], P(None, 'tp'), may hold values from -0.21875 to 0.21875
- w_up: bfloat16 [768, 1536], P(None, 'tp'), may hold values from -0.21875 to 0.21875
- w_down: bfloat16 [1536, 768], P('tp'), may hold values from -0.15625 to 0.15625
Outputs:
- mixed: bfloat16 [4096, 768], P('dp')
- token_grad: float32 [4096, 768], P('dp')
- grad_norm1: float32 [768], replicated
- grad_input: float32 [768, 768], P(None, 'tp')
- grad_forget: float32 [768, 384], P(None, 'tp')
- grad_outgate: float32 [768, 768], P(None, 'tp')
- grad_gap: float32 [384], P('tp')
- grad_phase: float32 [384], P('tp')
- grad_group: float32 [768], P('tp')
- grad_mix: float32 [768, 768], P('tp')
- grad_norm2: float32 [768], replicated
- grad_gate: float32 [768, 1536], P(None, 'tp')
- grad_up: float32 [768, 1536], P(None, 'tp')
- grad_down: float32 [1536, 768], P('tp')
The draws below stay inside these ranges and needn't reach their ends.
All inputs are finite; a program needn't handle non-finite values.
Results may differ from the reference program's by a relative error of at most 0.0085.
The reference program's roundings to bfloat16 on the way (of `low_in`, `low_mix`, `low_mid` and `hidden`) count: a program that leaves them out, or rounds other values in their place, can miss the bound.
Values may be sent and summed in bfloat16 or wider, within the bound.
A program may use at most 128 MiB of HBM per device.

```python
import math
import jax
import jax.numpy as jnp
from jax import lax

D = 768
C = 384
FF = 1536
GROUP = 64
TOKENS = 4096


def levels(own_key, dims, cuts, low, high):
    level = 1.0
    for axis_at, blocks in cuts:
        steps = jax.random.uniform(jax.random.fold_in(jax.random.fold_in(own_key, 6), axis_at), (blocks,), jnp.float32, low / len(cuts), high / len(cuts))
        level = level * jnp.repeat(jnp.exp(steps), dims[axis_at] // blocks).reshape((-1,) + (1,) * (len(dims) - 1 - axis_at))
    return level


def noise(rng, extent, width, bound, shards=(), dtype=jnp.bfloat16):
    factor_of = levels(rng, extent, shards, -0.22, 0.18) if shards else 1.0
    result = jax.random.normal(rng, extent, jnp.float32) * width * factor_of
    return jnp.minimum(jnp.maximum(result, -bound), bound).astype(dtype)


def setup_inputs(seed: int = 0) -> dict:
    key_list = jax.random.split(jax.random.key(seed), 15)
    return {
        "tokens": noise(key_list[0], (TOKENS, D), 1.0, 6.0, ((0, 8),)),
        "cotangent": noise(key_list[1], (TOKENS, D), 1.0, 6.0, ((0, 8),)),
        "norm1_gain": jnp.clip(1.0 + 0.18 * jax.random.normal(key_list[2], (D,), jnp.float32), 0.1, 1.9),
        "w_input": noise(key_list[3], (D, 2 * C), D ** -0.5, 0.21875, ((1, 4),)),
        "w_forget": noise(key_list[4], (D, C), D ** -0.5, 0.21875, ((1, 4),)),
        "w_outgate": noise(key_list[5], (D, 2 * C), D ** -0.5, 0.21875, ((1, 4),)),
        "forget_gap": jnp.clip(jnp.exp(math.log(0.05) - 6.214608 * jax.random.uniform(key_list[6], (C,), jnp.float32) ** levels(key_list[6], (C,), ((0, 4),), -0.2, 0.2)), 0.0001, 0.05),
        "phase_angle": jnp.clip(jax.random.uniform(key_list[7], (C,), jnp.float32, -3.140625, 3.140625), -3.140625, 3.140625),
        "group_gain": jnp.clip(1.0 + 0.18 * jax.random.normal(key_list[8], (2 * C,), jnp.float32), 0.1, 1.9),
        "w_mix": noise(key_list[9], (2 * C, D), (2 * C) ** -0.5, 0.21875, ((0, 4),)),
        "norm2_gain": jnp.clip(1.0 + 0.18 * jax.random.normal(key_list[10], (D,), jnp.float32), 0.1, 1.9),
        "w_gate": noise(key_list[11], (D, FF), D ** -0.5, 0.21875, ((1, 4),)),
        "w_up": noise(key_list[12], (D, FF), D ** -0.5, 0.21875, ((1, 4),)),
        "w_down": noise(key_list[13], (FF, D), FF ** -0.5, 0.15625, ((0, 4),)),
    }


@jax.custom_vjp
def low(v):
    return lax.optimization_barrier(v.astype(jnp.bfloat16)).astype(jnp.float32)

@jax.custom_vjp
def low_back(v):
    return v

def low_keep(v):
    return (low(v), None)

def low_pass(kept, grad):
    return (grad,)

def back_keep(v):
    return (v, None)

def back_low(kept, grad):
    return (low(grad),)
low.defvjp(low_keep, low_pass)
low_back.defvjp(back_keep, back_low)

def exact(left_side, right_side):
    return jnp.dot(left_side, right_side, precision=lax.Precision.HIGHEST, preferred_element_type=jnp.float32)

def rms_norm(values, scales):
    return values * lax.rsqrt(lax.optimization_barrier(jnp.mean(values * values, -1, keepdims=True)) + 1e-06) * scales

def combine(earlier, latter):
    return (latter[0] * earlier[0] - latter[1] * earlier[1], latter[0] * earlier[1] + latter[1] * earlier[0], latter[0] * earlier[2] - latter[1] * earlier[3] + latter[2], latter[0] * earlier[3] + latter[1] * earlier[2] + latter[3])

def recurrence(in_real, in_imag, forget, forget_gap, phase_angle):
    leak_rate = forget_gap * jax.nn.sigmoid(-forget)
    retain = 1.0 - leak_rate
    return lax.associative_scan(combine, (retain * jnp.cos(phase_angle), retain * jnp.sin(phase_angle), leak_rate * jax.nn.silu(in_real), leak_rate * jax.nn.silu(in_imag)), axis=0)

def gated_norm(state_real, state_imag, gate_pre, group_gain):
    count_rows = state_real.shape[0]
    whole = jnp.stack([state_real, state_imag], -1).reshape(count_rows, -1)
    grouped = whole.reshape(count_rows, -1, GROUP)
    group_mean = lax.optimization_barrier(jnp.mean(grouped, -1, keepdims=True))
    centered = grouped - group_mean
    group_var = lax.optimization_barrier(jnp.mean(centered * centered, -1, keepdims=True))
    normed = (centered * lax.rsqrt(group_var + 1e-05)).reshape(count_rows, -1)
    return normed * group_gain * jax.nn.silu(gate_pre)

def layer(inputs, norm1_gain, w_input, w_forget, w_outgate, forget_gap, phase_angle, group_gain, w_mix, norm2_gain, w_gate, w_up, w_down):
    low_in = low(rms_norm(inputs, norm1_gain))
    in_proj = low_back(exact(low_in, w_input))
    forget = low_back(exact(low_in, w_forget))
    gate_pre = low_back(exact(low_in, w_outgate))
    scanned = recurrence(in_proj[:, 0::2], in_proj[:, 1::2], forget, forget_gap, phase_angle)
    low_mix = low(gated_norm(scanned[2], scanned[3], gate_pre, group_gain))
    resid = inputs + low_back(exact(low_mix, w_mix))
    low_mid = low(rms_norm(resid, norm2_gain))
    gate_act = low_back(exact(low_mid, w_gate))
    up_act = low_back(exact(low_mid, w_up))
    hidden = low(jax.nn.silu(gate_act) * up_act)
    return resid + low_back(exact(hidden, w_down))

def reference(tokens, cotangent, norm1_gain, w_input, w_forget, w_outgate, forget_gap, phase_angle, group_gain, w_mix, norm2_gain, w_gate, w_up, w_down):
    params = tuple((param.astype(jnp.float32) for param in (norm1_gain, w_input, w_forget, w_outgate, forget_gap, phase_angle, group_gain, w_mix, norm2_gain, w_gate, w_up, w_down)))
    inputs = tokens.astype(jnp.float32).reshape(1, TOKENS, D)
    grads_out = cotangent.astype(jnp.float32).reshape(1, TOKENS, D)

    def one_sequence(totals, pair):
        outputs, pull = jax.vjp(layer, pair[0], *params)
        grads = pull(pair[1])
        return (tuple((total + grad for total, grad in zip(totals, grads[1:]))), (outputs.astype(jnp.bfloat16), grads[0]))
    totals, (mixed, token_grad) = lax.scan(one_sequence, tuple((jnp.zeros_like(param) for param in params)), (inputs, grads_out))
    return (mixed.reshape(TOKENS, D), token_grad.reshape(TOKENS, D), totals[0], totals[1], totals[2], totals[3], totals[4], totals[5], totals[6], totals[7], totals[8], totals[9], totals[10], totals[11])
```

```python
import functools

import jax
import jax.numpy as jnp
from jax import lax
from jax.experimental import pallas as pl
from jax.experimental.pallas import tpu as pltpu
from jax.sharding import PartitionSpec as P

MESH = pl.DeviceIdType.MESH
BF = jnp.bfloat16
F32 = jnp.float32
GROUP = 64
LANES = 128


def nn(a, b):
    return jnp.dot(a, b, preferred_element_type=F32)


def nt(a, b):
    return lax.dot_general(a, b, (((1,), (1,)), ((), ())), preferred_element_type=F32)


def tn(a, b):
    return lax.dot_general(a, b, (((0,), (0,)), ((), ())), preferred_element_type=F32)


def cells(shape, axis):
    return lax.broadcasted_iota(jnp.int32, shape, axis)


def one_hot(flags):
    return jnp.where(flags, 1.0, 0.0).astype(BF)


def down_sum(v):
    if v.shape[0] > 8:
        v = jnp.sum(v.reshape(v.shape[0] // 8, 8, v.shape[1]), 0)
    v = v[0:4] + v[4:8]
    v = v[0:2] + v[2:4]
    return v[0:1] + v[1:2]


def power(c, s, n):
    out = None
    while n:
        if n % 2:
            out = (c, s) if out is None else (out[0] * c - out[1] * s, out[0] * s + out[1] * c)
        c, s = c * c - s * s, 2.0 * c * s
        n //= 2
    return out


def scratch_list(nd, nt_, T):
    dma = pltpu.SemaphoreType.DMA
    return dict(
        WI=pltpu.VMEM((2, 8, nt_, 64, 384), BF),
        WX=pltpu.VMEM((2, 4, nt_, 48, 384), BF),
        WM=pltpu.VMEM((2, 8, nt_, 144, 384), BF),
        PAR=pltpu.VMEM((nt_, 8, LANES), F32),
        WRP=pltpu.VMEM((nt_, 640, 768), BF),
        WXP=pltpu.VMEM((nt_, 256, 768), BF),
        NAT=pltpu.VMEM((T, 768), F32),
        PERM=pltpu.VMEM((6, T, LANES), F32),
        X=pltpu.VMEM((T, 768), F32),
        GY=pltpu.VMEM((T, 768), BF),
        LOW=pltpu.VMEM((T, 768), BF),
        ACT=pltpu.VMEM((nt_, T, 640), F32),
        LAM=pltpu.VMEM((nt_, T, LANES), F32),
        BR=pltpu.VMEM((nt_, T, LANES), F32),
        BI=pltpu.VMEM((nt_, T, LANES), F32),
        HR=pltpu.VMEM((nt_, T + 8, LANES), F32),
        HI=pltpu.VMEM((nt_, T + 8, LANES), F32),
        NR=pltpu.VMEM((nt_, T, LANES), F32),
        NI=pltpu.VMEM((nt_, T, LANES), F32),
        RS=pltpu.VMEM((nt_, T, LANES), F32),
        MIX=pltpu.VMEM((nt_, T, 256), BF),
        RES=pltpu.VMEM((T, 768), F32),
        MID=pltpu.VMEM((T, 768), BF),
        GRES0=pltpu.VMEM((T, 768), BF),
        HID=pltpu.VMEM((nt_, T, 384), BF),
        DG=pltpu.VMEM((nt_, T, 768), BF),
        GRES=pltpu.VMEM((T, 768), F32),
        CH=pltpu.VMEM((3, nt_ * 8, LANES), F32),
        ST=pltpu.VMEM((2, nt_ * 8, LANES), F32),
        EXF=pltpu.VMEM((nd, 16, LANES), F32),
        EXB=pltpu.VMEM((nd, 16, LANES), F32),
        EXV=pltpu.VMEM((nd, 16, LANES), F32),
        SM=pltpu.VMEM((2, 8, 144, 384), BF),
        SM0=pltpu.VMEM((2, 4, 144, 384), BF),
        SM1=pltpu.VMEM((2, 2, 144, 384), BF),
        SM2=pltpu.VMEM((2, 1, 144, 384), BF),
        SME=pltpu.VMEM((2, max(1, nd.bit_length() - 4), 144, 384), BF),
        SMF=pltpu.VMEM((2, 8, 144, 384), BF),
        SI=pltpu.VMEM((2, 8, 48, 512), BF),
        SI0=pltpu.VMEM((2, 4, 48, 512), BF),
        SI1=pltpu.VMEM((2, 2, 48, 512), BF),
        SI2=pltpu.VMEM((2, 1, 48, 512), BF),
        SIE=pltpu.VMEM((2, max(1, nd.bit_length() - 4), 48, 512), BF),
        SIF=pltpu.VMEM((2, 8, 48, 512), BF),
        SX=pltpu.VMEM((2, 8, 32, 384), BF),
        SX0=pltpu.VMEM((2, 4, 32, 384), BF),
        SX1=pltpu.VMEM((2, 2, 32, 384), BF),
        SX2=pltpu.VMEM((2, 1, 32, 384), BF),
        SXE=pltpu.VMEM((2, max(1, nd.bit_length() - 4), 32, 384), BF),
        SXF=pltpu.VMEM((2, 8, 32, 384), BF),
        loc=dma((8,)),
        out=dma((8,)),
        ss=dma((160,)),
        rs=dma((160,)),
        es=dma((3, nd)),
        er=dma((3, nd)),
    )


class Links:
    def __init__(self, ss, rs):
        self.ss, self.rs, self.used, self.open = ss, rs, 0, []

    def send(self, src, dst, dev):
        k = self.used
        self.used += 1
        copy = pltpu.make_async_remote_copy(
            src, dst, self.ss.at[k], self.rs.at[k], device_id=dev, device_id_type=MESH
        )
        copy.start()
        self.open.append(copy)
        return copy

    def drain(self):
        for copy in self.open:
            copy.wait_send()
        self.open = []


def kernel(nd, nt_, T, names, *refs):
    r = dict(zip(names, refs))
    me, z = lax.axis_index("dp"), lax.axis_index("tp")
    steps = T // 8
    ch = r["gap"].shape[1]

    def flip(bit):
        return me + bit - 2 * bit * ((me // bit) % 2)

    bits = (me % 2, (me // 2) % 2, (me // 4) % 2)
    order = ((1, 2), (2, 1))
    place = [bits[0] * 4 + bits[f] * 2 + bits[s] for f, s in order]
    wide = [bits[0] * 2 + bits[f] for f, s in order]
    links = Links(r["ss"], r["rs"])

    WM = r["WM"]
    loads = [
        pltpu.make_async_copy(r["wg"], WM.at[0, :, 0, 0:96, :], r["loc"].at[0]),
        pltpu.make_async_copy(r["wu"], WM.at[1, :, 0, 0:96, :], r["loc"].at[1]),
        pltpu.make_async_copy(r["wd"].at[:, :, 0:384], WM.at[0, :, 0, 96:144, :], r["loc"].at[2]),
        pltpu.make_async_copy(r["wd"].at[:, :, 384:768], WM.at[1, :, 0, 96:144, :], r["loc"].at[3]),
    ]
    loads_in = [
        pltpu.make_async_copy(r["tokens"], r["MID"], r["loc"].at[4]),
        pltpu.make_async_copy(r["cot"], r["GRES0"], r["loc"].at[5]),
    ]
    for copy in loads_in + loads:
        copy.start()

    barrier = pltpu.get_barrier_semaphore()

    def greet_dp(o, c):
        pl.semaphore_signal(barrier, 1, device_id=(lax.rem(me + o, nd), z), device_id_type=MESH)
        return c

    def greet_tp(o, c):
        pl.semaphore_signal(barrier, 1, device_id=(me, lax.rem(z + o, nt_)), device_id_type=MESH)
        return c

    lax.fori_loop(1, nd, greet_dp, 0)
    lax.fori_loop(1, nt_, greet_tp, 0)

    WI, WX, WRP, WXP, PAR = r["WI"], r["WX"], r["WRP"], r["WXP"], r["PAR"]
    rows, cols = cells((2 * ch, 2 * ch), 0), cells((2 * ch, 2 * ch), 1)
    apart = one_hot(cols == jnp.where(rows < ch, 2 * rows, 2 * (rows - ch) + 1))
    eye = one_hot(cells((ch, ch), 0) == cells((ch, ch), 1))
    turned = jnp.concatenate(
        [
            nt(apart, r["w_in"][...]).astype(BF),
            nt(eye, r["w_f"][...]).astype(BF),
            nt(apart, r["w_o"][...]).astype(BF),
            jnp.zeros((32, 768), BF),
        ],
        axis=0,
    )
    mixed_rows = nn(apart, r["w_mix"][...]).astype(BF)
    for h in range(2):
        for p in range(8):
            WI[h, p, 0] = turned[64 * p : 64 * p + 64, 384 * h : 384 * h + 384]
        for p in range(4):
            WX[h, p, 0] = mixed_rows[48 * p : 48 * p + 48, 384 * h : 384 * h + 384]
    PAR[0] = jnp.zeros((8, LANES), F32)
    PAR[0, 0:1, 0:ch] = r["gap"][...]
    PAR[0, 1:2, 0:ch] = r["phase"][...]
    gains = lax.dot_general(
        jnp.broadcast_to(r["gg"][...], (8, 2 * ch)),
        apart.astype(F32),
        (((1,), (1,)), ((), ())),
        precision=lax.Precision.HIGHEST,
        preferred_element_type=F32,
    )
    PAR[0, 2:3, 0:ch] = gains[0:1, 0:ch]
    PAR[0, 3:4, 0:ch] = gains[0:1, ch : 2 * ch]

    for k in range(nt_):
        for g in range(5):
            WRP[k, g * 128 + 96 : g * 128 + 128, :] = jnp.zeros((32, 768), BF)
        for g in range(2):
            WXP[k, g * 128 + 96 : g * 128 + 128, :] = jnp.zeros((32, 768), BF)

    def spread_in(k):
        for g in range(5):
            for q in range(3):
                row = g * 96 + q * 32
                for h in range(2):
                    WRP[k, g * 128 + q * 32 : g * 128 + q * 32 + 32, 384 * h : 384 * h + 384] = WI[
                        h, row // 64, k, row % 64 : row % 64 + 32, :
                    ]

    def spread_mix(k):
        for p in range(4):
            row = (p // 2) * 128 + (p % 2) * 48
            for h in range(2):
                WXP[k, row : row + 48, 384 * h : 384 * h + 384] = WX[h, p, k]

    pl.semaphore_wait(barrier, nd - 1 + nt_ - 1)

    def across(o):
        return (me, lax.rem(z + nt_ - o, nt_))

    def partner(b):
        return (flip(1 << b), z)

    class Unit:
        def __init__(self, buf, slots, portions):
            self.buf, self.slots, self.portions = buf, slots, portions
            self.todo = []

        def view(self, h, start, count):
            return self.buf.at[h, pl.ds(start, count), pl.ds(self.slots[0], len(self.slots))]

        def stage(self, n):
            for copy in self.todo:
                copy.wait_recv()
            self.todo = []
            if n == 0:
                for h in range(2):
                    at = place[h] if self.portions == 8 else wide[h]
                    for o in self.slots:
                        self.todo.append(
                            links.send(self.buf.at[h, at, 0], self.buf.at[h, at, o], across(o))
                        )
            elif n in (1, 2, 3):
                for h in range(2):
                    f, s = order[h]
                    if self.portions == 8:
                        b, start, count = (
                            (s, place[h], 1),
                            (f, bits[0] * 4 + bits[f] * 2, 2),
                            (0, bits[0] * 4, 4),
                        )[n - 1]
                    else:
                        if n == 2:
                            continue
                        b, start, count = ((f, wide[h], 1), None, (0, bits[0] * 2, 2))[n - 1]
                    part = self.view(h, start, count)
                    self.todo.append(links.send(part, part, partner(b)))

    others = list(range(1, nt_))
    units = [Unit(WI, others, 8), Unit(WX, others, 4)] + [Unit(WM, [o], 8) for o in others]

    def gather_round(n):
        for u, unit in enumerate(units):
            if 0 <= n - u <= 4:
                unit.stage(n - u)

    par_copies = [links.send(PAR.at[0], PAR.at[o], across(o)) for o in others]
    gather_round(0)

    NAT, X, GY, LOW = r["NAT"], r["X"], r["GY"], r["LOW"]
    PERM = r["PERM"]
    for copy in loads_in:
        copy.wait()
    tiles = [slice(LANES * i, LANES * i + LANES) for i in range(6)]
    for i in range(6):
        PERM[i] = r["MID"][:, tiles[i]].astype(F32)

    def take(k, c):
        for i in range(6):
            X[pl.ds(pl.multiple_of(8 * k, 8), 8), tiles[i]] = PERM[i, pl.ds(k, 8, stride=steps), :]
        return c

    lax.fori_loop(0, steps, take, 0, unroll=4)
    def norm_rows(src, gain, dst):
        def body(i, c):
            at = pl.ds(pl.multiple_of(i * 128, 128), 128)
            v = src[at, :]
            q = lax.rsqrt(jnp.mean(v * v, -1, keepdims=True) + 1e-06)
            dst[at, :] = (v * q * gain[...]).astype(BF)
            return c

        lax.fori_loop(0, T // 128, body, 0)

    norm_rows(X, r["g1"], LOW)
    for i in range(6):
        PERM[i] = r["GRES0"][:, tiles[i]].astype(F32)

    def take_cot(k, c):
        for i in range(6):
            two = [PERM[i, pl.ds(2 * k + j, 8, stride=steps), :] for j in range(2)]
            GY[pl.ds(pl.multiple_of(16 * k, 16), 16), tiles[i]] = jnp.concatenate(two, axis=0).astype(BF)
        return c

    lax.fori_loop(0, steps // 2, take_cot, 0, unroll=2)

    ACT, LAM, BR, BI = r["ACT"], r["LAM"], r["BR"], r["BI"]

    def project(k):
        gap = PAR[k, 0:1, :]
        ACT[k] = nt(LOW[...], WRP[k])
        ur, ui, fg = ACT[k, :, 0:128], ACT[k, :, 128:256], ACT[k, :, 256:384]
        leak = gap * jax.nn.sigmoid(-fg)
        LAM[k] = 1.0 - leak
        BR[k] = leak * (ur * jax.nn.sigmoid(ur))
        BI[k] = leak * (ui * jax.nn.sigmoid(ui))

    spread_in(0)
    spread_mix(0)
    project(0)
    for copy in loads:
        copy.wait()
    for n in range(1, 4):
        gather_round(n)
    for copy in par_copies:
        copy.wait_recv()
    gather_round(4)

    def project_other(k, c):
        spread_in(k)
        project(k)
        return c

    lax.fori_loop(1, nt_, project_other, 0)

    CH, ST, HR, HI = r["CH"], r["ST"], r["HR"], r["HI"]
    turn = []
    for k in range(nt_):
        ph = PAR[k, 1:2, :]
        turn.append((jnp.cos(ph), jnp.sin(ph)))
    turn8 = [(jnp.broadcast_to(c, (8, LANES)), jnp.broadcast_to(s, (8, LANES))) for c, s in turn]
    cos4 = jnp.concatenate([c for c, s in turn], axis=0)
    sin4 = jnp.concatenate([s for c, s in turn], axis=0)
    chunk_c, chunk_s = power(cos4, sin4, steps)
    whole_c, whole_s = power(cos4, sin4, T)
    zero8 = jnp.zeros((8, LANES), F32)
    zero4 = jnp.zeros((nt_, LANES), F32)

    def rows_of(k):
        return pl.ds(pl.multiple_of(8 * k, 8), 8)

    def ends(n, carry):
        out = []
        for k in range(nt_):
            hr, hi, lp = carry[k]
            c, s = turn8[k]
            lam = LAM[k, rows_of(n), :]
            nr = lam * (c * hr - s * hi) + BR[k, rows_of(n), :]
            ni = lam * (c * hi + s * hr) + BI[k, rows_of(n), :]
            out.append((nr, ni, lp * lam))
        return tuple(out)

    last = lax.fori_loop(
        0, steps, ends, tuple((zero8, zero8, zero8 + 1.0) for k in range(nt_)), unroll=4
    )
    for k in range(nt_):
        CH[0, 8 * k : 8 * k + 8, :] = last[k][2]
        CH[1, 8 * k : 8 * k + 8, :] = last[k][0]
        CH[2, 8 * k : 8 * k + 8, :] = last[k][1]

    def chunk(i, c):
        return CH[i, pl.ds(c, nt_, stride=8), :]

    def chain(sr, si, sign, keep):
        for c in range(8) if sign > 0 else range(7, -1, -1):
            if keep:
                ST[0, pl.ds(c, nt_, stride=8), :] = sr
                ST[1, pl.ds(c, nt_, stride=8), :] = si
            lp = chunk(0, c)
            pr, pi = lp * chunk_c, sign * (lp * chunk_s)
            sr, si = pr * sr - pi * si + chunk(1, c), pr * si + pi * sr + chunk(2, c)
        return sr, si

    whole_lam = chunk(0, 0)
    for c in range(1, 8):
        whole_lam = whole_lam * chunk(0, c)

    def exchange(which, buf, start):
        def copy_to(o):
            at = lax.rem(me + o, nd)
            return pltpu.make_async_remote_copy(
                buf.at[me],
                buf.at[me],
                r["es"].at[which, o],
                r["er"].at[which, o],
                device_id=(at, z),
                device_id_type=MESH,
            )

        def wait_from(o):
            at = lax.rem(me + nd - o, nd)
            return pltpu.make_async_remote_copy(
                buf.at[at],
                buf.at[at],
                r["es"].at[which, o],
                r["er"].at[which, o],
                device_id=(at, z),
                device_id_type=MESH,
            )

        def go(o, c):
            copy_to(o).start()
            return c

        def arrive(o, c):
            wait_from(o).wait_recv()
            return c

        def leave(o, c):
            copy_to(o).wait_send()
            return c

        lax.fori_loop(1, nd, {"go": go, "arrive": arrive, "leave": leave}[start], 0)

    def post(buf, which, sr, si):
        buf[me, 0:4, :] = whole_lam
        buf[me, 4:8, :] = sr
        buf[me, 8:12, :] = si
        buf[me, 12:16, :] = zero4
        exchange(which, buf, "go")

    def carried(buf, which, sign):
        exchange(which, buf, "arrive")

        def lap(k, s):
            at = k if sign > 0 else nd - 1 - k
            reached = (at < me) if sign > 0 else (at > me)
            lp = buf[at, 0:4, :]
            pr, pi = lp * whole_c, sign * (lp * whole_s)
            nr = pr * s[0] - pi * s[1] + buf[at, 4:8, :]
            ni = pr * s[1] + pi * s[0] + buf[at, 8:12, :]
            return jnp.where(reached, nr, s[0]), jnp.where(reached, ni, s[1])

        return lax.fori_loop(0, nd, lap, (zero4, zero4))

    post(r["EXF"], 0, *chain(zero4, zero4, 1.0, False))
    gather_round(5)
    lax.fori_loop(1, nt_, lambda k, c: (spread_mix(k), c)[1], 0)
    start = carried(r["EXF"], 0, 1.0)
    chain(start[0], start[1], 1.0, True)
    for k in range(nt_):
        HR[k, 0:8, :] = ST[0, 8 * k : 8 * k + 8, :]
        HI[k, 0:8, :] = ST[1, 8 * k : 8 * k + 8, :]

    def states(n, carry):
        out = []
        for k in range(nt_):
            hr, hi = carry[k]
            c, s = turn8[k]
            lam = LAM[k, rows_of(n), :]
            nr = lam * (c * hr - s * hi) + BR[k, rows_of(n), :]
            ni = lam * (c * hi + s * hr) + BI[k, rows_of(n), :]
            HR[k, rows_of(n + 1), :] = nr
            HI[k, rows_of(n + 1), :] = ni
            out.append((nr, ni))
        return tuple(out)

    lax.fori_loop(
        0,
        steps,
        states,
        tuple((ST[0, 8 * k : 8 * k + 8, :], ST[1, 8 * k : 8 * k + 8, :]) for k in range(nt_)),
        unroll=4,
    )

    half = GROUP // 2
    same = one_hot(cells((LANES, LANES), 0) // half == cells((LANES, LANES), 1) // half)

    def group_mean(v):
        top = v.astype(BF)
        rest = (v - top.astype(F32)).astype(BF)
        return (nn(top, same) + nn(rest, same)) * (1.0 / GROUP)

    NR, NI, RS, MIX = r["NR"], r["NI"], r["RS"], r["MIX"]

    def normalise(k, c):
        hr, hi = HR[k, pl.ds(8, T), :], HI[k, pl.ds(8, T), :]
        mean = group_mean(hr + hi)
        hr, hi = hr - mean, hi - mean
        rstd = lax.rsqrt(group_mean(hr * hr + hi * hi) + 1e-05)
        RS[k] = rstd
        hr, hi = hr * rstd, hi * rstd
        NR[k] = hr
        NI[k] = hi
        gr, gi = ACT[k, :, 384:512], ACT[k, :, 512:640]
        MIX[k, :, 0:128] = (hr * PAR[k, 2:3, :] * (gr * jax.nn.sigmoid(gr))).astype(BF)
        MIX[k, :, 128:256] = (hi * PAR[k, 3:4, :] * (gi * jax.nn.sigmoid(gi))).astype(BF)
        return c

    lax.fori_loop(0, nt_, normalise, 0)

    def slot(k):
        return lax.rem(k + nt_ - z, nt_)

    RES, MID = r["RES"], r["MID"]
    RES[...] = X[...]

    def mix_in(k, c):
        RES[...] += nn(MIX[slot(k)], WXP[slot(k)])
        return c

    lax.fori_loop(0, nt_, mix_in, 0)

    norm_rows(RES, r["g2"], MID)

    HID, DG = r["HID"], r["DG"]

    def gate_w(k, h):
        return WM[h, :, pl.ds(k, 1), 0:96, :].reshape(768, 384)

    def down_w(k, h):
        return WM[h, :, pl.ds(k, 1), 96:144, :].reshape(384, 384)

    def swiglu(k):
        def tile(i, c):
            at = pl.ds(pl.multiple_of(i * 256, 256), 256)
            ga = nn(MID[at, :], gate_w(k, 0))
            ua = nn(MID[at, :], gate_w(k, 1))
            gh = nt(GY[at, 0:384], down_w(k, 0)) + nt(GY[at, 384:768], down_w(k, 1))
            s = jax.nn.sigmoid(ga)
            sl = ga * s
            HID[k, at, :] = (sl * ua).astype(BF)
            DG[k, at, 0:384] = (gh * ua * (s * (1.0 + ga * (1.0 - s)))).astype(BF)
            DG[k, at, 384:768] = (gh * sl).astype(BF)
            return c

        lax.fori_loop(0, T // 256, tile, 0)

    swiglu(0)
    SM = r["SM"]
    for h in range(2):
        SM[h, :, 0:96, :] = tn(MID[...], DG[0, :, 384 * h : 384 * h + 384]).astype(BF).reshape(8, 96, 384)
        SM[h, :, 96:144, :] = (
            tn(HID[0], GY[:, 384 * h : 384 * h + 384]).astype(BF).reshape(8, 48, 384)
        )

    class Summed:
        def __init__(self, parts):
            self.parts = parts
            self.todo = []

        def stage(self, n):
            for copy in self.todo:
                copy.wait_recv()
            self.todo = []
            for bufs in self.parts:
                for h in range(2):
                    f, s = order[h]
                    S = bufs[0]
                    spans = (
                        (0, 0, 4),
                        (f, bits[0] * 4, 2),
                        (s, bits[0] * 4 + bits[f] * 2, 1),
                    )
                    if 1 <= n <= 3:
                        b, start, count = spans[n - 1]
                        mine = pl.ds(start + bits[b] * count, count)
                        S[h, mine] = (S[h, mine].astype(F32) + bufs[n][h].astype(F32)).astype(BF)
                    if n == 3:
                        part = pl.ds(place[h], 1)
                        for b in range(3, nd.bit_length() - 1):
                            land = bufs[4].at[h, pl.ds(b - 3, 1)]
                            one = links.send(S.at[h, part], land, partner(b))
                            one.wait()
                            links.open = [c for c in links.open if c is not one]
                            S[h, part] = (
                                S[h, part].astype(F32) + bufs[4][h, b - 3 : b - 2].astype(F32)
                            ).astype(BF)
                        bufs[5][h, part] = S[h, part]
                    if n < 3:
                        b, start, count = spans[n]
                        away = start + (1 - bits[b]) * count
                        self.todo.append(
                            links.send(S.at[h, pl.ds(away, count)], bufs[n + 1].at[h], partner(b))
                        )
                    elif n < 6:
                        b, start, count = (
                            (s, place[h], 1),
                            (f, bits[0] * 4 + bits[f] * 2, 2),
                            (0, bits[0] * 4, 4),
                        )[n - 3]
                        part = bufs[5].at[h, pl.ds(start, count)]
                        self.todo.append(links.send(part, part, partner(b)))

    mlp_sum = Summed([(SM, r["SM0"], r["SM1"], r["SM2"], r["SME"], r["SMF"])])
    mlp_sum.stage(0)
    for n in range(6, 9):
        gather_round(n)
        swiglu(n - 5)

    GRES = r["GRES"]
    NAT[...] = jnp.zeros((T, 768), F32)

    def back_mid(k, c):
        j = slot(k)
        NAT[...] += nt(DG[j, :, 0:384], gate_w(j, 0)) + nt(DG[j, :, 384:768], gate_w(j, 1))
        return c

    lax.fori_loop(0, nt_, back_mid, 0)
    mlp_sum.stage(1)
    LOWR = r["MID"]

    def back_second(i, total):
        at = pl.ds(pl.multiple_of(i * 128, 128), 128)
        res, gmid = RES[at, :], NAT[at, :]
        q2 = lax.rsqrt(jnp.mean(res * res, -1, keepdims=True) + 1e-06)
        p = gmid * r["g2"][...]
        back = q2 * p - res * (q2 * q2 * q2) * jnp.mean(p * res, -1, keepdims=True)
        gres = GY[at, :].astype(F32) + back
        GRES[at, :] = gres
        LOWR[at, :] = gres.astype(BF)
        return total + jnp.sum((gmid * res * q2).reshape(16, 8, 768), 0)

    EXV = r["EXV"]
    gnorm2 = down_sum(lax.fori_loop(0, T // 128, back_second, jnp.zeros((8, 768), F32)))
    for i in range(6):
        EXV[me, 6 + i : 7 + i, :] = gnorm2[:, 128 * i : 128 * i + 128]
    mlp_sum.stage(2)

    G = DG

    def back_norm(k, want):
        gact = nt(LOWR[...], WXP[k])
        rstd = RS[k]
        parts, sums, dots = [], 0.0, 0.0
        for i, hn in enumerate((NR[k], NI[k])):
            pre = ACT[k, :, 384 + 128 * i : 512 + 128 * i]
            gain = PAR[k, 2 + i : 3 + i, :]
            ga = gact[:, 128 * i : 128 * i + 128]
            s = jax.nn.sigmoid(pre)
            sl = pre * s
            gh = ga * hn
            G[k, :, 384 + 128 * i : 512 + 128 * i] = (
                gh * gain * (s * (1.0 + pre * (1.0 - s)))
            ).astype(BF)
            if want:
                EXV[me, 14 + i : 15 + i, :] = down_sum(gh * sl)
            p = ga * gain * sl
            parts.append((p, hn))
            sums = sums + p
            dots = dots + p * hn
        sums, dots = group_mean(sums), group_mean(dots)
        for buf, (p, hn) in zip((BR, BI), parts):
            buf[k] = rstd * (p - sums - hn * dots)

    back_norm(0, True)
    lax.fori_loop(1, nt_, lambda k, c: (back_norm(k, False), c)[1], 0)
    mlp_sum.stage(3)

    def back_ends(n, carry):
        n = steps - 1 - n
        out = []
        for k in range(nt_):
            ur, ui = carry[k]
            c, s = turn8[k]
            lam = LAM[k, rows_of(n), :]
            er = BR[k, rows_of(n), :] + ur
            ei = BI[k, rows_of(n), :] + ui
            out.append((lam * (c * er + s * ei), lam * (c * ei - s * er)))
        return tuple(out)

    first = lax.fori_loop(0, steps, back_ends, tuple((zero8, zero8) for k in range(nt_)), unroll=4)
    for k in range(nt_):
        CH[1, 8 * k : 8 * k + 8, :] = first[k][0]
        CH[2, 8 * k : 8 * k + 8, :] = first[k][1]
    post(r["EXB"], 1, *chain(zero4, zero4, -1.0, False))
    SX = r["SX"]
    rows, cols = cells((256, 256), 0), cells((256, 256), 1)
    lane = rows % 128
    together = one_hot((cols == 2 * lane + rows // 128) & (lane < ch))
    low_mix = nn(MIX[0], together).astype(BF)
    for h in range(2):
        SX[h] = tn(low_mix, LOWR[:, 384 * h : 384 * h + 384]).astype(BF).reshape(8, 32, 384)
    mlp_sum.stage(4)

    start = carried(r["EXB"], 1, -1.0)
    chain(start[0], start[1], -1.0, True)

    def back_states(n, carry):
        n = steps - 1 - n
        out = []
        for k in range(nt_):
            ur, ui = carry[k]
            c, s = turn8[k]
            lam = LAM[k, rows_of(n), :]
            er = BR[k, rows_of(n), :] + ur
            ei = BI[k, rows_of(n), :] + ui
            BR[k, rows_of(n), :] = er
            BI[k, rows_of(n), :] = ei
            out.append((lam * (c * er + s * ei), lam * (c * ei - s * er)))
        return tuple(out)

    lax.fori_loop(
        0,
        steps,
        back_states,
        tuple((ST[0, 8 * k : 8 * k + 8, :], ST[1, 8 * k : 8 * k + 8, :]) for k in range(nt_)),
        unroll=4,
    )

    def back_gates(k, c, s, want):
        er, ei = BR[k], BI[k]
        hr, hi = HR[k, pl.ds(0, T), :], HI[k, pl.ds(0, T), :]
        gap = PAR[k, 0:1, :]
        gar, gai = er * hr + ei * hi, ei * hr - er * hi
        ur, ui, fg = ACT[k, :, 0:128], ACT[k, :, 128:256], ACT[k, :, 256:384]
        su, si, sf = jax.nn.sigmoid(ur), jax.nn.sigmoid(ui), jax.nn.sigmoid(-fg)
        leak = gap * sf
        gleak = er * (ur * su) + ei * (ui * si) - (c * gar + s * gai)
        G[k, :, 0:128] = (er * leak * (su * (1.0 + ur * (1.0 - su)))).astype(BF)
        G[k, :, 128:256] = (ei * leak * (si * (1.0 + ui * (1.0 - si)))).astype(BF)
        G[k, :, 256:384] = (-gleak * leak * (1.0 - sf)).astype(BF)
        if want:
            EXV[me, 12:13, :] = down_sum(gleak * sf)
            EXV[me, 13:14, :] = down_sum((1.0 - leak) * (c * gai - s * gar))

    back_gates(0, turn[0][0], turn[0][1], True)

    SI = r["SI"]
    rows, cols = cells((640, 512), 0), cells((640, 512), 1)
    lane, g = rows % 128, rows // 128
    to = jnp.where(
        g < 2,
        2 * lane + g,
        jnp.where(g == 2, 2 * ch + lane, 3 * ch + 2 * lane + (g - 3)),
    )
    gcat = nn(G[0, :, 0:640], one_hot((cols == to) & (lane < ch))).astype(BF)
    for h in range(2):
        SI[h] = tn(LOW[:, 384 * h : 384 * h + 384], gcat).astype(BF).reshape(8, 48, 512)
    rec_sum = Summed(
        [(SI, r["SI0"], r["SI1"], r["SI2"], r["SIE"], r["SIF"]), (SX, r["SX0"], r["SX1"], r["SX2"], r["SXE"], r["SXF"])]
    )
    rec_sum.stage(0)
    mlp_sum.stage(5)
    for k in range(1, nt_):
        back_gates(k, turn[k][0], turn[k][1], False)
    rec_sum.stage(1)

    NAT[...] = jnp.zeros((T, 768), F32)

    def back_in(k, c):
        NAT[...] += nn(G[slot(k), :, 0:640], WRP[slot(k)])
        return c

    lax.fori_loop(0, nt_, back_in, 0)
    rec_sum.stage(2)
    def back_first(i, total):
        at = pl.ds(pl.multiple_of(i * 128, 128), 128)
        x, gin = X[at, :], NAT[at, :]
        q1 = lax.rsqrt(jnp.mean(x * x, -1, keepdims=True) + 1e-06)
        p = gin * r["g1"][...]
        GRES[at, :] += q1 * p - x * (q1 * q1 * q1) * jnp.mean(p * x, -1, keepdims=True)
        return total + jnp.sum((gin * x * q1).reshape(16, 8, 768), 0)

    gnorm1 = down_sum(lax.fori_loop(0, T // 128, back_first, jnp.zeros((8, 768), F32)))
    for i in range(6):
        EXV[me, i : i + 1, :] = gnorm1[:, 128 * i : 128 * i + 128]
    exchange(2, EXV, "go")
    rec_sum.stage(3)

    finals = []

    def put_out(src, dst, k):
        copy = pltpu.make_async_copy(src, dst, r["out"].at[k])
        copy.start()
        finals.append(copy)

    def put_from(buf):
        def put(k, c):
            for i in range(6):
                PERM[i, pl.ds(k, 8, stride=steps), :] = buf[pl.ds(pl.multiple_of(8 * k, 8), 8), tiles[i]]
            return c

        lax.fori_loop(0, steps, put, 0, unroll=4)

    put_from(GRES)
    for i in range(6):
        NAT[:, tiles[i]] = PERM[i]
    put_out(NAT, r["tok"], 0)
    rec_sum.stage(4)

    def down(k, c):
        j = slot(k)
        for h in range(2):
            RES[:, 384 * h : 384 * h + 384] += nn(HID[j], down_w(j, h))
        return c

    lax.fori_loop(0, nt_, down, 0)

    put_from(RES)
    for i in range(6):
        r["GRES0"][:, tiles[i]] = PERM[i].astype(BF)
    put_out(r["GRES0"], r["mixed"], 1)
    rec_sum.stage(5)

    exchange(2, EXV, "arrive")
    total = EXV[0]
    for k in range(1, nd):
        total = total + EXV[k]
    r["vec"][...] = total
    mlp_sum.stage(6)
    put_out(r["SMF"], r["o_mlp"], 2)
    rec_sum.stage(6)
    put_out(r["SIF"], r["o_in"], 3)
    put_out(r["SXF"], r["o_mix"], 4)
    for which in range(3):
        exchange(which, (r["EXF"], r["EXB"], EXV)[which], "leave")
    links.drain()
    for copy in finals:
        copy.wait()


def local(nd, nt_, *args):
    (tokens, cot, g1, w_in, w_f, w_o, gap, phase, gg, w_mix, g2, wg, wu, wd) = args
    T, D = tokens.shape
    ch = w_f.shape[1]
    given = dict(
        tokens=tokens,
        cot=cot,
        g1=g1.reshape(1, D),
        w_in=w_in,
        w_f=w_f,
        w_o=w_o,
        gap=gap.reshape(1, ch),
        phase=phase.reshape(1, ch),
        gg=gg.reshape(1, 2 * ch),
        w_mix=w_mix,
        g2=g2.reshape(1, D),
        wg=wg.reshape(8, 96, 384),
        wu=wu.reshape(8, 96, 384),
        wd=wd.reshape(8, 48, D),
    )
    vmem = pl.BlockSpec(memory_space=pltpu.VMEM)
    in_specs = [pl.BlockSpec(memory_space=pl.ANY) if k in ("wg", "wu", "wd", "tokens", "cot") else vmem for k in given]
    outs = dict(
        mixed=jax.ShapeDtypeStruct((T, D), BF),
        tok=jax.ShapeDtypeStruct((T, D), F32),
        o_mlp=jax.ShapeDtypeStruct((2, 8, 144, 384), BF),
        o_in=jax.ShapeDtypeStruct((2, 8, 48, 512), BF),
        o_mix=jax.ShapeDtypeStruct((2, 8, 32, 384), BF),
        vec=jax.ShapeDtypeStruct((16, LANES), F32),
    )
    scratch = scratch_list(nd, nt_, T)
    names = list(given) + list(outs) + list(scratch)
    mixed, tok, o_mlp, o_in, o_mix, vec = pl.pallas_call(
        functools.partial(kernel, nd, nt_, T, names),
        out_shape=list(outs.values()),
        in_specs=in_specs,
        out_specs=[vmem if k == "vec" else pl.BlockSpec(memory_space=pl.ANY) for k in outs],
        scratch_shapes=list(scratch.values()),
        compiler_params=pltpu.CompilerParams(
            collective_id=0, has_side_effects=True, vmem_limit_bytes=63 * 2**20
        ),
    )(*given.values())

    grad_gate = o_mlp[0, :, 0:96].reshape(D, 384).astype(F32)
    grad_up = o_mlp[1, :, 0:96].reshape(D, 384).astype(F32)
    grad_down = (
        o_mlp[:, :, 96:144].reshape(2, 384, 384).transpose(1, 0, 2).reshape(384, D).astype(F32)
    )
    g_in = o_in.reshape(D, 512)
    grad_input = g_in[:, 0 : 2 * ch].astype(F32)
    grad_forget = g_in[:, 2 * ch : 3 * ch].astype(F32)
    grad_outgate = g_in[:, 3 * ch : 5 * ch].astype(F32)
    grad_mix = o_mix.reshape(2, 256, 384)[:, : 2 * ch].transpose(1, 0, 2).reshape(2 * ch, D).astype(F32)
    grad_group = jnp.stack([vec[14, :ch], vec[15, :ch]], -1).reshape(2 * ch)
    return (
        mixed,
        tok,
        vec[0:6].reshape(D),
        grad_input,
        grad_forget,
        grad_outgate,
        vec[12, :ch],
        vec[13, :ch],
        grad_group,
        grad_mix,
        vec[6:12].reshape(D),
        grad_gate,
        grad_up,
        grad_down,
    )


def solution(mesh):
    in_specs = (
        P("dp", None),
        P("dp", None),
        P(),
        P(None, "tp"),
        P(None, "tp"),
        P(None, "tp"),
        P("tp"),
        P("tp"),
        P("tp"),
        P("tp", None),
        P(),
        P(None, "tp"),
        P(None, "tp"),
        P("tp", None),
    )
    out_specs = (
        P("dp", None),
        P("dp", None),
        P(),
        P(None, "tp"),
        P(None, "tp"),
        P(None, "tp"),
        P("tp"),
        P("tp"),
        P("tp"),
        P("tp", None),
        P(),
        P(None, "tp"),
        P(None, "tp"),
        P("tp", None),
    )
    body = functools.partial(local, mesh.shape["dp"], mesh.shape["tp"])
    return jax.shard_map(body, mesh=mesh, in_specs=in_specs, out_specs=out_specs, check_vma=False)
```

```python
import functools

import jax
import jax.numpy as jnp
from jax import lax
from jax.experimental import pallas as pl
from jax.experimental.pallas import tpu as pltpu
from jax.sharding import PartitionSpec as P

MESH = pl.DeviceIdType.MESH
BF = jnp.bfloat16
F32 = jnp.float32
GROUP = 64
LANES = 128


def nn(a, b):
    return jnp.dot(a, b, preferred_element_type=F32)


def nt(a, b):
    return lax.dot_general(a, b, (((1,), (1,)), ((), ())), preferred_element_type=F32)


def tn(a, b):
    return lax.dot_general(a, b, (((0,), (0,)), ((), ())), preferred_element_type=F32)


def exact(a, b, dims):
    return lax.dot_general(
        a, b, (dims, ((), ())), precision=lax.Precision.HIGHEST, preferred_element_type=F32
    )


def cells(shape, axis):
    return lax.broadcasted_iota(jnp.int32, shape, axis)


def one_hot(flags):
    return jnp.where(flags, 1.0, 0.0).astype(BF)


def down_sum(v):
    if v.shape[0] > 8:
        v = jnp.sum(v.reshape(v.shape[0] // 8, 8, v.shape[1]), 0)
    v = v[0:4] + v[4:8]
    v = v[0:2] + v[2:4]
    return v[0:1] + v[1:2]


def power(c, s, n):
    out = None
    while n:
        if n % 2:
            out = (c, s) if out is None else (out[0] * c - out[1] * s, out[0] * s + out[1] * c)
        c, s = c * c - s * s, 2.0 * c * s
        n //= 2
    return out


def sum_buffers(name, nd, rows):
    further = max(1, nd.bit_length() - 4)
    counts = (("", 8), ("0", 4), ("1", 2), ("2", 1), ("E", further), ("F", 8))
    return {name + k: pltpu.VMEM((2, n, rows, 384), BF) for k, n in counts}


def scratch_list(nd, nt_, T):
    dma = pltpu.SemaphoreType.DMA
    return dict(
        RI=pltpu.VMEM((192, 768), BF),
        RF=pltpu.VMEM((96, 768), BF),
        RO=pltpu.VMEM((192, 768), BF),
        RM=pltpu.VMEM((192, 768), BF),
        WI=pltpu.VMEM((2, 8, nt_, 64, 384), BF),
        WX=pltpu.VMEM((2, 4, nt_, 48, 384), BF),
        WM=pltpu.VMEM((2, 8, nt_, 144, 384), BF),
        PAR=pltpu.VMEM((nt_, 8, LANES), F32),
        WRP=pltpu.VMEM((nt_, 640, 768), BF),
        WXP=pltpu.VMEM((nt_, 256, 768), BF),
        PERM=pltpu.VMEM((6, T, LANES), F32),
        X=pltpu.VMEM((T, 768), F32),
        GY=pltpu.VMEM((T, 768), BF),
        LOW=pltpu.VMEM((T, 768), BF),
        ACT=pltpu.VMEM((nt_, T, 640), F32),
        LAM=pltpu.VMEM((nt_, T, LANES), F32),
        BR=pltpu.VMEM((nt_, T, LANES), F32),
        BI=pltpu.VMEM((nt_, T, LANES), F32),
        HR=pltpu.VMEM((nt_, T + 8, LANES), F32),
        HI=pltpu.VMEM((nt_, T + 8, LANES), F32),
        NR=pltpu.VMEM((nt_, T, LANES), F32),
        NI=pltpu.VMEM((nt_, T, LANES), F32),
        RS=pltpu.VMEM((nt_, T, LANES), F32),
        MIX=pltpu.VMEM((nt_, T, 256), BF),
        RES=pltpu.VMEM((T, 768), F32),
        MID=pltpu.VMEM((T, 768), BF),
        COT=pltpu.VMEM((T, 768), BF),
        HID=pltpu.VMEM((nt_, T, 384), BF),
        DG=pltpu.VMEM((nt_, T, 768), BF),
        NAT=pltpu.VMEM((T, 768), F32),
        GRES=pltpu.VMEM((T, 768), F32),
        CH=pltpu.VMEM((3, nt_ * 8, LANES), F32),
        ST=pltpu.VMEM((2, nt_ * 8, LANES), F32),
        EX0=pltpu.VMEM((nd, 16, LANES), F32),
        EX1=pltpu.VMEM((nd, 16, LANES), F32),
        EX2=pltpu.VMEM((nd, 16, LANES), F32),
        EX3=pltpu.VMEM((nd, 16, LANES), F32),
        **sum_buffers("SM", nd, 144),
        **sum_buffers("SE", nd, 48),
        **sum_buffers("SL", nd, 48),
        loc=dma((16,)),
        out=dma((8,)),
        ss=dma((160,)),
        rs=dma((160,)),
        es=dma((4, nd)),
        er=dma((4, nd)),
    )


class Links:
    def __init__(self, ss, rs):
        self.ss, self.rs, self.used, self.open = ss, rs, 0, []

    def send(self, src, dst, dev):
        k = self.used
        self.used += 1
        copy = pltpu.make_async_remote_copy(
            src, dst, self.ss.at[k], self.rs.at[k], device_id=dev, device_id_type=MESH
        )
        copy.start()
        self.open.append(copy)
        return copy

    def drain(self):
        for copy in self.open:
            copy.wait_send()
        self.open = []


def kernel(nd, nt_, T, names, *refs):
    r = dict(zip(names, refs))
    me, z = lax.axis_index("dp"), lax.axis_index("tp")
    steps = T // 8
    ch = r["w_f"].shape[0]
    blocks = list(range(nt_))

    def flip(bit):
        return me + bit - 2 * bit * ((me // bit) % 2)

    bits = (me % 2, (me // 2) % 2, (me // 4) % 2)
    order = ((1, 2), (2, 1))
    place = [bits[0] * 4 + bits[f] * 2 + bits[s] for f, s in order]
    wide = [bits[0] * 2 + bits[f] for f, s in order]
    links = Links(r["ss"], r["rs"])
    away = [0, 1, 3, 2] if nt_ == 4 else blocks

    def slot(k):
        o = lax.rem(k + nt_ - z, nt_)
        if nt_ != 4:
            return o
        return jnp.where(o == 2, 3, jnp.where(o == 3, 2, o))

    barrier = pltpu.get_barrier_semaphore()

    def greet_dp(o, c):
        pl.semaphore_signal(barrier, 1, device_id=(lax.rem(me + o, nd), z), device_id_type=MESH)
        return c

    def greet_tp(o, c):
        pl.semaphore_signal(barrier, 1, device_id=(me, lax.rem(z + o, nt_)), device_id_type=MESH)
        return c

    lax.fori_loop(1, nt_, greet_tp, 0)
    lax.fori_loop(1, nd, greet_dp, 0)

    WM = r["WM"]
    loads = {}
    for k, (name, src, dst) in enumerate(
        (
            ("w_i", r["w_i"], r["RI"]),
            ("w_f", r["w_f"], r["RF"]),
            ("w_o", r["w_o"], r["RO"]),
            ("tokens", r["tokens"], r["MID"]),
            ("w_x", r["w_mix"], r["RM"]),
            ("g", r["wg"], WM.at[0, :, 0, 0:96, :]),
            ("u", r["wu"], WM.at[1, :, 0, 0:96, :]),
            ("d0", r["wd"].at[:, :, 0:384], WM.at[0, :, 0, 96:144, :]),
            ("d1", r["wd"].at[:, :, 384:768], WM.at[1, :, 0, 96:144, :]),
            ("cot", r["cot"], r["COT"]),
        )
    ):
        loads[name] = pltpu.make_async_copy(src, dst, r["loc"].at[k])
        loads[name].start()

    WI, WX, WRP, WXP, PAR = r["WI"], r["WX"], r["WRP"], r["WXP"], r["PAR"]
    rows, cols = cells((2 * ch, 2 * ch), 0), cells((2 * ch, 2 * ch), 1)
    apart = one_hot(cols == jnp.where(rows < ch, 2 * rows, 2 * (rows - ch) + 1))
    for k in ("w_i", "w_f", "w_o"):
        loads[k].wait()
    turned = jnp.concatenate(
        [
            nn(apart, r["RI"][...]).astype(BF),
            r["RF"][...],
            nn(apart, r["RO"][...]).astype(BF),
            jnp.zeros((32, 768), BF),
        ],
        axis=0,
    )
    for h in range(2):
        for p in range(8):
            WI[h, p, 0] = turned[64 * p : 64 * p + 64, 384 * h : 384 * h + 384]
    PAR[0] = jnp.zeros((8, LANES), F32)
    PAR[0, 0:1, 0:ch] = r["gap"][...]
    PAR[0, 1:2, 0:ch] = r["phase"][...]
    gains = exact(
        jnp.broadcast_to(r["gg"][...], (8, 2 * ch)), apart.astype(F32), ((1,), (1,))
    )
    PAR[0, 2:3, 0:ch] = gains[0:1, 0:ch]
    PAR[0, 3:4, 0:ch] = gains[0:1, ch : 2 * ch]

    def across(o):
        return (me, lax.rem(z + nt_ - o, nt_))

    def partner(b):
        return (flip(1 << b), z)

    class Unit:
        def __init__(self, buf, slots, portions):
            self.buf, self.slots, self.portions = buf, slots, portions
            self.todo = []

        def wait(self):
            for copy in self.todo:
                copy.wait_recv()
            self.todo = []

        def hop(self, h, b, start, count):
            part = self.buf.at[h, pl.ds(start, count), pl.ds(self.slots[0], len(self.slots))]
            self.todo.append(links.send(part, part, partner(b)))

        def z(self):
            for s in self.slots:
                for h in range(2):
                    at = place[h] if self.portions == 8 else wide[h]
                    self.todo.append(
                        links.send(self.buf.at[h, at, 0], self.buf.at[h, at, s], across(away[s]))
                    )

        def s(self):
            self.wait()
            for h in range(2):
                f, s = order[h]
                if self.portions == 8:
                    self.hop(h, s, place[h], 1)
                else:
                    self.hop(h, f, wide[h], 1)

        def f(self):
            self.wait()
            for h in range(2):
                f, s = order[h]
                self.hop(h, f, bits[0] * 4 + bits[f] * 2, 2)

        def c(self):
            self.wait()
            n = self.portions // 2
            for h in range(2):
                self.hop(h, 0, bits[0] * n, n)

    I1, I2 = Unit(WI, blocks[1:3], 8), Unit(WI, blocks[3:], 8)
    XM = Unit(WX, blocks[1:], 4)
    M1, M2, M3 = [Unit(WM, [s], 8) for s in blocks[1:]]

    pl.semaphore_wait(barrier, nd - 1 + nt_ - 1)
    I1.z()
    par_copies = [links.send(PAR.at[0], PAR.at[s], across(away[s])) for s in blocks[1:]]

    PERM, X, GY, LOW = r["PERM"], r["X"], r["GY"], r["LOW"]
    loads["tokens"].wait()
    tiles = [slice(LANES * i, LANES * i + LANES) for i in range(6)]
    for i in range(6):
        PERM[i] = r["MID"][:, tiles[i]].astype(F32)

    def take(k, c):
        for i in range(6):
            X[pl.ds(pl.multiple_of(8 * k, 8), 8), tiles[i]] = PERM[i, pl.ds(k, 8, stride=steps), :]
        return c

    lax.fori_loop(0, steps, take, 0, unroll=4)

    def whole_row(ref):
        return jnp.concatenate([ref[i : i + 1, :] for i in range(6)], axis=1)

    gain1, gain2 = whole_row(r["g1"]), whole_row(r["g2"])

    def norm_rows(src, gain, dst):
        def body(i, c):
            at = pl.ds(pl.multiple_of(i * 128, 128), 128)
            v = src[at, :]
            q = lax.rsqrt(jnp.mean(v * v, -1, keepdims=True) + 1e-06)
            dst[at, :] = (v * q * gain).astype(BF)
            return c

        lax.fori_loop(0, T // 128, body, 0)

    norm_rows(X, gain1, LOW)
    I2.z()

    for k in blocks:
        for g in range(5):
            WRP[k, g * 128 + 96 : g * 128 + 128, :] = jnp.zeros((32, 768), BF)
        for g in range(2):
            WXP[k, g * 128 + 96 : g * 128 + 128, :] = jnp.zeros((32, 768), BF)

    def spread_in(k):
        for g in range(5):
            for q in range(3):
                row = g * 96 + q * 32
                for h in range(2):
                    WRP[k, g * 128 + q * 32 : g * 128 + q * 32 + 32, 384 * h : 384 * h + 384] = WI[
                        h, row // 64, k, row % 64 : row % 64 + 32, :
                    ]

    def spread_mix(k):
        for p in range(4):
            row = (p // 2) * 128 + (p % 2) * 48
            for h in range(2):
                WXP[k, row : row + 48, 384 * h : 384 * h + 384] = WX[h, p, k]

    ACT, LAM, BR, BI = r["ACT"], r["LAM"], r["BR"], r["BI"]

    def project(k):
        spread_in(k)
        gap = PAR[k, 0:1, :]
        ACT[k] = nt(LOW[...], WRP[k])
        ur, ui, fg = ACT[k, :, 0:128], ACT[k, :, 128:256], ACT[k, :, 256:384]
        leak = gap * jax.nn.sigmoid(-fg)
        LAM[k] = 1.0 - leak
        BR[k] = leak * (ur * jax.nn.sigmoid(ur))
        BI[k] = leak * (ui * jax.nn.sigmoid(ui))

    loads["w_x"].wait()
    mixed_rows = nn(apart, r["RM"][...]).astype(BF)
    for h in range(2):
        for p in range(4):
            WX[h, p, 0] = mixed_rows[48 * p : 48 * p + 48, 384 * h : 384 * h + 384]
    spread_mix(0)
    I1.s()
    XM.z()
    project(0)
    for k in ("g", "u", "d0", "d1", "cot"):
        loads[k].wait()
    I1.f()
    I2.s()
    M1.z()

    for i in range(6):
        PERM[i] = r["COT"][:, tiles[i]].astype(F32)

    def take_cot(k, c):
        for i in range(6):
            two = [PERM[i, pl.ds(2 * k + j, 8, stride=steps), :] for j in range(2)]
            GY[pl.ds(pl.multiple_of(16 * k, 16), 16), tiles[i]] = jnp.concatenate(two, axis=0).astype(BF)
        return c

    lax.fori_loop(0, steps // 2, take_cot, 0, unroll=2)
    I2.f()
    I1.c()
    XM.s()
    M2.z()
    for copy in par_copies:
        copy.wait_recv()
    I1.wait()
    lax.fori_loop(1, 3, lambda k, c: (project(k), c)[1], 0)
    I2.c()
    M1.s()
    M3.z()
    XM.c()
    I2.wait()
    project(3)
    M1.f()

    CH, ST, HR, HI = r["CH"], r["ST"], r["HR"], r["HI"]
    turn = []
    for k in blocks:
        ph = PAR[k, 1:2, :]
        turn.append((jnp.cos(ph), jnp.sin(ph)))
    turn8 = [(jnp.broadcast_to(c, (8, LANES)), jnp.broadcast_to(s, (8, LANES))) for c, s in turn]
    cos4 = jnp.concatenate([c for c, s in turn], axis=0)
    sin4 = jnp.concatenate([s for c, s in turn], axis=0)
    chunk_c, chunk_s = power(cos4, sin4, steps)
    whole_c, whole_s = power(cos4, sin4, T)
    zero8 = jnp.zeros((8, LANES), F32)
    zero4 = jnp.zeros((nt_, LANES), F32)

    def rows_of(k):
        return pl.ds(pl.multiple_of(8 * k, 8), 8)

    def ends(n, carry):
        out = []
        for k in blocks:
            hr, hi, lp = carry[k]
            c, s = turn8[k]
            lam = LAM[k, rows_of(n), :]
            nr = lam * (c * hr - s * hi) + BR[k, rows_of(n), :]
            ni = lam * (c * hi + s * hr) + BI[k, rows_of(n), :]
            out.append((nr, ni, lp * lam))
        return tuple(out)

    last = lax.fori_loop(0, steps, ends, tuple((zero8, zero8, zero8 + 1.0) for k in blocks), unroll=4)
    for k in blocks:
        CH[0, 8 * k : 8 * k + 8, :] = last[k][2]
        CH[1, 8 * k : 8 * k + 8, :] = last[k][0]
        CH[2, 8 * k : 8 * k + 8, :] = last[k][1]

    def chunk(i, c):
        return CH[i, pl.ds(c, nt_, stride=8), :]

    def chain(sr, si, sign, keep):
        for c in range(8) if sign > 0 else range(7, -1, -1):
            if keep:
                ST[0, pl.ds(c, nt_, stride=8), :] = sr
                ST[1, pl.ds(c, nt_, stride=8), :] = si
            lp = chunk(0, c)
            pr, pi = lp * chunk_c, sign * (lp * chunk_s)
            sr, si = pr * sr - pi * si + chunk(1, c), pr * si + pi * sr + chunk(2, c)
        return sr, si

    whole_lam = chunk(0, 0)
    for c in range(1, 8):
        whole_lam = whole_lam * chunk(0, c)

    def exchange(which, buf, start):
        def copy_of(o, back):
            at = lax.rem(me + nd - o, nd) if back else lax.rem(me + o, nd)
            row = at if back else me
            return pltpu.make_async_remote_copy(
                buf.at[row],
                buf.at[row],
                r["es"].at[which, o],
                r["er"].at[which, o],
                device_id=(at, z),
                device_id_type=MESH,
            )

        def go(o, c):
            copy_of(o, False).start()
            return c

        def arrive(o, c):
            copy_of(o, True).wait_recv()
            return c

        def leave(o, c):
            copy_of(o, False).wait_send()
            return c

        lax.fori_loop(1, nd, {"go": go, "arrive": arrive, "leave": leave}[start], 0)

    def post(buf, which, sr, si):
        buf[me, 0:4, :] = whole_lam
        buf[me, 4:8, :] = sr
        buf[me, 8:12, :] = si
        buf[me, 12:16, :] = zero4
        exchange(which, buf, "go")

    def carried(buf, which, sign):
        exchange(which, buf, "arrive")

        def lap(k, s):
            at = k if sign > 0 else nd - 1 - k
            reached = (at < me) if sign > 0 else (at > me)
            lp = buf[at, 0:4, :]
            pr, pi = lp * whole_c, sign * (lp * whole_s)
            nr = pr * s[0] - pi * s[1] + buf[at, 4:8, :]
            ni = pr * s[1] + pi * s[0] + buf[at, 8:12, :]
            return jnp.where(reached, nr, s[0]), jnp.where(reached, ni, s[1])

        return lax.fori_loop(0, nd, lap, (zero4, zero4))

    post(r["EX0"], 0, *chain(zero4, zero4, 1.0, False))
    XM.wait()
    lax.fori_loop(1, nt_, lambda k, c: (spread_mix(k), c)[1], 0)
    M2.s()
    start = carried(r["EX0"], 0, 1.0)
    chain(start[0], start[1], 1.0, True)
    for k in blocks:
        HR[k, 0:8, :] = ST[0, 8 * k : 8 * k + 8, :]
        HI[k, 0:8, :] = ST[1, 8 * k : 8 * k + 8, :]

    def states(n, carry):
        out = []
        for k in blocks:
            hr, hi = carry[k]
            c, s = turn8[k]
            lam = LAM[k, rows_of(n), :]
            nr = lam * (c * hr - s * hi) + BR[k, rows_of(n), :]
            ni = lam * (c * hi + s * hr) + BI[k, rows_of(n), :]
            HR[k, rows_of(n + 1), :] = nr
            HI[k, rows_of(n + 1), :] = ni
            out.append((nr, ni))
        return tuple(out)

    def held(k):
        return ST[0, 8 * k : 8 * k + 8, :], ST[1, 8 * k : 8 * k + 8, :]

    lax.fori_loop(0, steps, states, tuple(held(k) for k in blocks), unroll=4)
    M1.c()
    M2.f()

    half = GROUP // 2
    same = one_hot(cells((LANES, LANES), 0) // half == cells((LANES, LANES), 1) // half)

    def group_mean(v):
        top = v.astype(BF)
        rest = (v - top.astype(F32)).astype(BF)
        return (nn(top, same) + nn(rest, same)) * (1.0 / GROUP)

    NR, NI, RS, MIX = r["NR"], r["NI"], r["RS"], r["MIX"]

    def normalise(k, c):
        hr, hi = HR[k, pl.ds(8, T), :], HI[k, pl.ds(8, T), :]
        mean = group_mean(hr + hi)
        hr, hi = hr - mean, hi - mean
        rstd = lax.rsqrt(group_mean(hr * hr + hi * hi) + 1e-05)
        RS[k] = rstd
        hr, hi = hr * rstd, hi * rstd
        NR[k] = hr
        NI[k] = hi
        gr, gi = ACT[k, :, 384:512], ACT[k, :, 512:640]
        MIX[k, :, 0:128] = (hr * PAR[k, 2:3, :] * (gr * jax.nn.sigmoid(gr))).astype(BF)
        MIX[k, :, 128:256] = (hi * PAR[k, 3:4, :] * (gi * jax.nn.sigmoid(gi))).astype(BF)
        return c

    lax.fori_loop(0, nt_, normalise, 0)
    M3.s()

    RES, MID = r["RES"], r["MID"]
    RES[...] = X[...]

    def mix_in(k, c):
        RES[...] += nn(MIX[slot(k)], WXP[slot(k)])
        return c

    lax.fori_loop(0, nt_, mix_in, 0)
    norm_rows(RES, gain2, MID)
    M2.c()
    M3.f()

    HID, DG = r["HID"], r["DG"]

    def gate_w(k, h):
        return WM[h, :, pl.ds(k, 1), 0:96, :].reshape(768, 384)

    def down_w(k, h):
        return WM[h, :, pl.ds(k, 1), 96:144, :].reshape(384, 384)

    def swiglu(k):
        def tile(i, c):
            at = pl.ds(pl.multiple_of(i * 256, 256), 256)
            ga = nn(MID[at, :], gate_w(k, 0))
            ua = nn(MID[at, :], gate_w(k, 1))
            gh = nt(GY[at, 0:384], down_w(k, 0)) + nt(GY[at, 384:768], down_w(k, 1))
            s = jax.nn.sigmoid(ga)
            sl = ga * s
            HID[k, at, :] = (sl * ua).astype(BF)
            DG[k, at, 0:384] = (gh * ua * (s * (1.0 + ga * (1.0 - s)))).astype(BF)
            DG[k, at, 384:768] = (gh * sl).astype(BF)
            return c

        lax.fori_loop(0, T // 256, tile, 0)

    swiglu(0)
    SM = r["SM"]
    for h in range(2):
        SM[h, :, 0:96, :] = (
            tn(MID[...], DG[0, :, 384 * h : 384 * h + 384]).astype(BF).reshape(8, 96, 384)
        )
        SM[h, :, 96:144, :] = (
            tn(HID[0], GY[:, 384 * h : 384 * h + 384]).astype(BF).reshape(8, 48, 384)
        )

    class Summed:
        def __init__(self, name):
            self.bufs = [r[name + k] for k in ("", "0", "1", "2")]
            self.further, self.whole = r[name + "E"], r[name + "F"]
            self.todo = []

        def stage(self, n):
            for copy in self.todo:
                copy.wait_recv()
            self.todo = []
            S = self.bufs[0]
            for h in range(2):
                f, s = order[h]
                spans = ((0, 0, 4), (f, bits[0] * 4, 2), (s, bits[0] * 4 + bits[f] * 2, 1))
                if 1 <= n <= 3:
                    b, first, count = spans[n - 1]
                    mine = pl.ds(first + bits[b] * count, count)
                    S[h, mine] = (S[h, mine].astype(F32) + self.bufs[n][h].astype(F32)).astype(BF)
                if n == 3:
                    part = pl.ds(place[h], 1)
                    for b in range(3, nd.bit_length() - 1):
                        land = self.further.at[h, pl.ds(b - 3, 1)]
                        one = links.send(S.at[h, part], land, partner(b))
                        one.wait()
                        links.open = [c for c in links.open if c is not one]
                        S[h, part] = (
                            S[h, part].astype(F32) + self.further[h, b - 3 : b - 2].astype(F32)
                        ).astype(BF)
                    self.whole[h, part] = S[h, part]
                if n < 3:
                    b, first, count = spans[n]
                    give = first + (1 - bits[b]) * count
                    self.todo.append(
                        links.send(S.at[h, pl.ds(give, count)], self.bufs[n + 1].at[h], partner(b))
                    )
                elif n < 6:
                    b, first, count = (
                        (s, place[h], 1),
                        (f, bits[0] * 4 + bits[f] * 2, 2),
                        (0, bits[0] * 4, 4),
                    )[n - 3]
                    part = self.whole.at[h, pl.ds(first, count)]
                    self.todo.append(links.send(part, part, partner(b)))

    finals = []

    def put_out(src, dst):
        copy = pltpu.make_async_copy(src, dst, r["out"].at[len(finals)])
        copy.start()
        finals.append(copy)

    mlp_sum, early_sum, late_sum = Summed("SM"), Summed("SE"), Summed("SL")
    mlp_sum.stage(0)
    M1.wait()
    swiglu(1)
    M3.c()
    mlp_sum.stage(1)
    M2.wait()
    swiglu(2)
    M3.wait()
    swiglu(3)

    GRES, NAT = r["GRES"], r["NAT"]
    NAT[...] = jnp.zeros((T, 768), F32)

    def back_mid(k, c):
        j = slot(k)
        NAT[...] += nt(DG[j, :, 0:384], gate_w(j, 0)) + nt(DG[j, :, 384:768], gate_w(j, 1))
        return c

    lax.fori_loop(0, nt_, back_mid, 0)
    mlp_sum.stage(2)
    LOWR = r["MID"]

    def back_second(i, total):
        at = pl.ds(pl.multiple_of(i * 128, 128), 128)
        res, gmid = RES[at, :], NAT[at, :]
        q2 = lax.rsqrt(jnp.mean(res * res, -1, keepdims=True) + 1e-06)
        p = gmid * gain2
        back = q2 * p - res * (q2 * q2 * q2) * jnp.mean(p * res, -1, keepdims=True)
        gres = GY[at, :].astype(F32) + back
        GRES[at, :] = gres
        LOWR[at, :] = gres.astype(BF)
        return total + jnp.sum((gmid * res * q2).reshape(16, 8, 768), 0)

    VEC = r["EX3"]
    gnorm2 = down_sum(lax.fori_loop(0, T // 128, back_second, jnp.zeros((8, 768), F32)))
    for i in range(6):
        VEC[me, 6 + i : 7 + i, :] = gnorm2[:, 128 * i : 128 * i + 128]

    G = DG
    rows, cols = cells((256, 256), 0), cells((256, 256), 1)
    lane = rows % 128
    together = one_hot((cols == 2 * lane + rows // 128) & (lane < ch))

    def back_norm(k, own):
        gact = nt(LOWR[...], WXP[k])
        rstd = RS[k]
        parts, sums, dots = [], 0.0, 0.0
        group = []
        for i, hn in enumerate((NR[k], NI[k])):
            pre = ACT[k, :, 384 + 128 * i : 512 + 128 * i]
            gain = PAR[k, 2 + i : 3 + i, :]
            ga = gact[:, 128 * i : 128 * i + 128]
            s = jax.nn.sigmoid(pre)
            sl = pre * s
            gh = ga * hn
            G[k, :, 384 + 128 * i : 512 + 128 * i] = (
                gh * gain * (s * (1.0 + pre * (1.0 - s)))
            ).astype(BF)
            if own:
                group.append(down_sum(gh * sl))
            p = ga * gain * sl
            parts.append((p, hn))
            sums = sums + p
            dots = dots + p * hn
        sums, dots = group_mean(sums), group_mean(dots)
        for buf, (p, hn) in zip((BR, BI), parts):
            buf[k] = rstd * (p - sums - hn * dots)
        if own:
            both = jnp.broadcast_to(jnp.concatenate(group, axis=1), (8, 256))
            both = exact(both, together.astype(F32), ((1,), (0,)))
            VEC[me, 14:15, :] = both[0:1, 0:128]
            VEC[me, 15:16, :] = both[0:1, 128:256]

    def back_step(n, carry, some, keep):
        n = steps - 1 - n
        out = []
        for k, (ur, ui) in zip(some, carry):
            c, s = turn8[k]
            lam = LAM[k, rows_of(n), :]
            er = BR[k, rows_of(n), :] + ur
            ei = BI[k, rows_of(n), :] + ui
            if keep:
                BR[k, rows_of(n), :] = er
                BI[k, rows_of(n), :] = ei
            out.append((lam * (c * er + s * ei), lam * (c * ei - s * er)))
        return tuple(out)

    def back_ends(some, buf, which):
        body = functools.partial(back_step, some=some, keep=False)
        first = lax.fori_loop(0, steps, body, tuple((zero8, zero8) for k in some), unroll=4)
        for k, (ur, ui) in zip(some, first):
            CH[1, 8 * k : 8 * k + 8, :] = ur
            CH[2, 8 * k : 8 * k + 8, :] = ui
        post(buf, which, *chain(zero4, zero4, -1.0, False))

    def back_states(some, buf, which):
        sr, si = carried(buf, which, -1.0)
        chain(sr, si, -1.0, True)
        body = functools.partial(back_step, some=some, keep=True)
        lax.fori_loop(0, steps, body, tuple(held(k) for k in some), unroll=4)

    def back_gates(k, own):
        c, s = turn[k]
        er, ei = BR[k], BI[k]
        hr, hi = HR[k, pl.ds(0, T), :], HI[k, pl.ds(0, T), :]
        gap = PAR[k, 0:1, :]
        gar, gai = er * hr + ei * hi, ei * hr - er * hi
        ur, ui, fg = ACT[k, :, 0:128], ACT[k, :, 128:256], ACT[k, :, 256:384]
        su, si, sf = jax.nn.sigmoid(ur), jax.nn.sigmoid(ui), jax.nn.sigmoid(-fg)
        leak = gap * sf
        gleak = er * (ur * su) + ei * (ui * si) - (c * gar + s * gai)
        G[k, :, 0:128] = (er * leak * (su * (1.0 + ur * (1.0 - su)))).astype(BF)
        G[k, :, 128:256] = (ei * leak * (si * (1.0 + ui * (1.0 - si)))).astype(BF)
        G[k, :, 256:384] = (-gleak * leak * (1.0 - sf)).astype(BF)
        if own:
            VEC[me, 12:13, :] = down_sum(gleak * sf)
            VEC[me, 13:14, :] = down_sum((1.0 - leak) * (c * gai - s * gar))

    back_norm(0, True)
    back_ends([0], r["EX1"], 1)
    mlp_sum.stage(3)

    SE, SL = r["SE"], r["SL"]
    gate_cols = nn(G[0, :, 384:640], together)[:, 0 : 2 * ch].astype(BF)
    mix_cols = nn(MIX[0], together)[:, 0 : 2 * ch].astype(BF)
    for h in range(2):
        at = slice(384 * h, 384 * h + 384)
        SE[h, 0:4] = tn(gate_cols, LOW[:, at]).astype(BF).reshape(4, 48, 384)
        SE[h, 4:8] = tn(mix_cols, LOWR[:, at]).astype(BF).reshape(4, 48, 384)
    early_sum.stage(0)
    lax.fori_loop(1, nt_, lambda k, c: (back_norm(k, False), c)[1], 0)
    mlp_sum.stage(4)
    early_sum.stage(1)
    back_states([0], r["EX1"], 1)
    back_gates(0, True)
    rows, cols = cells((384, 384), 0), cells((384, 384), 1)
    lane, g = rows % 128, rows // 128
    to = jnp.where(g < 2, 2 * lane + g, 2 * ch + lane)
    late_cols = nn(G[0, :, 0:384], one_hot((cols == to) & (lane < ch))).astype(BF)
    for h in range(2):
        SL[h] = tn(late_cols, LOW[:, 384 * h : 384 * h + 384]).astype(BF).reshape(8, 48, 384)
    late_sum.stage(0)
    early_sum.stage(2)

    back_ends(blocks[1:], r["EX2"], 2)
    late_sum.stage(1)
    mlp_sum.stage(5)
    early_sum.stage(3)

    def down(k, c):
        j = slot(k)
        for h in range(2):
            RES[:, 384 * h : 384 * h + 384] += nn(HID[j], down_w(j, h))
        return c

    lax.fori_loop(0, nt_, down, 0)
    late_sum.stage(2)
    early_sum.stage(4)
    back_states(blocks[1:], r["EX2"], 2)
    late_sum.stage(3)
    for k in blocks[1:]:
        back_gates(k, False)
    early_sum.stage(5)
    late_sum.stage(4)
    mlp_sum.stage(6)
    put_out(r["SMF"], r["o_mlp"])

    NAT[...] = jnp.zeros((T, 768), F32)

    def back_in(k, c):
        NAT[...] += nn(G[slot(k), :, 0:640], WRP[slot(k)])
        return c

    lax.fori_loop(0, nt_, back_in, 0)

    def back_first(i, total):
        at = pl.ds(pl.multiple_of(i * 128, 128), 128)
        x, gin = X[at, :], NAT[at, :]
        q1 = lax.rsqrt(jnp.mean(x * x, -1, keepdims=True) + 1e-06)
        p = gin * gain1
        GRES[at, :] += q1 * p - x * (q1 * q1 * q1) * jnp.mean(p * x, -1, keepdims=True)
        return total + jnp.sum((gin * x * q1).reshape(16, 8, 768), 0)

    gnorm1 = down_sum(lax.fori_loop(0, T // 128, back_first, jnp.zeros((8, 768), F32)))
    for i in range(6):
        VEC[me, i : i + 1, :] = gnorm1[:, 128 * i : 128 * i + 128]
    exchange(3, VEC, "go")
    late_sum.stage(5)
    early_sum.stage(6)
    put_out(r["SEF"], r["o_early"])

    def put_from(buf):
        def put(k, c):
            for i in range(6):
                PERM[i, pl.ds(k, 8, stride=steps), :] = buf[pl.ds(pl.multiple_of(8 * k, 8), 8), tiles[i]]
            return c

        lax.fori_loop(0, steps, put, 0, unroll=4)

    put_from(GRES)
    for i in range(6):
        NAT[:, tiles[i]] = PERM[i]
    put_out(NAT, r["tok"])
    put_from(RES)
    for i in range(6):
        r["COT"][:, tiles[i]] = PERM[i].astype(BF)
    put_out(r["COT"], r["mixed"])
    late_sum.stage(6)
    put_out(r["SLF"], r["o_late"])

    exchange(3, VEC, "arrive")
    total = VEC[0]
    for k in range(1, nd):
        total = total + VEC[k]
    r["vec"][...] = total
    for which in range(4):
        exchange(which, r["EX%d" % which], "leave")
    links.drain()
    for copy in finals:
        copy.wait()


def writer(names, *refs):
    r = dict(zip(names, refs))
    sem = r["sem"]
    count = [0]

    def copy(src, dst):
        c = pltpu.make_async_copy(src, dst, sem.at[count[0]])
        count[0] += 1
        c.start()
        return c

    ins = {
        "late": copy(r["late"], r["L"]),
        "early": copy(r["early"], r["E"]),
        "mlp": copy(r["mlp"], r["M"]),
    }
    outs = [copy(r["mixed_in"], r["mixed"]), copy(r["tok_in"], r["tok"])]
    ch = r["gap"].shape[1]
    vec = r["vec"]
    r["gn1"][...] = vec[0:6, :]
    r["gn2"][...] = vec[6:12, :]
    r["gap"][...] = vec[12:13, 0:ch]
    r["phase"][...] = vec[13:14, 0:ch]
    r["group"][...] = jnp.concatenate([vec[14:15, :], vec[15:16, 0 : 2 * ch - LANES]], axis=1)
    for name, a, outs_of in (
        ("late", "L", (("LF", 0, 6, (("g_in", 0, 4), ("g_f", 4, 6))),)),
        ("early", "E", (("EF", 0, 8, (("g_o", 0, 4), ("g_x", 4, 8))),)),
    ):
        ins[name].wait()
        for f, lo, hi, dests in outs_of:
            for h in range(2):
                r[f][lo:hi, :, 384 * h : 384 * h + 384] = r[a][h, lo:hi].astype(F32)
            for dst, p, q in dests:
                outs.append(copy(r[f].at[p:q], r[dst]))
    ins["mlp"].wait()
    for h, name in ((0, "g_g"), (1, "g_u")):
        r["GF"][h] = r["M"][h, :, 0:96, :].astype(F32)
        outs.append(copy(r["GF"].at[h], r[name]))
        r["DF"][:, :, 384 * h : 384 * h + 384] = r["M"][h, :, 96:144, :].astype(F32)
    outs.append(copy(r["DF"], r["g_d"]))
    for c in outs:
        c.wait()


def local(nd, nt_, *args):
    (tokens, cot, g1, w_in, w_f, w_o, gap, phase, gg, w_mix, g2, wg, wu, wd) = args
    T, D = tokens.shape
    ch = w_f.shape[1]
    vmem = pl.BlockSpec(memory_space=pltpu.VMEM)
    hbm = pl.BlockSpec(memory_space=pl.ANY)
    given = dict(
        tokens=tokens,
        cot=cot,
        g1=g1.reshape(6, LANES),
        w_i=w_in.T,
        w_f=w_f.T,
        w_o=w_o.T,
        gap=gap.reshape(1, ch),
        phase=phase.reshape(1, ch),
        gg=gg.reshape(1, 2 * ch),
        w_mix=w_mix,
        g2=g2.reshape(6, LANES),
        wg=wg.reshape(8, 96, 384),
        wu=wu.reshape(8, 96, 384),
        wd=wd.reshape(8, 48, D),
    )
    small = ("g1", "g2", "gap", "phase", "gg", "vec")
    shape = jax.ShapeDtypeStruct
    raw = dict(
        mixed=shape((T, D), BF),
        tok=shape((T, D), F32),
        o_mlp=shape((2, 8, 144, 384), BF),
        o_early=shape((2, 8, 48, 384), BF),
        o_late=shape((2, 8, 48, 384), BF),
        vec=shape((16, LANES), F32),
    )
    scratch = scratch_list(nd, nt_, T)
    mixed, tok, o_mlp, o_early, o_late, vec = pl.pallas_call(
        functools.partial(kernel, nd, nt_, T, list(given) + list(raw) + list(scratch)),
        out_shape=list(raw.values()),
        in_specs=[vmem if k in small else hbm for k in given],
        out_specs=[vmem if k in small else hbm for k in raw],
        scratch_shapes=list(scratch.values()),
        compiler_params=pltpu.CompilerParams(
            collective_id=0, has_side_effects=True, vmem_limit_bytes=63 * 2**20
        ),
        name="layer",
    )(*given.values())

    got = dict(mixed_in=mixed, tok_in=tok, mlp=o_mlp, early=o_early, late=o_late, vec=vec)
    final = dict(
        mixed=shape((T, D), BF),
        tok=shape((T, D), F32),
        gn1=shape((6, LANES), F32),
        g_in=shape((4, 48, D), F32),
        g_f=shape((2, 48, D), F32),
        g_o=shape((4, 48, D), F32),
        gap=shape((1, ch), F32),
        phase=shape((1, ch), F32),
        group=shape((1, 2 * ch), F32),
        g_x=shape((4, 48, D), F32),
        gn2=shape((6, LANES), F32),
        g_g=shape((8, 96, 384), F32),
        g_u=shape((8, 96, 384), F32),
        g_d=shape((8, 48, D), F32),
    )
    held = dict(
        L=pltpu.VMEM((2, 8, 48, 384), BF),
        E=pltpu.VMEM((2, 8, 48, 384), BF),
        M=pltpu.VMEM((2, 8, 144, 384), BF),
        LF=pltpu.VMEM((6, 48, D), F32),
        EF=pltpu.VMEM((8, 48, D), F32),
        GF=pltpu.VMEM((2, 8, 96, 384), F32),
        DF=pltpu.VMEM((8, 48, D), F32),
        sem=pltpu.SemaphoreType.DMA((16,)),
    )
    blocky = ("gn1", "gn2", "gap", "phase", "group")
    outs = pl.pallas_call(
        functools.partial(writer, list(got) + list(final) + list(held)),
        out_shape=list(final.values()),
        in_specs=[vmem if k == "vec" else hbm for k in got],
        out_specs=[vmem if k in blocky else hbm for k in final],
        scratch_shapes=list(held.values()),
        compiler_params=pltpu.CompilerParams(vmem_limit_bytes=32 * 2**20),
        name="writer",
    )(*got.values())
    o = dict(zip(final, outs))
    return (
        o["mixed"],
        o["tok"],
        o["gn1"].reshape(D),
        o["g_in"].reshape(2 * ch, D).T,
        o["g_f"].reshape(ch, D).T,
        o["g_o"].reshape(2 * ch, D).T,
        o["gap"].reshape(ch),
        o["phase"].reshape(ch),
        o["group"].reshape(2 * ch),
        o["g_x"].reshape(2 * ch, D),
        o["gn2"].reshape(D),
        o["g_g"].reshape(D, 384),
        o["g_u"].reshape(D, 384),
        o["g_d"].reshape(384, D),
    )


def solution(mesh):
    in_specs = (
        P("dp", None),
        P("dp", None),
        P(),
        P(None, "tp"),
        P(None, "tp"),
        P(None, "tp"),
        P("tp"),
        P("tp"),
        P("tp"),
        P("tp", None),
        P(),
        P(None, "tp"),
        P(None, "tp"),
        P("tp", None),
    )
    out_specs = (
        P("dp", None),
        P("dp", None),
        P(),
        P(None, "tp"),
        P(None, "tp"),
        P(None, "tp"),
        P("tp"),
        P("tp"),
        P("tp"),
        P("tp", None),
        P(),
        P(None, "tp"),
        P(None, "tp"),
        P("tp", None),
    )
    body = functools.partial(local, mesh.shape["dp"], mesh.shape["tp"])
    return jax.shard_map(body, mesh=mesh, in_specs=in_specs, out_specs=out_specs, check_vma=False)
```

```python
import functools

import jax
import jax.numpy as jnp
from jax import lax
from jax.experimental import pallas as pl
from jax.experimental.pallas import tpu as pltpu
from jax.sharding import PartitionSpec as P

MESH = pl.DeviceIdType.MESH
BF = jnp.bfloat16
F32 = jnp.float32
GROUP = 64
LANES = 128
SENDS = 56


def nn(a, b):
    return jnp.dot(a, b, preferred_element_type=F32)


def nt(a, b):
    return lax.dot_general(a, b, (((1,), (1,)), ((), ())), preferred_element_type=F32)


def tn(a, b):
    return lax.dot_general(a, b, (((0,), (0,)), ((), ())), preferred_element_type=F32)


def exact(a, b, dims):
    return lax.dot_general(
        a, b, (dims, ((), ())), precision=lax.Precision.HIGHEST, preferred_element_type=F32
    )


def cells(shape, axis):
    return lax.broadcasted_iota(jnp.int32, shape, axis)


def one_hot(flags):
    return jnp.where(flags, 1.0, 0.0).astype(BF)


def down_sum(v):
    if v.shape[0] > 8:
        v = jnp.sum(v.reshape(v.shape[0] // 8, 8, v.shape[1]), 0)
    v = v[0:4] + v[4:8]
    v = v[0:2] + v[2:4]
    return v[0:1] + v[1:2]


def power(c, s, n):
    out = None
    while n:
        if n % 2:
            out = (c, s) if out is None else (out[0] * c - out[1] * s, out[0] * s + out[1] * c)
        c, s = c * c - s * s, 2.0 * c * s
        n //= 2
    return out


def sum_buffers(name, nd, rows):
    further = max(1, nd.bit_length() - 4)
    counts = (("", 8), ("0", 4), ("1", 2), ("2", 1), ("E", further), ("F", 8))
    return {name + k: pltpu.VMEM((2, n, rows, 384), BF) for k, n in counts}


def scratch_list(nd, nt_, T):
    dma = pltpu.SemaphoreType.DMA
    return dict(
        RI=pltpu.VMEM((192, 768), BF),
        RF=pltpu.VMEM((96, 768), BF),
        RO=pltpu.VMEM((192, 768), BF),
        RM=pltpu.VMEM((192, 768), BF),
        WI=pltpu.VMEM((2, 8, nt_, 64, 384), BF),
        WX=pltpu.VMEM((2, 4, nt_, 48, 384), BF),
        WM=pltpu.VMEM((2, 8, nt_, 144, 384), BF),
        PAR=pltpu.VMEM((nt_, 8, LANES), F32),
        WRP=pltpu.VMEM((nt_, 640, 768), BF),
        WXP=pltpu.VMEM((nt_, 256, 768), BF),
        X=pltpu.VMEM((T, 768), F32),
        GY=pltpu.VMEM((T, 768), BF),
        LOW=pltpu.VMEM((T, 768), BF),
        ACT=pltpu.VMEM((nt_, T, 640), F32),
        LAM=pltpu.VMEM((nt_, T, LANES), F32),
        BR=pltpu.VMEM((nt_, T, LANES), F32),
        BI=pltpu.VMEM((nt_, T, LANES), F32),
        HR=pltpu.VMEM((nt_, T + 8, LANES), F32),
        HI=pltpu.VMEM((nt_, T + 8, LANES), F32),
        N2=pltpu.VMEM((max(6, 2 * nt_), T, LANES), F32),
        RS=pltpu.VMEM((nt_, T, LANES), F32),
        MIX=pltpu.VMEM((nt_, T, 256), BF),
        RES=pltpu.VMEM((T, 768), F32),
        MID=pltpu.VMEM((T, 768), BF),
        HID=pltpu.VMEM((nt_, T, 384), BF),
        DG=pltpu.VMEM((nt_, T, 768), BF),
        ACC=pltpu.VMEM((nt_, T, 768), F32),
        CH=pltpu.VMEM((3, nt_ * 8, LANES), F32),
        ST=pltpu.VMEM((2, nt_ * 8, LANES), F32),
        EX0=pltpu.VMEM((nd, 16, LANES), F32),
        EX1=pltpu.VMEM((nd, 16, LANES), F32),
        EX2=pltpu.VMEM((nd, 16, LANES), F32),
        EX3=pltpu.VMEM((nd, 16, LANES), F32),
        **sum_buffers("SM", nd, 144),
        **sum_buffers("SE", nd, 48),
        **sum_buffers("SL", nd, 48),
        loc=dma((16,)),
        out=dma((8,)),
        ss=dma((SENDS,)),
        rs=dma((92 + 6 * max(0, nd.bit_length() - 4),)),
        fs=dma((8,)),
        es=dma((4, nd)),
        er=dma((4, nd)),
    )


class Links:
    def __init__(self, ss, rs, fs):
        self.ss, self.rs, self.fs = ss, rs, fs
        self.free, self.received, self.asked = list(range(SENDS)), 0, 0
        self.open, self.old, self.some = [], [], []

    def send(self, src, dst, dev):
        k, n = self.received, self.free.pop(0)
        self.received += 1
        copy = pltpu.make_async_remote_copy(
            src, dst, self.ss.at[n], self.rs.at[k], device_id=dev, device_id_type=MESH
        )
        copy.start()
        self.open.append((copy, n))
        return copy

    def retire(self, copies):
        self.old += [pair for c in copies for pair in self.open if pair[0] is c]
        while len(self.old) > 4:
            pair = self.old.pop(0)
            pair[0].wait_send()
            self.free.append(pair[1])
            self.open = [p for p in self.open if p is not pair]

    def send_if(self, flag, k, src, dst, dev):
        n = self.asked
        self.asked += 1
        copy = pltpu.make_async_remote_copy(
            src, dst, self.fs.at[n], self.rs.at[k], device_id=dev, device_id_type=MESH
        )

        @pl.when(flag)
        def _():
            copy.start()

        self.some.append((flag, copy))
        return copy

    def drain(self):
        for copy, _ in self.open:
            copy.wait_send()
        for flag, copy in self.some:
            pl.when(flag)(copy.wait_send)


def kernel(nd, nt_, T, names, *refs):
    r = dict(zip(names, refs))
    me, z = lax.axis_index("dp"), lax.axis_index("tp")
    steps = T // 8
    ch = r["w_f"].shape[0]
    blocks = list(range(nt_))

    def flip(bit):
        return me + bit - 2 * bit * ((me // bit) % 2)

    bits = (me % 2, (me // 2) % 2, (me // 4) % 2)
    order = ((1, 2), (2, 1))
    place = [bits[0] * 4 + bits[f] * 2 + bits[s] for f, s in order]
    wide = [bits[0] * 2 + bits[f] for f, s in order]
    links = Links(r["ss"], r["rs"], r["fs"])
    away = [0, 1, 3, 2] if nt_ == 4 else blocks

    def slot(k):
        o = lax.rem(k + nt_ - z, nt_)
        if nt_ != 4:
            return o
        return jnp.where(o == 2, 3, jnp.where(o == 3, 2, o))

    barrier = pltpu.get_barrier_semaphore()

    def greet_dp(o, c):
        pl.semaphore_signal(barrier, 1, device_id=(lax.rem(me + o, nd), z), device_id_type=MESH)
        return c

    def greet_tp(o, c):
        pl.semaphore_signal(barrier, 1, device_id=(me, lax.rem(z + o, nt_)), device_id_type=MESH)
        return c

    lax.fori_loop(1, nt_, greet_tp, 0)
    lax.fori_loop(1, nd, greet_dp, 0)

    WM = r["WM"]
    COT = r["DG"].at[nt_ - 1]
    loads = {}
    for k, (name, src, dst) in enumerate(
        (
            ("w_i", r["w_i"], r["RI"]),
            ("w_f", r["w_f"], r["RF"]),
            ("w_o", r["w_o"], r["RO"]),
            ("tokens", r["tokens"], r["MID"]),
            ("w_x", r["w_mix"], r["RM"]),
            ("g", r["wg"], WM.at[0, :, 0, 0:96, :]),
            ("u", r["wu"], WM.at[1, :, 0, 0:96, :]),
            ("d0", r["wd"].at[:, :, 0:384], WM.at[0, :, 0, 96:144, :]),
            ("d1", r["wd"].at[:, :, 384:768], WM.at[1, :, 0, 96:144, :]),
            ("cot", r["cot"], COT),
        )
    ):
        loads[name] = pltpu.make_async_copy(src, dst, r["loc"].at[k])
        loads[name].start()

    WI, WX, WRP, WXP, PAR = r["WI"], r["WX"], r["WRP"], r["WXP"], r["PAR"]
    rows, cols = cells((2 * ch, 2 * ch), 0), cells((2 * ch, 2 * ch), 1)
    apart = one_hot(cols == jnp.where(rows < ch, 2 * rows, 2 * (rows - ch) + 1))
    for k in ("w_i", "w_f", "w_o"):
        loads[k].wait()
    turned = jnp.concatenate(
        [
            nn(apart, r["RI"][...]).astype(BF),
            r["RF"][...],
            nn(apart, r["RO"][...]).astype(BF),
            jnp.zeros((32, 768), BF),
        ],
        axis=0,
    )
    for h in range(2):
        for p in range(8):
            WI[h, p, 0] = turned[64 * p : 64 * p + 64, 384 * h : 384 * h + 384]
    PAR[0] = jnp.zeros((8, LANES), F32)
    PAR[0, 0:1, 0:ch] = r["gap"][...]
    PAR[0, 1:2, 0:ch] = r["phase"][...]
    gains = exact(
        jnp.broadcast_to(r["gg"][...], (8, 2 * ch)), apart.astype(F32), ((1,), (1,))
    )
    PAR[0, 2:3, 0:ch] = gains[0:1, 0:ch]
    PAR[0, 3:4, 0:ch] = gains[0:1, ch : 2 * ch]

    def across(o):
        return (me, lax.rem(z + nt_ - o, nt_))

    def partner(b):
        return (flip(1 << b), z)

    class Unit:
        def __init__(self, buf, slots, portions, far=None):
            self.buf, self.slots, self.portions, self.far = buf, slots, portions, far
            self.at = place if portions == 8 else wide
            self.todo = []

        def wait(self):
            for copy in self.todo:
                copy.wait_recv()
            links.retire(self.todo)
            self.todo = []

        def hop(self, h, b, start, count):
            part = self.buf.at[h, pl.ds(start, count), pl.ds(self.slots[0], len(self.slots))]
            self.todo.append(links.send(part, part, partner(b)))

        def held(self, h, s):
            if self.far is None:
                return self.buf.at[h, self.at[h], s]
            return self.buf.at[h, pl.ds(bits[0] * 4 + bits[order[h][0]] * 2, 2), s]

        def z(self):
            for s in self.slots:
                for h in range(2):
                    own, to = self.held(h, 0), self.held(h, s)
                    if self.far is None or nt_ != 4:
                        self.todo.append(links.send(own, to, across(away[s])))
                    else:
                        k = links.received
                        links.received += 1
                        flag = z != (0 if s == 1 else 3)
                        self.todo.append(links.send_if(flag, k, own, to, across(away[s])))
                        self.first = k - h

        def forward(self):
            if nt_ != 4:
                return
            s = self.slots[0]
            who, end = (2, 3) if s == 1 else (1, 0)
            for h in range(2):
                held, to = self.held(h, self.far), self.held(h, s)
                links.send_if(z == who, self.first + h, held, to, (me, end))

        def s(self):
            self.wait()
            for h in range(2):
                f, s = order[h]
                if self.portions == 8:
                    self.hop(h, s, place[h], 1)
                else:
                    self.hop(h, f, wide[h], 1)

        def f(self):
            self.wait()
            for h in range(2):
                f, s = order[h]
                self.hop(h, f, bits[0] * 4 + bits[f] * 2, 2)

        def c(self):
            self.wait()
            n = self.portions // 2
            for h in range(2):
                self.hop(h, 0, bits[0] * n, n)

    I1, I2 = Unit(WI, blocks[1:3], 8), Unit(WI, blocks[3:], 8)
    XM = Unit(WX, blocks[1:], 4)
    M1, M2, M3 = Unit(WM, [1], 8, 3), Unit(WM, [2], 8, 3), Unit(WM, [3], 8)

    pl.semaphore_wait(barrier, nd - 1 + nt_ - 1)
    I1.z()
    par_copies = [links.send(PAR.at[0], PAR.at[s], across(away[s])) for s in blocks[1:]]

    PERM, X, GY, LOW = r["N2"], r["X"], r["GY"], r["LOW"]
    loads["tokens"].wait()
    tiles = [slice(LANES * i, LANES * i + LANES) for i in range(6)]
    for i in range(6):
        PERM[i] = r["MID"][:, tiles[i]].astype(F32)

    def take(k, c):
        for i in range(6):
            X[pl.ds(pl.multiple_of(8 * k, 8), 8), tiles[i]] = PERM[i, pl.ds(k, 8, stride=steps), :]
        return c

    lax.fori_loop(0, steps, take, 0, unroll=4)

    def whole_row(ref):
        return jnp.concatenate([ref[i : i + 1, :] for i in range(6)], axis=1)

    gain1, gain2 = whole_row(r["g1"]), whole_row(r["g2"])

    def norm_rows(src, gain, dst):
        def body(i, c):
            at = pl.ds(pl.multiple_of(i * 128, 128), 128)
            v = src[at, :]
            q = lax.rsqrt(jnp.mean(v * v, -1, keepdims=True) + 1e-06)
            dst[at, :] = (v * q * gain).astype(BF)
            return c

        lax.fori_loop(0, T // 128, body, 0)

    norm_rows(X, gain1, LOW)
    I2.z()
    for k in ("g", "u", "d0", "d1", "cot"):
        loads[k].wait()
    M3.z()

    for k in blocks:
        for g in range(5):
            WRP[k, g * 128 + 96 : g * 128 + 128, :] = jnp.zeros((32, 768), BF)
        for g in range(2):
            WXP[k, g * 128 + 96 : g * 128 + 128, :] = jnp.zeros((32, 768), BF)

    def spread_in(k):
        for g in range(5):
            for q in range(3):
                row = g * 96 + q * 32
                for h in range(2):
                    WRP[k, g * 128 + q * 32 : g * 128 + q * 32 + 32, 384 * h : 384 * h + 384] = WI[
                        h, row // 64, k, row % 64 : row % 64 + 32, :
                    ]

    def spread_mix(k):
        for p in range(4):
            row = (p // 2) * 128 + (p % 2) * 48
            for h in range(2):
                WXP[k, row : row + 48, 384 * h : 384 * h + 384] = WX[h, p, k]

    ACT, LAM, BR, BI = r["ACT"], r["LAM"], r["BR"], r["BI"]

    def project(k):
        spread_in(k)
        gap = PAR[k, 0:1, :]
        ACT[k] = nt(LOW[...], WRP[k])
        ur, ui, fg = ACT[k, :, 0:128], ACT[k, :, 128:256], ACT[k, :, 256:384]
        leak = gap * jax.nn.sigmoid(-fg)
        LAM[k] = 1.0 - leak
        BR[k] = leak * (ur * jax.nn.sigmoid(ur))
        BI[k] = leak * (ui * jax.nn.sigmoid(ui))

    loads["w_x"].wait()
    mixed_rows = nn(apart, r["RM"][...]).astype(BF)
    for h in range(2):
        for p in range(4):
            WX[h, p, 0] = mixed_rows[48 * p : 48 * p + 48, 384 * h : 384 * h + 384]
    spread_mix(0)
    I1.s()
    project(0)
    I1.f()
    M1.z()
    M2.z()
    I2.s()

    for i in range(6):
        PERM[i] = COT[:, tiles[i]].astype(F32)

    def take_cot(k, c):
        for i in range(6):
            two = [PERM[i, pl.ds(2 * k + j, 8, stride=steps), :] for j in range(2)]
            GY[pl.ds(pl.multiple_of(16 * k, 16), 16), tiles[i]] = jnp.concatenate(two, axis=0).astype(BF)
        return c

    lax.fori_loop(0, steps // 2, take_cot, 0, unroll=2)
    I1.c()
    I2.f()
    XM.z()
    for copy in par_copies:
        copy.wait_recv()
    I1.wait()
    lax.fori_loop(1, 3, lambda k, c: (project(k), c)[1], 0)
    M3.s()
    I2.c()
    I2.wait()
    project(3)
    M3.f()
    M1.forward()
    M2.forward()

    CH, ST, HR, HI = r["CH"], r["ST"], r["HR"], r["HI"]
    turn = []
    for k in blocks:
        ph = PAR[k, 1:2, :]
        turn.append((jnp.cos(ph), jnp.sin(ph)))
    turn8 = [(jnp.broadcast_to(c, (8, LANES)), jnp.broadcast_to(s, (8, LANES))) for c, s in turn]
    cos4 = jnp.concatenate([c for c, s in turn], axis=0)
    sin4 = jnp.concatenate([s for c, s in turn], axis=0)
    chunk_c, chunk_s = power(cos4, sin4, steps)
    whole_c, whole_s = power(cos4, sin4, T)
    zero8 = jnp.zeros((8, LANES), F32)
    zero4 = jnp.zeros((nt_, LANES), F32)

    def rows_of(k):
        return pl.ds(pl.multiple_of(8 * k, 8), 8)

    def ends(n, carry):
        out = []
        for k in blocks:
            hr, hi, lp = carry[k]
            c, s = turn8[k]
            lam = LAM[k, rows_of(n), :]
            nr = lam * (c * hr - s * hi) + BR[k, rows_of(n), :]
            ni = lam * (c * hi + s * hr) + BI[k, rows_of(n), :]
            out.append((nr, ni, lp * lam))
        return tuple(out)

    last = lax.fori_loop(0, steps, ends, tuple((zero8, zero8, zero8 + 1.0) for k in blocks), unroll=4)
    for k in blocks:
        CH[0, 8 * k : 8 * k + 8, :] = last[k][2]
        CH[1, 8 * k : 8 * k + 8, :] = last[k][0]
        CH[2, 8 * k : 8 * k + 8, :] = last[k][1]

    def chunk(i, c):
        return CH[i, pl.ds(c, nt_, stride=8), :]

    def chain(sr, si, sign, keep):
        for c in range(8) if sign > 0 else range(7, -1, -1):
            if keep:
                ST[0, pl.ds(c, nt_, stride=8), :] = sr
                ST[1, pl.ds(c, nt_, stride=8), :] = si
            lp = chunk(0, c)
            pr, pi = lp * chunk_c, sign * (lp * chunk_s)
            sr, si = pr * sr - pi * si + chunk(1, c), pr * si + pi * sr + chunk(2, c)
        return sr, si

    whole_lam = chunk(0, 0)
    for c in range(1, 8):
        whole_lam = whole_lam * chunk(0, c)

    def exchange(which, buf, start):
        def copy_of(o, back):
            at = lax.rem(me + nd - o, nd) if back else lax.rem(me + o, nd)
            row = at if back else me
            return pltpu.make_async_remote_copy(
                buf.at[row],
                buf.at[row],
                r["es"].at[which, o],
                r["er"].at[which, o],
                device_id=(at, z),
                device_id_type=MESH,
            )

        def go(o, c):
            copy_of(o, False).start()
            return c

        def arrive(o, c):
            copy_of(o, True).wait_recv()
            return c

        def leave(o, c):
            copy_of(o, False).wait_send()
            return c

        lax.fori_loop(1, nd, {"go": go, "arrive": arrive, "leave": leave}[start], 0)

    def post(buf, which, sr, si):
        buf[me, 0:4, :] = whole_lam
        buf[me, 4:8, :] = sr
        buf[me, 8:12, :] = si
        buf[me, 12:16, :] = zero4
        exchange(which, buf, "go")

    def carried(buf, which, sign):
        exchange(which, buf, "arrive")

        def lap(k, s):
            at = k if sign > 0 else nd - 1 - k
            reached = (at < me) if sign > 0 else (at > me)
            lp = buf[at, 0:4, :]
            pr, pi = lp * whole_c, sign * (lp * whole_s)
            nr = pr * s[0] - pi * s[1] + buf[at, 4:8, :]
            ni = pr * s[1] + pi * s[0] + buf[at, 8:12, :]
            return jnp.where(reached, nr, s[0]), jnp.where(reached, ni, s[1])

        return lax.fori_loop(0, nd, lap, (zero4, zero4))

    post(r["EX0"], 0, *chain(zero4, zero4, 1.0, False))
    XM.s()
    start = carried(r["EX0"], 0, 1.0)
    chain(start[0], start[1], 1.0, True)
    for k in blocks:
        HR[k, 0:8, :] = ST[0, 8 * k : 8 * k + 8, :]
        HI[k, 0:8, :] = ST[1, 8 * k : 8 * k + 8, :]

    def states(n, carry):
        out = []
        for k in blocks:
            hr, hi = carry[k]
            c, s = turn8[k]
            lam = LAM[k, rows_of(n), :]
            nr = lam * (c * hr - s * hi) + BR[k, rows_of(n), :]
            ni = lam * (c * hi + s * hr) + BI[k, rows_of(n), :]
            HR[k, rows_of(n + 1), :] = nr
            HI[k, rows_of(n + 1), :] = ni
            out.append((nr, ni))
        return tuple(out)

    def held(k):
        return ST[0, 8 * k : 8 * k + 8, :], ST[1, 8 * k : 8 * k + 8, :]

    lax.fori_loop(0, steps, states, tuple(held(k) for k in blocks), unroll=4)
    M3.c()
    M1.f()
    M2.f()
    XM.c()

    half = GROUP // 2
    same = one_hot(cells((LANES, LANES), 0) // half == cells((LANES, LANES), 1) // half)

    def group_mean(v):
        top = v.astype(BF)
        rest = (v - top.astype(F32)).astype(BF)
        return (nn(top, same) + nn(rest, same)) * (1.0 / GROUP)

    NR, NI = r["N2"].at[pl.ds(0, nt_)], r["N2"].at[pl.ds(nt_, nt_)]
    RS, MIX = r["RS"], r["MIX"]

    def normalise(k, c):
        hr, hi = HR[k, pl.ds(8, T), :], HI[k, pl.ds(8, T), :]
        mean = group_mean(hr + hi)
        hr, hi = hr - mean, hi - mean
        rstd = lax.rsqrt(group_mean(hr * hr + hi * hi) + 1e-05)
        RS[k] = rstd
        hr, hi = hr * rstd, hi * rstd
        NR[k] = hr
        NI[k] = hi
        gr, gi = ACT[k, :, 384:512], ACT[k, :, 512:640]
        MIX[k, :, 0:128] = (hr * PAR[k, 2:3, :] * (gr * jax.nn.sigmoid(gr))).astype(BF)
        MIX[k, :, 128:256] = (hi * PAR[k, 3:4, :] * (gi * jax.nn.sigmoid(gi))).astype(BF)
        return c

    lax.fori_loop(0, nt_, normalise, 0)
    XM.wait()
    lax.fori_loop(1, nt_, lambda k, c: (spread_mix(k), c)[1], 0)

    RES, MID = r["RES"], r["MID"]
    RES[...] = X[...]

    def mix_in(k, c):
        RES[...] += nn(MIX[slot(k)], WXP[slot(k)])
        return c

    lax.fori_loop(0, nt_, mix_in, 0)
    norm_rows(RES, gain2, MID)
    M1.c()
    M2.c()

    HID, DG = r["HID"], r["DG"]

    def gate_w(k, h):
        return WM[h, :, pl.ds(k, 1), 0:96, :].reshape(768, 384)

    def down_w(k, h):
        return WM[h, :, pl.ds(k, 1), 96:144, :].reshape(384, 384)

    def swiglu(k):
        def tile(i, c):
            at = pl.ds(pl.multiple_of(i * 256, 256), 256)
            ga = nn(MID[at, :], gate_w(k, 0))
            ua = nn(MID[at, :], gate_w(k, 1))
            gh = nt(GY[at, 0:384], down_w(k, 0)) + nt(GY[at, 384:768], down_w(k, 1))
            s = jax.nn.sigmoid(ga)
            sl = ga * s
            HID[k, at, :] = (sl * ua).astype(BF)
            DG[k, at, 0:384] = (gh * ua * (s * (1.0 + ga * (1.0 - s)))).astype(BF)
            DG[k, at, 384:768] = (gh * sl).astype(BF)
            return c

        lax.fori_loop(0, T // 256, tile, 0)

    swiglu(0)
    SM = r["SM"]
    for h in range(2):
        SM[h, :, 0:96, :] = (
            tn(MID[...], DG[0, :, 384 * h : 384 * h + 384]).astype(BF).reshape(8, 96, 384)
        )
        SM[h, :, 96:144, :] = (
            tn(HID[0], GY[:, 384 * h : 384 * h + 384]).astype(BF).reshape(8, 48, 384)
        )

    class Summed:
        def __init__(self, name):
            self.bufs = [r[name + k] for k in ("", "0", "1", "2")]
            self.further, self.whole = r[name + "E"], r[name + "F"]
            self.todo = []

        def stage(self, n):
            for copy in self.todo:
                copy.wait_recv()
            links.retire(self.todo)
            self.todo = []
            S = self.bufs[0]
            for h in range(2):
                f, s = order[h]
                spans = ((0, 0, 4), (f, bits[0] * 4, 2), (s, bits[0] * 4 + bits[f] * 2, 1))
                if 1 <= n <= 3:
                    b, first, count = spans[n - 1]
                    mine = pl.ds(first + bits[b] * count, count)
                    S[h, mine] = (S[h, mine].astype(F32) + self.bufs[n][h].astype(F32)).astype(BF)
                if n == 3:
                    part = pl.ds(place[h], 1)
                    for b in range(3, nd.bit_length() - 1):
                        land = self.further.at[h, pl.ds(b - 3, 1)]
                        one = links.send(S.at[h, part], land, partner(b))
                        one.wait_recv()
                        one.wait_send()
                        links.free.append(links.open.pop()[1])
                        S[h, part] = (
                            S[h, part].astype(F32) + self.further[h, b - 3 : b - 2].astype(F32)
                        ).astype(BF)
                    self.whole[h, part] = S[h, part]
                if n < 3:
                    b, first, count = spans[n]
                    give = first + (1 - bits[b]) * count
                    self.todo.append(
                        links.send(S.at[h, pl.ds(give, count)], self.bufs[n + 1].at[h], partner(b))
                    )
                elif n < 6:
                    b, first, count = (
                        (s, place[h], 1),
                        (f, bits[0] * 4 + bits[f] * 2, 2),
                        (0, bits[0] * 4, 4),
                    )[n - 3]
                    part = self.whole.at[h, pl.ds(first, count)]
                    self.todo.append(links.send(part, part, partner(b)))

    finals = []

    def put_out(src, dst):
        copy = pltpu.make_async_copy(src, dst, r["out"].at[len(finals)])
        copy.start()
        finals.append(copy)

    ACC = r["ACC"]
    NAT, GRES = ACC.at[0], ACC.at[1]

    def back_mid(k):
        ACC[k] = nt(DG[k, :, 0:384], gate_w(k, 0)) + nt(DG[k, :, 384:768], gate_w(k, 1))

    mlp_sum, early_sum, late_sum = Summed("SM"), Summed("SE"), Summed("SL")
    mlp_sum.stage(0)
    back_mid(0)
    M3.wait()
    swiglu(3)
    back_mid(3)
    mlp_sum.stage(1)
    M1.wait()
    swiglu(1)
    back_mid(1)
    M2.wait()
    swiglu(2)
    back_mid(2)

    LOWR = r["MID"]

    def back_second(i, total):
        at = pl.ds(pl.multiple_of(i * 128, 128), 128)
        res, gmid = RES[at, :], ACC[slot(0), at, :]
        for k in blocks[1:]:
            gmid = gmid + ACC[slot(k), at, :]
        q2 = lax.rsqrt(jnp.mean(res * res, -1, keepdims=True) + 1e-06)
        p = gmid * gain2
        back = q2 * p - res * (q2 * q2 * q2) * jnp.mean(p * res, -1, keepdims=True)
        gres = GY[at, :].astype(F32) + back
        GRES[at, :] = gres
        LOWR[at, :] = gres.astype(BF)
        return total + jnp.sum((gmid * res * q2).reshape(16, 8, 768), 0)

    VEC = r["EX3"]
    gnorm2 = down_sum(lax.fori_loop(0, T // 128, back_second, jnp.zeros((8, 768), F32)))
    for i in range(6):
        VEC[me, 6 + i : 7 + i, :] = gnorm2[:, 128 * i : 128 * i + 128]

    G = DG
    rows, cols = cells((256, 256), 0), cells((256, 256), 1)
    lane = rows % 128
    together = one_hot((cols == 2 * lane + rows // 128) & (lane < ch))

    def back_norm(k, own):
        gact = nt(LOWR[...], WXP[k])
        rstd = RS[k]
        parts, sums, dots = [], 0.0, 0.0
        group = []
        for i, hn in enumerate((NR[k], NI[k])):
            pre = ACT[k, :, 384 + 128 * i : 512 + 128 * i]
            gain = PAR[k, 2 + i : 3 + i, :]
            ga = gact[:, 128 * i : 128 * i + 128]
            s = jax.nn.sigmoid(pre)
            sl = pre * s
            gh = ga * hn
            G[k, :, 384 + 128 * i : 512 + 128 * i] = (
                gh * gain * (s * (1.0 + pre * (1.0 - s)))
            ).astype(BF)
            if own:
                group.append(down_sum(gh * sl))
            p = ga * gain * sl
            parts.append((p, hn))
            sums = sums + p
            dots = dots + p * hn
        sums, dots = group_mean(sums), group_mean(dots)
        for buf, (p, hn) in zip((BR, BI), parts):
            buf[k] = rstd * (p - sums - hn * dots)
        if own:
            both = jnp.broadcast_to(jnp.concatenate(group, axis=1), (8, 256))
            both = exact(both, together.astype(F32), ((1,), (0,)))
            VEC[me, 14:15, :] = both[0:1, 0:128]
            VEC[me, 15:16, :] = both[0:1, 128:256]

    def back_step(n, carry, some, keep):
        n = steps - 1 - n
        out = []
        for k, (ur, ui) in zip(some, carry):
            c, s = turn8[k]
            lam = LAM[k, rows_of(n), :]
            er = BR[k, rows_of(n), :] + ur
            ei = BI[k, rows_of(n), :] + ui
            if keep:
                BR[k, rows_of(n), :] = er
                BI[k, rows_of(n), :] = ei
            out.append((lam * (c * er + s * ei), lam * (c * ei - s * er)))
        return tuple(out)

    def back_ends(some, buf, which):
        body = functools.partial(back_step, some=some, keep=False)
        first = lax.fori_loop(0, steps, body, tuple((zero8, zero8) for k in some), unroll=4)
        for k, (ur, ui) in zip(some, first):
            CH[1, 8 * k : 8 * k + 8, :] = ur
            CH[2, 8 * k : 8 * k + 8, :] = ui
        post(buf, which, *chain(zero4, zero4, -1.0, False))

    def back_states(some, buf, which):
        sr, si = carried(buf, which, -1.0)
        chain(sr, si, -1.0, True)
        body = functools.partial(back_step, some=some, keep=True)
        lax.fori_loop(0, steps, body, tuple(held(k) for k in some), unroll=4)

    def back_gates(k, own):
        c, s = turn[k]
        er, ei = BR[k], BI[k]
        hr, hi = HR[k, pl.ds(0, T), :], HI[k, pl.ds(0, T), :]
        gap = PAR[k, 0:1, :]
        gar, gai = er * hr + ei * hi, ei * hr - er * hi
        ur, ui, fg = ACT[k, :, 0:128], ACT[k, :, 128:256], ACT[k, :, 256:384]
        su, si, sf = jax.nn.sigmoid(ur), jax.nn.sigmoid(ui), jax.nn.sigmoid(-fg)
        leak = gap * sf
        gleak = er * (ur * su) + ei * (ui * si) - (c * gar + s * gai)
        G[k, :, 0:128] = (er * leak * (su * (1.0 + ur * (1.0 - su)))).astype(BF)
        G[k, :, 128:256] = (ei * leak * (si * (1.0 + ui * (1.0 - si)))).astype(BF)
        G[k, :, 256:384] = (-gleak * leak * (1.0 - sf)).astype(BF)
        if own:
            VEC[me, 12:13, :] = down_sum(gleak * sf)
            VEC[me, 13:14, :] = down_sum((1.0 - leak) * (c * gai - s * gar))

    back_norm(0, True)
    back_ends([0], r["EX1"], 1)

    SE, SL = r["SE"], r["SL"]
    gate_cols = nn(G[0, :, 384:640], together)[:, 0 : 2 * ch].astype(BF)
    mix_cols = nn(MIX[0], together)[:, 0 : 2 * ch].astype(BF)
    for h in range(2):
        at = slice(384 * h, 384 * h + 384)
        SE[h, 0:4] = tn(gate_cols, LOW[:, at]).astype(BF).reshape(4, 48, 384)
        SE[h, 4:8] = tn(mix_cols, LOWR[:, at]).astype(BF).reshape(4, 48, 384)
    early_sum.stage(0)
    mlp_sum.stage(2)
    lax.fori_loop(1, nt_, lambda k, c: (back_norm(k, False), c)[1], 0)
    early_sum.stage(1)
    back_ends(blocks[1:], r["EX2"], 2)
    mlp_sum.stage(3)
    back_states([0], r["EX1"], 1)
    back_gates(0, True)
    rows, cols = cells((384, 384), 0), cells((384, 384), 1)
    lane, g = rows % 128, rows // 128
    to = jnp.where(g < 2, 2 * lane + g, 2 * ch + lane)
    late_cols = nn(G[0, :, 0:384], one_hot((cols == to) & (lane < ch))).astype(BF)
    for h in range(2):
        SL[h] = tn(late_cols, LOW[:, 384 * h : 384 * h + 384]).astype(BF).reshape(8, 48, 384)
    late_sum.stage(0)
    early_sum.stage(2)
    mlp_sum.stage(4)

    back_states(blocks[1:], r["EX2"], 2)
    late_sum.stage(1)
    for k in blocks[1:]:
        back_gates(k, False)
    early_sum.stage(3)
    late_sum.stage(2)
    mlp_sum.stage(5)

    def back_in(k, c):
        NAT[...] += nn(G[slot(k), :, 0:640], WRP[slot(k)])
        return c

    NAT[...] = nn(G[slot(0), :, 0:640], WRP[slot(0)])
    lax.fori_loop(1, nt_ // 2, back_in, 0)
    late_sum.stage(3)
    lax.fori_loop(nt_ // 2, nt_, back_in, 0)
    early_sum.stage(4)

    def back_first(i, total):
        at = pl.ds(pl.multiple_of(i * 128, 128), 128)
        x, gin = X[at, :], NAT[at, :]
        q1 = lax.rsqrt(jnp.mean(x * x, -1, keepdims=True) + 1e-06)
        p = gin * gain1
        GRES[at, :] += q1 * p - x * (q1 * q1 * q1) * jnp.mean(p * x, -1, keepdims=True)
        return total + jnp.sum((gin * x * q1).reshape(16, 8, 768), 0)

    gnorm1 = down_sum(lax.fori_loop(0, T // 128, back_first, jnp.zeros((8, 768), F32)))
    for i in range(6):
        VEC[me, i : i + 1, :] = gnorm1[:, 128 * i : 128 * i + 128]
    exchange(3, VEC, "go")
    late_sum.stage(4)

    def put_from(buf):
        def put(k, c):
            for i in range(6):
                PERM[i, pl.ds(k, 8, stride=steps), :] = buf[pl.ds(pl.multiple_of(8 * k, 8), 8), tiles[i]]
            return c

        lax.fori_loop(0, steps, put, 0, unroll=4)

    put_from(GRES)
    for i in range(6):
        NAT[:, tiles[i]] = PERM[i]
    put_out(NAT, r["tok"])
    mlp_sum.stage(6)
    put_out(r["SMF"], r["o_mlp"])

    def down(k, c):
        j = slot(k)
        for h in range(2):
            RES[:, 384 * h : 384 * h + 384] += nn(HID[j], down_w(j, h))
        return c

    lax.fori_loop(0, nt_, down, 0)
    late_sum.stage(5)
    early_sum.stage(5)
    put_from(RES)
    for i in range(6):
        COT[:, tiles[i]] = PERM[i].astype(BF)
    put_out(COT, r["mixed"])
    late_sum.stage(6)
    put_out(r["SLF"], r["o_late"])
    early_sum.stage(6)
    put_out(r["SEF"], r["o_early"])

    exchange(3, VEC, "arrive")
    total = VEC[0]
    for k in range(1, nd):
        total = total + VEC[k]
    r["vec"][...] = total
    for which in range(4):
        exchange(which, r["EX%d" % which], "leave")
    links.drain()
    for copy in finals:
        copy.wait()


def writer(names, *refs):
    r = dict(zip(names, refs))
    sem = r["sem"]
    count = [0]

    def copy(src, dst):
        c = pltpu.make_async_copy(src, dst, sem.at[count[0]])
        count[0] += 1
        c.start()
        return c

    ins = {}
    for name, src, dst in (
        ("tok", "tok_in", "TK"),
        ("mlp", "mlp", "M"),
        ("mixed", "mixed_in", "MX"),
        ("early", "early", "E"),
        ("late", "late", "L"),
    ):
        ins[name] = copy(r[src], r[dst])
    outs = []
    ins["tok"].wait()
    outs.append(copy(r["TK"], r["tok"]))
    ins["mlp"].wait()
    for h, name in ((0, "g_g"), (1, "g_u")):
        r["GF"][h] = r["M"][h, :, 0:96, :].astype(F32)
        outs.append(copy(r["GF"].at[h], r[name]))
    ins["mixed"].wait()
    outs.append(copy(r["MX"], r["mixed"]))
    for h in range(2):
        r["DF"][:, :, 384 * h : 384 * h + 384] = r["M"][h, :, 96:144, :].astype(F32)
    outs.append(copy(r["DF"], r["g_d"]))
    for name, a, f, n, dests in (
        ("early", "E", "EF", 8, (("g_o", 0, 4), ("g_x", 4, 8))),
        ("late", "L", "LF", 6, (("g_in", 0, 4), ("g_f", 4, 6))),
    ):
        ins[name].wait()
        for h in range(2):
            r[f][:, :, 384 * h : 384 * h + 384] = r[a][h, 0:n].astype(F32)
        for dst, p, q in dests:
            outs.append(copy(r[f].at[p:q], r[dst]))
    ch = r["gap"].shape[1]
    vec = r["vec"]
    r["gn1"][...] = vec[0:6, :]
    r["gn2"][...] = vec[6:12, :]
    r["gap"][...] = vec[12:13, 0:ch]
    r["phase"][...] = vec[13:14, 0:ch]
    r["group"][...] = jnp.concatenate([vec[14:15, :], vec[15:16, 0 : 2 * ch - LANES]], axis=1)
    for c in outs:
        c.wait()


def local(nd, nt_, *args):
    (tokens, cot, g1, w_in, w_f, w_o, gap, phase, gg, w_mix, g2, wg, wu, wd) = args
    T, D = tokens.shape
    ch = w_f.shape[1]
    vmem = pl.BlockSpec(memory_space=pltpu.VMEM)
    hbm = pl.BlockSpec(memory_space=pl.ANY)
    given = dict(
        tokens=tokens,
        cot=cot,
        g1=g1.reshape(6, LANES),
        w_i=w_in.T,
        w_f=w_f.T,
        w_o=w_o.T,
        gap=gap.reshape(1, ch),
        phase=phase.reshape(1, ch),
        gg=gg.reshape(1, 2 * ch),
        w_mix=w_mix,
        g2=g2.reshape(6, LANES),
        wg=wg.reshape(8, 96, 384),
        wu=wu.reshape(8, 96, 384),
        wd=wd.reshape(8, 48, D),
    )
    small = ("g1", "g2", "gap", "phase", "gg", "vec")
    shape = jax.ShapeDtypeStruct
    raw = dict(
        mixed=shape((T, D), BF),
        tok=shape((T, D), F32),
        o_mlp=shape((2, 8, 144, 384), BF),
        o_early=shape((2, 8, 48, 384), BF),
        o_late=shape((2, 8, 48, 384), BF),
        vec=shape((16, LANES), F32),
    )
    scratch = scratch_list(nd, nt_, T)
    mixed, tok, o_mlp, o_early, o_late, vec = pl.pallas_call(
        functools.partial(kernel, nd, nt_, T, list(given) + list(raw) + list(scratch)),
        out_shape=list(raw.values()),
        in_specs=[vmem if k in small else hbm for k in given],
        out_specs=[vmem if k in small else hbm for k in raw],
        scratch_shapes=list(scratch.values()),
        compiler_params=pltpu.CompilerParams(
            collective_id=0, has_side_effects=True, vmem_limit_bytes=63 * 2**20
        ),
        name="layer",
    )(*given.values())

    got = dict(mixed_in=mixed, tok_in=tok, mlp=o_mlp, early=o_early, late=o_late, vec=vec)
    final = dict(
        mixed=shape((T, D), BF),
        tok=shape((T, D), F32),
        gn1=shape((6, LANES), F32),
        g_in=shape((4, 48, D), F32),
        g_f=shape((2, 48, D), F32),
        g_o=shape((4, 48, D), F32),
        gap=shape((1, ch), F32),
        phase=shape((1, ch), F32),
        group=shape((1, 2 * ch), F32),
        g_x=shape((4, 48, D), F32),
        gn2=shape((6, LANES), F32),
        g_g=shape((8, 96, 384), F32),
        g_u=shape((8, 96, 384), F32),
        g_d=shape((8, 48, D), F32),
    )
    held = dict(
        L=pltpu.VMEM((2, 8, 48, 384), BF),
        E=pltpu.VMEM((2, 8, 48, 384), BF),
        M=pltpu.VMEM((2, 8, 144, 384), BF),
        MX=pltpu.VMEM((T, D), BF),
        TK=pltpu.VMEM((T, D), F32),
        LF=pltpu.VMEM((6, 48, D), F32),
        EF=pltpu.VMEM((8, 48, D), F32),
        GF=pltpu.VMEM((2, 8, 96, 384), F32),
        DF=pltpu.VMEM((8, 48, D), F32),
        sem=pltpu.SemaphoreType.DMA((15,)),
    )
    blocky = ("gn1", "gn2", "gap", "phase", "group")
    outs = pl.pallas_call(
        functools.partial(writer, list(got) + list(final) + list(held)),
        out_shape=list(final.values()),
        in_specs=[vmem if k == "vec" else hbm for k in got],
        out_specs=[vmem if k in blocky else hbm for k in final],
        scratch_shapes=list(held.values()),
        compiler_params=pltpu.CompilerParams(vmem_limit_bytes=62 * 2**20),
        name="writer",
    )(*got.values())
    o = dict(zip(final, outs))
    return (
        o["mixed"],
        o["tok"],
        o["gn1"].reshape(D),
        o["g_in"].reshape(2 * ch, D).T,
        o["g_f"].reshape(ch, D).T,
        o["g_o"].reshape(2 * ch, D).T,
        o["gap"].reshape(ch),
        o["phase"].reshape(ch),
        o["group"].reshape(2 * ch),
        o["g_x"].reshape(2 * ch, D),
        o["gn2"].reshape(D),
        o["g_g"].reshape(D, 384),
        o["g_u"].reshape(D, 384),
        o["g_d"].reshape(384, D),
    )


def solution(mesh):
    in_specs = (
        P("dp", None),
        P("dp", None),
        P(),
        P(None, "tp"),
        P(None, "tp"),
        P(None, "tp"),
        P("tp"),
        P("tp"),
        P("tp"),
        P("tp", None),
        P(),
        P(None, "tp"),
        P(None, "tp"),
        P("tp", None),
    )
    out_specs = (
        P("dp", None),
        P("dp", None),
        P(),
        P(None, "tp"),
        P(None, "tp"),
        P(None, "tp"),
        P("tp"),
        P("tp"),
        P("tp"),
        P("tp", None),
        P(),
        P(None, "tp"),
        P(None, "tp"),
        P("tp", None),
    )
    body = functools.partial(local, mesh.shape["dp"], mesh.shape["tp"])
    return jax.shard_map(body, mesh=mesh, in_specs=in_specs, out_specs=out_specs, check_vma=False)
```

```python
import functools

import jax
import jax.numpy as jnp
from jax import lax
from jax.experimental import pallas as pl
from jax.experimental.pallas import tpu as pltpu
from jax.sharding import PartitionSpec as P

MESH = pl.DeviceIdType.MESH
BF = jnp.bfloat16
F32 = jnp.float32
GROUP = 64
LANES = 128
SENDS = 56


def nn(a, b):
    return jnp.dot(a, b, preferred_element_type=F32)


def nt(a, b):
    return lax.dot_general(a, b, (((1,), (1,)), ((), ())), preferred_element_type=F32)


def tn(a, b):
    return lax.dot_general(a, b, (((0,), (0,)), ((), ())), preferred_element_type=F32)


def exact(a, b, dims):
    return lax.dot_general(
        a, b, (dims, ((), ())), precision=lax.Precision.HIGHEST, preferred_element_type=F32
    )


def cells(shape, axis):
    return lax.broadcasted_iota(jnp.int32, shape, axis)


def one_hot(flags):
    return jnp.where(flags, 1.0, 0.0).astype(BF)


def down_sum(v):
    if v.shape[0] > 8:
        v = jnp.sum(v.reshape(v.shape[0] // 8, 8, v.shape[1]), 0)
    v = v[0:4] + v[4:8]
    v = v[0:2] + v[2:4]
    return v[0:1] + v[1:2]


def power(c, s, n):
    out = None
    while n:
        if n % 2:
            out = (c, s) if out is None else (out[0] * c - out[1] * s, out[0] * s + out[1] * c)
        c, s = c * c - s * s, 2.0 * c * s
        n //= 2
    return out


def sum_buffers(name, nd, rows):
    further = max(1, nd.bit_length() - 4)
    counts = (("", 8), ("0", 4), ("1", 2), ("2", 1), ("E", further), ("F", 8))
    return {name + k: pltpu.VMEM((2, n, rows, 384), BF) for k, n in counts}


def scratch_list(nd, nt_, T):
    dma = pltpu.SemaphoreType.DMA
    return dict(
        RI=pltpu.VMEM((192, 768), BF),
        RF=pltpu.VMEM((96, 768), BF),
        RO=pltpu.VMEM((192, 768), BF),
        RM=pltpu.VMEM((192, 768), BF),
        WI=pltpu.VMEM((2, 8, nt_, 64, 384), BF),
        WX=pltpu.VMEM((2, 4, nt_, 48, 384), BF),
        WM=pltpu.VMEM((2, 8, nt_, 144, 384), BF),
        PAR=pltpu.VMEM((nt_, 8, LANES), F32),
        WRP=pltpu.VMEM((nt_, 640, 768), BF),
        WXP=pltpu.VMEM((nt_, 256, 768), BF),
        X=pltpu.VMEM((T, 768), F32),
        GY=pltpu.VMEM((T, 768), BF),
        LOW=pltpu.VMEM((T, 768), BF),
        ACT=pltpu.VMEM((nt_, T, 640), F32),
        LAM=pltpu.VMEM((nt_, T, LANES), F32),
        BR=pltpu.VMEM((nt_, T, LANES), F32),
        BI=pltpu.VMEM((nt_, T, LANES), F32),
        HR=pltpu.VMEM((nt_, T + 8, LANES), F32),
        HI=pltpu.VMEM((nt_, T + 8, LANES), F32),
        N2=pltpu.VMEM((max(6, 2 * nt_), T, LANES), F32),
        RS=pltpu.VMEM((nt_, T, LANES), F32),
        MIX=pltpu.VMEM((nt_, T, 256), BF),
        RES=pltpu.VMEM((T, 768), F32),
        MID=pltpu.VMEM((T, 768), BF),
        HID=pltpu.VMEM((nt_, T, 384), BF),
        DG=pltpu.VMEM((nt_, T, 768), BF),
        ACC=pltpu.VMEM((nt_, T, 768), F32),
        CH=pltpu.VMEM((3, nt_ * 8, LANES), F32),
        ST=pltpu.VMEM((2, nt_ * 8, LANES), F32),
        EX0=pltpu.VMEM((nd, 16, LANES), F32),
        EX1=pltpu.VMEM((nd, 16, LANES), F32),
        EX2=pltpu.VMEM((nd, 16, LANES), F32),
        EX3=pltpu.VMEM((nd, 16, LANES), F32),
        **sum_buffers("SM", nd, 144),
        **sum_buffers("SE", nd, 48),
        **sum_buffers("SL", nd, 48),
        loc=dma((16,)),
        out=dma((8,)),
        ss=dma((SENDS,)),
        rs=dma((92 + 6 * max(0, nd.bit_length() - 4),)),
        fs=dma((8,)),
        es=dma((4, nd)),
        er=dma((4, nd)),
    )


class Links:
    def __init__(self, ss, rs, fs):
        self.ss, self.rs, self.fs = ss, rs, fs
        self.free, self.received, self.asked = list(range(SENDS)), 0, 0
        self.open, self.old, self.some = [], [], []

    def send(self, src, dst, dev):
        k, n = self.received, self.free.pop(0)
        self.received += 1
        copy = pltpu.make_async_remote_copy(
            src, dst, self.ss.at[n], self.rs.at[k], device_id=dev, device_id_type=MESH
        )
        copy.start()
        self.open.append((copy, n))
        return copy

    def retire(self, copies):
        self.old += [pair for c in copies for pair in self.open if pair[0] is c]
        while len(self.old) > 4:
            pair = self.old.pop(0)
            pair[0].wait_send()
            self.free.append(pair[1])
            self.open = [p for p in self.open if p is not pair]

    def send_if(self, flag, k, src, dst, dev):
        n = self.asked
        self.asked += 1
        copy = pltpu.make_async_remote_copy(
            src, dst, self.fs.at[n], self.rs.at[k], device_id=dev, device_id_type=MESH
        )

        @pl.when(flag)
        def _():
            copy.start()

        self.some.append((flag, copy))
        return copy

    def drain(self):
        for copy, _ in self.open:
            copy.wait_send()
        for flag, copy in self.some:
            pl.when(flag)(copy.wait_send)


def kernel(nd, nt_, T, names, *refs):
    r = dict(zip(names, refs))
    me, z = lax.axis_index("dp"), lax.axis_index("tp")
    steps = T // 8
    ch = r["w_f"].shape[0]
    blocks = list(range(nt_))

    def flip(bit):
        return me + bit - 2 * bit * ((me // bit) % 2)

    bits = (me % 2, (me // 2) % 2, (me // 4) % 2)
    order = ((1, 2), (2, 1))
    place = [bits[0] * 4 + bits[f] * 2 + bits[s] for f, s in order]
    wide = [bits[0] * 2 + bits[f] for f, s in order]
    links = Links(r["ss"], r["rs"], r["fs"])
    away = [0, 1, 3, 2] if nt_ == 4 else blocks

    def slot(k):
        o = lax.rem(k + nt_ - z, nt_)
        if nt_ != 4:
            return o
        return jnp.where(o == 2, 3, jnp.where(o == 3, 2, o))

    barrier = pltpu.get_barrier_semaphore()

    def greet_dp(o, c):
        pl.semaphore_signal(barrier, 1, device_id=(lax.rem(me + o, nd), z), device_id_type=MESH)
        return c

    def greet_tp(o, c):
        pl.semaphore_signal(barrier, 1, device_id=(me, lax.rem(z + o, nt_)), device_id_type=MESH)
        return c

    lax.fori_loop(1, nt_, greet_tp, 0)
    lax.fori_loop(1, nd, greet_dp, 0)

    WM = r["WM"]
    COT = r["DG"].at[nt_ - 1]
    loads = {}
    for k, (name, src, dst) in enumerate(
        (
            ("w_i", r["w_i"], r["RI"]),
            ("w_f", r["w_f"], r["RF"]),
            ("w_o", r["w_o"], r["RO"]),
            ("tokens", r["tokens"], r["MID"]),
            ("w_x", r["w_mix"], r["RM"]),
            ("g", r["wg"], WM.at[0, :, 0, 0:96, :]),
            ("u", r["wu"], WM.at[1, :, 0, 0:96, :]),
            ("d0", r["wd"].at[:, :, 0:384], WM.at[0, :, 0, 96:144, :]),
            ("d1", r["wd"].at[:, :, 384:768], WM.at[1, :, 0, 96:144, :]),
            ("cot", r["cot"], COT),
        )
    ):
        loads[name] = pltpu.make_async_copy(src, dst, r["loc"].at[k])
        loads[name].start()

    WI, WX, WRP, WXP, PAR = r["WI"], r["WX"], r["WRP"], r["WXP"], r["PAR"]
    rows, cols = cells((2 * ch, 2 * ch), 0), cells((2 * ch, 2 * ch), 1)
    apart = one_hot(cols == jnp.where(rows < ch, 2 * rows, 2 * (rows - ch) + 1))
    for k in ("w_i", "w_f", "w_o"):
        loads[k].wait()
    turned = jnp.concatenate(
        [
            nn(apart, r["RI"][...]).astype(BF),
            r["RF"][...],
            nn(apart, r["RO"][...]).astype(BF),
            jnp.zeros((32, 768), BF),
        ],
        axis=0,
    )
    for h in range(2):
        for p in range(8):
            WI[h, p, 0] = turned[64 * p : 64 * p + 64, 384 * h : 384 * h + 384]
    PAR[0] = jnp.zeros((8, LANES), F32)
    PAR[0, 0:1, 0:ch] = r["gap"][...]
    PAR[0, 1:2, 0:ch] = r["phase"][...]
    gains = exact(
        jnp.broadcast_to(r["gg"][...], (8, 2 * ch)), apart.astype(F32), ((1,), (1,))
    )
    PAR[0, 2:3, 0:ch] = gains[0:1, 0:ch]
    PAR[0, 3:4, 0:ch] = gains[0:1, ch : 2 * ch]

    def across(o):
        return (me, lax.rem(z + nt_ - o, nt_))

    def partner(b):
        return (flip(1 << b), z)

    class Unit:
        def __init__(self, buf, slots, portions, far=None):
            self.buf, self.slots, self.portions, self.far = buf, slots, portions, far
            self.at = place if portions == 8 else wide
            self.todo = []

        def wait(self):
            for copy in self.todo:
                copy.wait_recv()
            links.retire(self.todo)
            self.todo = []

        def hop(self, h, b, start, count):
            part = self.buf.at[h, pl.ds(start, count), pl.ds(self.slots[0], len(self.slots))]
            self.todo.append(links.send(part, part, partner(b)))

        def held(self, h, s):
            if self.far is None:
                return self.buf.at[h, self.at[h], s]
            return self.buf.at[h, pl.ds(bits[0] * 4 + bits[order[h][0]] * 2, 2), s]

        def z(self):
            for s in self.slots:
                for h in range(2):
                    own, to = self.held(h, 0), self.held(h, s)
                    if self.far is None or nt_ != 4:
                        self.todo.append(links.send(own, to, across(away[s])))
                    else:
                        k = links.received
                        links.received += 1
                        flag = z != (0 if s == 1 else 3)
                        self.todo.append(links.send_if(flag, k, own, to, across(away[s])))
                        self.first = k - h

        def forward(self):
            if nt_ != 4:
                return
            s = self.slots[0]
            who, end = (2, 3) if s == 1 else (1, 0)
            for h in range(2):
                held, to = self.held(h, self.far), self.held(h, s)
                links.send_if(z == who, self.first + h, held, to, (me, end))

        def s(self):
            self.wait()
            for h in range(2):
                f, s = order[h]
                if self.portions == 8:
                    self.hop(h, s, place[h], 1)
                else:
                    self.hop(h, f, wide[h], 1)

        def f(self):
            self.wait()
            for h in range(2):
                f, s = order[h]
                self.hop(h, f, bits[0] * 4 + bits[f] * 2, 2)

        def c(self):
            self.wait()
            n = self.portions // 2
            for h in range(2):
                self.hop(h, 0, bits[0] * n, n)

    I1, I2 = Unit(WI, blocks[1:3], 8), Unit(WI, blocks[3:], 8)
    XM = Unit(WX, blocks[1:], 4)
    M1, M2, M3 = Unit(WM, [1], 8, 3), Unit(WM, [2], 8, 3), Unit(WM, [3], 8)

    pl.semaphore_wait(barrier, nd - 1 + nt_ - 1)
    I1.z()
    par_copies = [links.send(PAR.at[0], PAR.at[s], across(away[s])) for s in blocks[1:]]

    PERM, X, GY, LOW = r["N2"], r["X"], r["GY"], r["LOW"]
    loads["tokens"].wait()
    tiles = [slice(LANES * i, LANES * i + LANES) for i in range(6)]
    for i in range(6):
        PERM[i] = r["MID"][:, tiles[i]].astype(F32)

    def take(k, c):
        for i in range(6):
            X[pl.ds(pl.multiple_of(8 * k, 8), 8), tiles[i]] = PERM[i, pl.ds(k, 8, stride=steps), :]
        return c

    lax.fori_loop(0, steps, take, 0, unroll=4)

    def whole_row(ref):
        return jnp.concatenate([ref[i : i + 1, :] for i in range(6)], axis=1)

    gain1, gain2 = whole_row(r["g1"]), whole_row(r["g2"])

    def norm_rows(src, gain, dst):
        def body(i, c):
            at = pl.ds(pl.multiple_of(i * 128, 128), 128)
            v = src[at, :]
            q = lax.rsqrt(jnp.mean(v * v, -1, keepdims=True) + 1e-06)
            dst[at, :] = (v * q * gain).astype(BF)
            return c

        lax.fori_loop(0, T // 128, body, 0)

    norm_rows(X, gain1, LOW)
    I2.z()
    for k in ("g", "u", "d0", "d1", "cot"):
        loads[k].wait()
    M3.z()

    for k in blocks:
        for g in range(5):
            WRP[k, g * 128 + 96 : g * 128 + 128, :] = jnp.zeros((32, 768), BF)
        for g in range(2):
            WXP[k, g * 128 + 96 : g * 128 + 128, :] = jnp.zeros((32, 768), BF)

    def spread_in(k):
        for g in range(5):
            for q in range(3):
                row = g * 96 + q * 32
                for h in range(2):
                    WRP[k, g * 128 + q * 32 : g * 128 + q * 32 + 32, 384 * h : 384 * h + 384] = WI[
                        h, row // 64, k, row % 64 : row % 64 + 32, :
                    ]

    def spread_mix(k):
        for p in range(4):
            row = (p // 2) * 128 + (p % 2) * 48
            for h in range(2):
                WXP[k, row : row + 48, 384 * h : 384 * h + 384] = WX[h, p, k]

    ACT, LAM, BR, BI = r["ACT"], r["LAM"], r["BR"], r["BI"]

    def project(k):
        spread_in(k)
        gap = PAR[k, 0:1, :]
        ACT[k] = nt(LOW[...], WRP[k])
        ur, ui, fg = ACT[k, :, 0:128], ACT[k, :, 128:256], ACT[k, :, 256:384]
        leak = gap * jax.nn.sigmoid(-fg)
        LAM[k] = 1.0 - leak
        BR[k] = leak * (ur * jax.nn.sigmoid(ur))
        BI[k] = leak * (ui * jax.nn.sigmoid(ui))

    loads["w_x"].wait()
    mixed_rows = nn(apart, r["RM"][...]).astype(BF)
    for h in range(2):
        for p in range(4):
            WX[h, p, 0] = mixed_rows[48 * p : 48 * p + 48, 384 * h : 384 * h + 384]
    spread_mix(0)
    I1.s()
    project(0)
    I1.f()
    M1.z()
    M2.z()
    I2.s()

    for i in range(6):
        PERM[i] = COT[:, tiles[i]].astype(F32)

    def take_cot(k, c):
        for i in range(6):
            two = [PERM[i, pl.ds(2 * k + j, 8, stride=steps), :] for j in range(2)]
            GY[pl.ds(pl.multiple_of(16 * k, 16), 16), tiles[i]] = jnp.concatenate(two, axis=0).astype(BF)
        return c

    lax.fori_loop(0, steps // 2, take_cot, 0, unroll=2)
    I1.c()
    I2.f()
    XM.z()
    for copy in par_copies:
        copy.wait_recv()
    I1.wait()
    lax.fori_loop(1, 3, lambda k, c: (project(k), c)[1], 0)
    M3.s()
    I2.c()
    I2.wait()
    project(3)
    M3.f()
    M1.forward()
    M2.forward()

    CH, ST, HR, HI = r["CH"], r["ST"], r["HR"], r["HI"]
    turn = []
    for k in blocks:
        ph = PAR[k, 1:2, :]
        turn.append((jnp.cos(ph), jnp.sin(ph)))
    turn8 = [(jnp.broadcast_to(c, (8, LANES)), jnp.broadcast_to(s, (8, LANES))) for c, s in turn]
    cos4 = jnp.concatenate([c for c, s in turn], axis=0)
    sin4 = jnp.concatenate([s for c, s in turn], axis=0)
    chunk_c, chunk_s = power(cos4, sin4, steps)
    whole_c, whole_s = power(cos4, sin4, T)
    zero8 = jnp.zeros((8, LANES), F32)
    zero4 = jnp.zeros((nt_, LANES), F32)

    def rows_of(k):
        return pl.ds(pl.multiple_of(8 * k, 8), 8)

    def ends(n, carry):
        out = []
        for k in blocks:
            hr, hi, lp = carry[k]
            c, s = turn8[k]
            lam = LAM[k, rows_of(n), :]
            nr = lam * (c * hr - s * hi) + BR[k, rows_of(n), :]
            ni = lam * (c * hi + s * hr) + BI[k, rows_of(n), :]
            out.append((nr, ni, lp * lam))
        return tuple(out)

    last = lax.fori_loop(0, steps, ends, tuple((zero8, zero8, zero8 + 1.0) for k in blocks), unroll=4)
    for k in blocks:
        CH[0, 8 * k : 8 * k + 8, :] = last[k][2]
        CH[1, 8 * k : 8 * k + 8, :] = last[k][0]
        CH[2, 8 * k : 8 * k + 8, :] = last[k][1]

    def chunk(i, c):
        return CH[i, pl.ds(c, nt_, stride=8), :]

    def chain(sr, si, sign, keep):
        for c in range(8) if sign > 0 else range(7, -1, -1):
            if keep:
                ST[0, pl.ds(c, nt_, stride=8), :] = sr
                ST[1, pl.ds(c, nt_, stride=8), :] = si
            lp = chunk(0, c)
            pr, pi = lp * chunk_c, sign * (lp * chunk_s)
            sr, si = pr * sr - pi * si + chunk(1, c), pr * si + pi * sr + chunk(2, c)
        return sr, si

    whole_lam = chunk(0, 0)
    for c in range(1, 8):
        whole_lam = whole_lam * chunk(0, c)

    def exchange(which, buf, start):
        def copy_of(o, back):
            at = lax.rem(me + nd - o, nd) if back else lax.rem(me + o, nd)
            row = at if back else me
            return pltpu.make_async_remote_copy(
                buf.at[row],
                buf.at[row],
                r["es"].at[which, o],
                r["er"].at[which, o],
                device_id=(at, z),
                device_id_type=MESH,
            )

        def go(o, c):
            copy_of(o, False).start()
            return c

        def arrive(o, c):
            copy_of(o, True).wait_recv()
            return c

        def leave(o, c):
            copy_of(o, False).wait_send()
            return c

        lax.fori_loop(1, nd, {"go": go, "arrive": arrive, "leave": leave}[start], 0)

    def post(buf, which, sr, si):
        buf[me, 0:4, :] = whole_lam
        buf[me, 4:8, :] = sr
        buf[me, 8:12, :] = si
        buf[me, 12:16, :] = zero4
        exchange(which, buf, "go")

    def carried(buf, which, sign):
        exchange(which, buf, "arrive")

        def lap(k, s):
            at = k if sign > 0 else nd - 1 - k
            reached = (at < me) if sign > 0 else (at > me)
            lp = buf[at, 0:4, :]
            pr, pi = lp * whole_c, sign * (lp * whole_s)
            nr = pr * s[0] - pi * s[1] + buf[at, 4:8, :]
            ni = pr * s[1] + pi * s[0] + buf[at, 8:12, :]
            return jnp.where(reached, nr, s[0]), jnp.where(reached, ni, s[1])

        return lax.fori_loop(0, nd, lap, (zero4, zero4))

    post(r["EX0"], 0, *chain(zero4, zero4, 1.0, False))
    XM.s()
    start = carried(r["EX0"], 0, 1.0)
    chain(start[0], start[1], 1.0, True)
    for k in blocks:
        HR[k, 0:8, :] = ST[0, 8 * k : 8 * k + 8, :]
        HI[k, 0:8, :] = ST[1, 8 * k : 8 * k + 8, :]

    def states(n, carry):
        out = []
        for k in blocks:
            hr, hi = carry[k]
            c, s = turn8[k]
            lam = LAM[k, rows_of(n), :]
            nr = lam * (c * hr - s * hi) + BR[k, rows_of(n), :]
            ni = lam * (c * hi + s * hr) + BI[k, rows_of(n), :]
            HR[k, rows_of(n + 1), :] = nr
            HI[k, rows_of(n + 1), :] = ni
            out.append((nr, ni))
        return tuple(out)

    def held(k):
        return ST[0, 8 * k : 8 * k + 8, :], ST[1, 8 * k : 8 * k + 8, :]

    lax.fori_loop(0, steps, states, tuple(held(k) for k in blocks), unroll=4)
    M3.c()
    M1.f()
    M2.f()
    XM.c()

    half = GROUP // 2
    same = one_hot(cells((LANES, LANES), 0) // half == cells((LANES, LANES), 1) // half)

    def group_mean(v):
        top = v.astype(BF)
        rest = (v - top.astype(F32)).astype(BF)
        return (nn(top, same) + nn(rest, same)) * (1.0 / GROUP)

    NR, NI = r["N2"].at[pl.ds(0, nt_)], r["N2"].at[pl.ds(nt_, nt_)]
    RS, MIX = r["RS"], r["MIX"]

    def normalise(k, c):
        hr, hi = HR[k, pl.ds(8, T), :], HI[k, pl.ds(8, T), :]
        mean = group_mean(hr + hi)
        hr, hi = hr - mean, hi - mean
        rstd = lax.rsqrt(group_mean(hr * hr + hi * hi) + 1e-05)
        RS[k] = rstd
        hr, hi = hr * rstd, hi * rstd
        NR[k] = hr
        NI[k] = hi
        gr, gi = ACT[k, :, 384:512], ACT[k, :, 512:640]
        MIX[k, :, 0:128] = (hr * PAR[k, 2:3, :] * (gr * jax.nn.sigmoid(gr))).astype(BF)
        MIX[k, :, 128:256] = (hi * PAR[k, 3:4, :] * (gi * jax.nn.sigmoid(gi))).astype(BF)
        return c

    lax.fori_loop(0, nt_, normalise, 0)
    XM.wait()
    lax.fori_loop(1, nt_, lambda k, c: (spread_mix(k), c)[1], 0)

    RES, MID = r["RES"], r["MID"]

    def mix_in(i, c):
        at = pl.ds(pl.multiple_of(i * 256, 256), 256)
        total = nn(MIX[slot(0), at, :], WXP[slot(0)])
        for k in blocks[1:]:
            total = total + nn(MIX[slot(k), at, :], WXP[slot(k)])
        RES[at, :] = X[at, :] + total
        return c

    lax.fori_loop(0, T // 256, mix_in, 0)
    norm_rows(RES, gain2, MID)

    HID, DG = r["HID"], r["DG"]

    def gate_w(k, h):
        return WM[h, :, pl.ds(k, 1), 0:96, :].reshape(768, 384)

    def down_w(k, h):
        return WM[h, :, pl.ds(k, 1), 96:144, :].reshape(384, 384)

    def swiglu(k):
        def tile(i, c):
            at = pl.ds(pl.multiple_of(i * 256, 256), 256)
            ga = nn(MID[at, :], gate_w(k, 0))
            ua = nn(MID[at, :], gate_w(k, 1))
            gh = nt(GY[at, 0:384], down_w(k, 0)) + nt(GY[at, 384:768], down_w(k, 1))
            s = jax.nn.sigmoid(ga)
            sl = ga * s
            HID[k, at, :] = (sl * ua).astype(BF)
            DG[k, at, 0:384] = (gh * ua * (s * (1.0 + ga * (1.0 - s)))).astype(BF)
            DG[k, at, 384:768] = (gh * sl).astype(BF)
            return c

        lax.fori_loop(0, T // 256, tile, 0)

    swiglu(0)
    SM = r["SM"]
    for h in range(2):
        SM[h, :, 0:96, :] = (
            tn(MID[...], DG[0, :, 384 * h : 384 * h + 384]).astype(BF).reshape(8, 96, 384)
        )
        SM[h, :, 96:144, :] = (
            tn(HID[0], GY[:, 384 * h : 384 * h + 384]).astype(BF).reshape(8, 48, 384)
        )

    class Summed:
        def __init__(self, name):
            self.bufs = [r[name + k] for k in ("", "0", "1", "2")]
            self.further, self.whole = r[name + "E"], r[name + "F"]
            self.todo = []

        def stage(self, n):
            for copy in self.todo:
                copy.wait_recv()
            links.retire(self.todo)
            self.todo = []
            S = self.bufs[0]
            for h in range(2):
                f, s = order[h]
                spans = ((0, 0, 4), (f, bits[0] * 4, 2), (s, bits[0] * 4 + bits[f] * 2, 1))
                if 1 <= n <= 3:
                    b, first, count = spans[n - 1]
                    mine = pl.ds(first + bits[b] * count, count)
                    S[h, mine] = (S[h, mine].astype(F32) + self.bufs[n][h].astype(F32)).astype(BF)
                if n == 3:
                    part = pl.ds(place[h], 1)
                    for b in range(3, nd.bit_length() - 1):
                        land = self.further.at[h, pl.ds(b - 3, 1)]
                        one = links.send(S.at[h, part], land, partner(b))
                        one.wait_recv()
                        one.wait_send()
                        links.free.append(links.open.pop()[1])
                        S[h, part] = (
                            S[h, part].astype(F32) + self.further[h, b - 3 : b - 2].astype(F32)
                        ).astype(BF)
                    self.whole[h, part] = S[h, part]
                if n < 3:
                    b, first, count = spans[n]
                    give = first + (1 - bits[b]) * count
                    self.todo.append(
                        links.send(S.at[h, pl.ds(give, count)], self.bufs[n + 1].at[h], partner(b))
                    )
                elif n < 6:
                    b, first, count = (
                        (s, place[h], 1),
                        (f, bits[0] * 4 + bits[f] * 2, 2),
                        (0, bits[0] * 4, 4),
                    )[n - 3]
                    part = self.whole.at[h, pl.ds(first, count)]
                    self.todo.append(links.send(part, part, partner(b)))

    finals = []

    def put_out(src, dst):
        copy = pltpu.make_async_copy(src, dst, r["out"].at[len(finals)])
        copy.start()
        finals.append(copy)

    ACC = r["ACC"]
    NAT, GRES = ACC.at[0], ACC.at[1]

    def back_mid(k):
        ACC[k] = nt(DG[k, :, 0:384], gate_w(k, 0)) + nt(DG[k, :, 384:768], gate_w(k, 1))

    mlp_sum, early_sum, late_sum = Summed("SM"), Summed("SE"), Summed("SL")
    mlp_sum.stage(0)
    back_mid(0)
    M1.c()
    M2.c()
    M3.wait()
    swiglu(3)
    back_mid(3)
    M1.wait()
    mlp_sum.stage(1)
    swiglu(1)
    back_mid(1)
    M2.wait()
    swiglu(2)
    back_mid(2)

    LOWR = r["MID"]

    def back_second(i, total):
        at = pl.ds(pl.multiple_of(i * 128, 128), 128)
        res, gmid = RES[at, :], ACC[slot(0), at, :]
        for k in blocks[1:]:
            gmid = gmid + ACC[slot(k), at, :]
        q2 = lax.rsqrt(jnp.mean(res * res, -1, keepdims=True) + 1e-06)
        p = gmid * gain2
        back = q2 * p - res * (q2 * q2 * q2) * jnp.mean(p * res, -1, keepdims=True)
        gres = GY[at, :].astype(F32) + back
        GRES[at, :] = gres
        LOWR[at, :] = gres.astype(BF)
        return total + jnp.sum((gmid * res * q2).reshape(16, 8, 768), 0)

    VEC = r["EX3"]
    gnorm2 = down_sum(lax.fori_loop(0, T // 128, back_second, jnp.zeros((8, 768), F32)))
    for i in range(6):
        VEC[me, 6 + i : 7 + i, :] = gnorm2[:, 128 * i : 128 * i + 128]

    G = DG
    rows, cols = cells((256, 256), 0), cells((256, 256), 1)
    lane = rows % 128
    together = one_hot((cols == 2 * lane + rows // 128) & (lane < ch))

    def back_norm(k, own):
        gact = nt(LOWR[...], WXP[k])
        rstd = RS[k]
        parts, sums, dots = [], 0.0, 0.0
        group = []
        for i, hn in enumerate((NR[k], NI[k])):
            pre = ACT[k, :, 384 + 128 * i : 512 + 128 * i]
            gain = PAR[k, 2 + i : 3 + i, :]
            ga = gact[:, 128 * i : 128 * i + 128]
            s = jax.nn.sigmoid(pre)
            sl = pre * s
            gh = ga * hn
            G[k, :, 384 + 128 * i : 512 + 128 * i] = (
                gh * gain * (s * (1.0 + pre * (1.0 - s)))
            ).astype(BF)
            if own:
                group.append(down_sum(gh * sl))
            p = ga * gain * sl
            parts.append((p, hn))
            sums = sums + p
            dots = dots + p * hn
        sums, dots = group_mean(sums), group_mean(dots)
        for buf, (p, hn) in zip((BR, BI), parts):
            buf[k] = rstd * (p - sums - hn * dots)
        if own:
            both = jnp.broadcast_to(jnp.concatenate(group, axis=1), (8, 256))
            both = exact(both, together.astype(F32), ((1,), (0,)))
            VEC[me, 14:15, :] = both[0:1, 0:128]
            VEC[me, 15:16, :] = both[0:1, 128:256]

    def back_step(n, carry, some, keep):
        n = steps - 1 - n
        out = []
        for k, (ur, ui) in zip(some, carry):
            c, s = turn8[k]
            lam = LAM[k, rows_of(n), :]
            er = BR[k, rows_of(n), :] + ur
            ei = BI[k, rows_of(n), :] + ui
            if keep:
                BR[k, rows_of(n), :] = er
                BI[k, rows_of(n), :] = ei
            out.append((lam * (c * er + s * ei), lam * (c * ei - s * er)))
        return tuple(out)

    def back_ends(some, buf, which):
        body = functools.partial(back_step, some=some, keep=False)
        first = lax.fori_loop(0, steps, body, tuple((zero8, zero8) for k in some), unroll=4)
        for k, (ur, ui) in zip(some, first):
            CH[1, 8 * k : 8 * k + 8, :] = ur
            CH[2, 8 * k : 8 * k + 8, :] = ui
        post(buf, which, *chain(zero4, zero4, -1.0, False))

    def back_states(some, buf, which):
        sr, si = carried(buf, which, -1.0)
        chain(sr, si, -1.0, True)
        body = functools.partial(back_step, some=some, keep=True)
        lax.fori_loop(0, steps, body, tuple(held(k) for k in some), unroll=4)

    def back_gates(k, own):
        c, s = turn[k]
        er, ei = BR[k], BI[k]
        hr, hi = HR[k, pl.ds(0, T), :], HI[k, pl.ds(0, T), :]
        gap = PAR[k, 0:1, :]
        gar, gai = er * hr + ei * hi, ei * hr - er * hi
        ur, ui, fg = ACT[k, :, 0:128], ACT[k, :, 128:256], ACT[k, :, 256:384]
        su, si, sf = jax.nn.sigmoid(ur), jax.nn.sigmoid(ui), jax.nn.sigmoid(-fg)
        leak = gap * sf
        gleak = er * (ur * su) + ei * (ui * si) - (c * gar + s * gai)
        G[k, :, 0:128] = (er * leak * (su * (1.0 + ur * (1.0 - su)))).astype(BF)
        G[k, :, 128:256] = (ei * leak * (si * (1.0 + ui * (1.0 - si)))).astype(BF)
        G[k, :, 256:384] = (-gleak * leak * (1.0 - sf)).astype(BF)
        if own:
            VEC[me, 12:13, :] = down_sum(gleak * sf)
            VEC[me, 13:14, :] = down_sum((1.0 - leak) * (c * gai - s * gar))

    back_norm(0, True)
    back_ends([0], r["EX1"], 1)

    SE, SL = r["SE"], r["SL"]
    gate_cols = nn(G[0, :, 384:640], together)[:, 0 : 2 * ch].astype(BF)
    mix_cols = nn(MIX[0], together)[:, 0 : 2 * ch].astype(BF)
    for h in range(2):
        at = slice(384 * h, 384 * h + 384)
        SE[h, 0:4] = tn(gate_cols, LOW[:, at]).astype(BF).reshape(4, 48, 384)
        SE[h, 4:8] = tn(mix_cols, LOWR[:, at]).astype(BF).reshape(4, 48, 384)
    early_sum.stage(0)
    mlp_sum.stage(2)
    lax.fori_loop(1, nt_, lambda k, c: (back_norm(k, False), c)[1], 0)
    early_sum.stage(1)
    back_ends(blocks[1:], r["EX2"], 2)
    back_states([0], r["EX1"], 1)
    back_gates(0, True)
    rows, cols = cells((384, 384), 0), cells((384, 384), 1)
    lane, g = rows % 128, rows // 128
    to = jnp.where(g < 2, 2 * lane + g, 2 * ch + lane)
    late_cols = nn(G[0, :, 0:384], one_hot((cols == to) & (lane < ch))).astype(BF)
    for h in range(2):
        SL[h] = tn(late_cols, LOW[:, 384 * h : 384 * h + 384]).astype(BF).reshape(8, 48, 384)
    late_sum.stage(0)
    mlp_sum.stage(3)

    back_states(blocks[1:], r["EX2"], 2)
    late_sum.stage(1)
    early_sum.stage(2)
    mlp_sum.stage(4)
    for k in blocks[1:]:
        back_gates(k, False)
    early_sum.stage(3)
    late_sum.stage(2)

    def back_in(k, c):
        NAT[...] += nn(G[slot(k), :, 0:640], WRP[slot(k)])
        return c

    NAT[...] = nn(G[slot(0), :, 0:640], WRP[slot(0)])
    lax.fori_loop(1, nt_ // 2, back_in, 0)
    late_sum.stage(3)
    lax.fori_loop(nt_ // 2, nt_, back_in, 0)
    mlp_sum.stage(5)
    early_sum.stage(4)

    def back_first(i, total):
        at = pl.ds(pl.multiple_of(i * 128, 128), 128)
        x, gin = X[at, :], NAT[at, :]
        q1 = lax.rsqrt(jnp.mean(x * x, -1, keepdims=True) + 1e-06)
        p = gin * gain1
        GRES[at, :] += q1 * p - x * (q1 * q1 * q1) * jnp.mean(p * x, -1, keepdims=True)
        return total + jnp.sum((gin * x * q1).reshape(16, 8, 768), 0)

    gnorm1 = down_sum(lax.fori_loop(0, T // 128, back_first, jnp.zeros((8, 768), F32)))
    for i in range(6):
        VEC[me, i : i + 1, :] = gnorm1[:, 128 * i : 128 * i + 128]
    exchange(3, VEC, "go")
    late_sum.stage(4)

    def put_from(buf):
        def put(k, c):
            for i in range(6):
                PERM[i, pl.ds(k, 8, stride=steps), :] = buf[pl.ds(pl.multiple_of(8 * k, 8), 8), tiles[i]]
            return c

        lax.fori_loop(0, steps, put, 0, unroll=4)

    put_from(GRES)
    for i in range(6):
        NAT[:, tiles[i]] = PERM[i]
    put_out(NAT, r["tok"])
    mlp_sum.stage(6)
    put_out(r["SMF"], r["o_mlp"])

    def down(k, c):
        j = slot(k)
        for h in range(2):
            RES[:, 384 * h : 384 * h + 384] += nn(HID[j], down_w(j, h))
        return c

    lax.fori_loop(0, nt_, down, 0)
    late_sum.stage(5)
    early_sum.stage(5)
    put_from(RES)
    for i in range(6):
        COT[:, tiles[i]] = PERM[i].astype(BF)
    put_out(COT, r["mixed"])
    late_sum.stage(6)
    put_out(r["SLF"], r["o_late"])
    early_sum.stage(6)
    put_out(r["SEF"], r["o_early"])

    exchange(3, VEC, "arrive")
    total = VEC[0]
    for k in range(1, nd):
        total = total + VEC[k]
    r["vec"][...] = total
    for which in range(4):
        exchange(which, r["EX%d" % which], "leave")
    links.drain()
    for copy in finals:
        copy.wait()


def writer(names, *refs):
    r = dict(zip(names, refs))
    sem = r["sem"]
    count = [0]

    def copy(src, dst):
        c = pltpu.make_async_copy(src, dst, sem.at[count[0]])
        count[0] += 1
        c.start()
        return c

    ins = {}
    for name, src, dst in (
        ("tok", "tok_in", "TK"),
        ("mlp", "mlp", "M"),
        ("mixed", "mixed_in", "MX"),
        ("early", "early", "E"),
        ("late", "late", "L"),
    ):
        ins[name] = copy(r[src], r[dst])
    outs = []
    ins["tok"].wait()
    outs.append(copy(r["TK"], r["tok"]))
    ins["mlp"].wait()
    for h, name in ((0, "g_g"), (1, "g_u")):
        r["GF"][h] = r["M"][h, :, 0:96, :].astype(F32)
        outs.append(copy(r["GF"].at[h], r[name]))
    ins["mixed"].wait()
    outs.append(copy(r["MX"], r["mixed"]))
    for h in range(2):
        r["DF"][:, :, 384 * h : 384 * h + 384] = r["M"][h, :, 96:144, :].astype(F32)
    outs.append(copy(r["DF"], r["g_d"]))
    for name, a, f, n, dests in (
        ("early", "E", "EF", 8, (("g_o", 0, 4), ("g_x", 4, 8))),
        ("late", "L", "LF", 6, (("g_in", 0, 4), ("g_f", 4, 6))),
    ):
        ins[name].wait()
        for h in range(2):
            r[f][:, :, 384 * h : 384 * h + 384] = r[a][h, 0:n].astype(F32)
        for dst, p, q in dests:
            outs.append(copy(r[f].at[p:q], r[dst]))
    ch = r["gap"].shape[1]
    vec = r["vec"]
    r["gn1"][...] = vec[0:6, :]
    r["gn2"][...] = vec[6:12, :]
    r["gap"][...] = vec[12:13, 0:ch]
    r["phase"][...] = vec[13:14, 0:ch]
    r["group"][...] = jnp.concatenate([vec[14:15, :], vec[15:16, 0 : 2 * ch - LANES]], axis=1)
    for c in outs:
        c.wait()


def local(nd, nt_, *args):
    (tokens, cot, g1, w_in, w_f, w_o, gap, phase, gg, w_mix, g2, wg, wu, wd) = args
    T, D = tokens.shape
    ch = w_f.shape[1]
    vmem = pl.BlockSpec(memory_space=pltpu.VMEM)
    hbm = pl.BlockSpec(memory_space=pl.ANY)
    given = dict(
        tokens=tokens,
        cot=cot,
        g1=g1.reshape(6, LANES),
        w_i=w_in.T,
        w_f=w_f.T,
        w_o=w_o.T,
        gap=gap.reshape(1, ch),
        phase=phase.reshape(1, ch),
        gg=gg.reshape(1, 2 * ch),
        w_mix=w_mix,
        g2=g2.reshape(6, LANES),
        wg=wg.reshape(8, 96, 384),
        wu=wu.reshape(8, 96, 384),
        wd=wd.reshape(8, 48, D),
    )
    small = ("g1", "g2", "gap", "phase", "gg", "vec")
    shape = jax.ShapeDtypeStruct
    raw = dict(
        mixed=shape((T, D), BF),
        tok=shape((T, D), F32),
        o_mlp=shape((2, 8, 144, 384), BF),
        o_early=shape((2, 8, 48, 384), BF),
        o_late=shape((2, 8, 48, 384), BF),
        vec=shape((16, LANES), F32),
    )
    scratch = scratch_list(nd, nt_, T)
    mixed, tok, o_mlp, o_early, o_late, vec = pl.pallas_call(
        functools.partial(kernel, nd, nt_, T, list(given) + list(raw) + list(scratch)),
        out_shape=list(raw.values()),
        in_specs=[vmem if k in small else hbm for k in given],
        out_specs=[vmem if k in small else hbm for k in raw],
        scratch_shapes=list(scratch.values()),
        compiler_params=pltpu.CompilerParams(
            collective_id=0, has_side_effects=True, vmem_limit_bytes=63 * 2**20
        ),
        name="layer",
    )(*given.values())

    got = dict(mixed_in=mixed, tok_in=tok, mlp=o_mlp, early=o_early, late=o_late, vec=vec)
    final = dict(
        mixed=shape((T, D), BF),
        tok=shape((T, D), F32),
        gn1=shape((6, LANES), F32),
        g_in=shape((4, 48, D), F32),
        g_f=shape((2, 48, D), F32),
        g_o=shape((4, 48, D), F32),
        gap=shape((1, ch), F32),
        phase=shape((1, ch), F32),
        group=shape((1, 2 * ch), F32),
        g_x=shape((4, 48, D), F32),
        gn2=shape((6, LANES), F32),
        g_g=shape((8, 96, 384), F32),
        g_u=shape((8, 96, 384), F32),
        g_d=shape((8, 48, D), F32),
    )
    held = dict(
        L=pltpu.VMEM((2, 8, 48, 384), BF),
        E=pltpu.VMEM((2, 8, 48, 384), BF),
        M=pltpu.VMEM((2, 8, 144, 384), BF),
        MX=pltpu.VMEM((T, D), BF),
        TK=pltpu.VMEM((T, D), F32),
        LF=pltpu.VMEM((6, 48, D), F32),
        EF=pltpu.VMEM((8, 48, D), F32),
        GF=pltpu.VMEM((2, 8, 96, 384), F32),
        DF=pltpu.VMEM((8, 48, D), F32),
        sem=pltpu.SemaphoreType.DMA((15,)),
    )
    blocky = ("gn1", "gn2", "gap", "phase", "group")
    outs = pl.pallas_call(
        functools.partial(writer, list(got) + list(final) + list(held)),
        out_shape=list(final.values()),
        in_specs=[vmem if k == "vec" else hbm for k in got],
        out_specs=[vmem if k in blocky else hbm for k in final],
        scratch_shapes=list(held.values()),
        compiler_params=pltpu.CompilerParams(vmem_limit_bytes=62 * 2**20),
        name="writer",
    )(*got.values())
    o = dict(zip(final, outs))
    return (
        o["mixed"],
        o["tok"],
        o["gn1"].reshape(D),
        o["g_in"].reshape(2 * ch, D).T,
        o["g_f"].reshape(ch, D).T,
        o["g_o"].reshape(2 * ch, D).T,
        o["gap"].reshape(ch),
        o["phase"].reshape(ch),
        o["group"].reshape(2 * ch),
        o["g_x"].reshape(2 * ch, D),
        o["gn2"].reshape(D),
        o["g_g"].reshape(D, 384),
        o["g_u"].reshape(D, 384),
        o["g_d"].reshape(384, D),
    )


def solution(mesh):
    in_specs = (
        P("dp", None),
        P("dp", None),
        P(),
        P(None, "tp"),
        P(None, "tp"),
        P(None, "tp"),
        P("tp"),
        P("tp"),
        P("tp"),
        P("tp", None),
        P(),
        P(None, "tp"),
        P(None, "tp"),
        P("tp", None),
    )
    out_specs = (
        P("dp", None),
        P("dp", None),
        P(),
        P(None, "tp"),
        P(None, "tp"),
        P(None, "tp"),
        P("tp"),
        P("tp"),
        P("tp"),
        P("tp", None),
        P(),
        P(None, "tp"),
        P(None, "tp"),
        P("tp", None),
    )
    body = functools.partial(local, mesh.shape["dp"], mesh.shape["tp"])
    return jax.shard_map(body, mesh=mesh, in_specs=in_specs, out_specs=out_specs, check_vma=False)
```

```python
import functools

import jax
import jax.numpy as jnp
from jax import lax
from jax.experimental import pallas as pl
from jax.experimental.pallas import tpu as pltpu
from jax.sharding import PartitionSpec as P

MESH = pl.DeviceIdType.MESH
BF = jnp.bfloat16
F32 = jnp.float32
GROUP = 64
LANES = 128
SENDS = 40


def nn(a, b):
    return jnp.dot(a, b, preferred_element_type=F32)


def nt(a, b):
    return lax.dot_general(a, b, (((1,), (1,)), ((), ())), preferred_element_type=F32)


def tn(a, b):
    return lax.dot_general(a, b, (((0,), (0,)), ((), ())), preferred_element_type=F32)


def exact(a, b, dims):
    return lax.dot_general(
        a, b, (dims, ((), ())), precision=lax.Precision.HIGHEST, preferred_element_type=F32
    )


def cells(shape, axis):
    return lax.broadcasted_iota(jnp.int32, shape, axis)


def one_hot(flags):
    return jnp.where(flags, 1.0, 0.0).astype(BF)


def down_sum(v):
    if v.shape[0] > 8:
        v = jnp.sum(v.reshape(v.shape[0] // 8, 8, v.shape[1]), 0)
    v = v[0:4] + v[4:8]
    v = v[0:2] + v[2:4]
    return v[0:1] + v[1:2]


def power(c, s, n):
    out = None
    while n:
        if n % 2:
            out = (c, s) if out is None else (out[0] * c - out[1] * s, out[0] * s + out[1] * c)
        c, s = c * c - s * s, 2.0 * c * s
        n //= 2
    return out


def sum_buffers(name, nd, rows):
    further = max(1, nd.bit_length() - 4)
    counts = (("", 8), ("0", 4), ("1", 2), ("2", 1), ("E", further), ("F", 8))
    return {name + k: pltpu.VMEM((2, n, rows, 384), BF) for k, n in counts}


def scratch_list(nd, nt_, T):
    dma = pltpu.SemaphoreType.DMA
    return dict(
        RI=pltpu.VMEM((192, 768), BF),
        RF=pltpu.VMEM((96, 768), BF),
        RO=pltpu.VMEM((192, 768), BF),
        RM=pltpu.VMEM((192, 768), BF),
        WI=pltpu.VMEM((2, 8, nt_, 64, 384), BF),
        WX=pltpu.VMEM((2, 4, nt_, 48, 384), BF),
        WM=pltpu.VMEM((2, 8, nt_, 144, 384), BF),
        PAR=pltpu.VMEM((nt_, 8, LANES), F32),
        WRP=pltpu.VMEM((nt_, 640, 768), BF),
        WXP=pltpu.VMEM((nt_, 256, 768), BF),
        X=pltpu.VMEM((T, 768), F32),
        GY=pltpu.VMEM((T, 768), BF),
        LOW=pltpu.VMEM((T, 768), BF),
        ACT=pltpu.VMEM((nt_, T, 640), F32),
        LAM=pltpu.VMEM((nt_, T, LANES), F32),
        BR=pltpu.VMEM((nt_, T, LANES), F32),
        BI=pltpu.VMEM((nt_, T, LANES), F32),
        HR=pltpu.VMEM((nt_, T + 8, LANES), F32),
        HI=pltpu.VMEM((nt_, T + 8, LANES), F32),
        N2=pltpu.VMEM((max(6, 2 * nt_), T, LANES), F32),
        RS=pltpu.VMEM((nt_, T, LANES), F32),
        MIX=pltpu.VMEM((nt_, T, 256), BF),
        RES=pltpu.VMEM((T, 768), F32),
        MID=pltpu.VMEM((T, 768), BF),
        HID=pltpu.VMEM((nt_, T, 384), BF),
        DG=pltpu.VMEM((nt_, T, 768), BF),
        ACC=pltpu.VMEM((nt_, T, 768), F32),
        CH=pltpu.VMEM((3, nt_ * 8, LANES), F32),
        ST=pltpu.VMEM((2, nt_ * 8, LANES), F32),
        EX0=pltpu.VMEM((nd, 16, LANES), F32),
        EX1=pltpu.VMEM((nd, 16, LANES), F32),
        EX2=pltpu.VMEM((nd, 16, LANES), F32),
        EX3=pltpu.VMEM((nd, 16, LANES), F32),
        **sum_buffers("SM", nd, 144),
        **sum_buffers("SE", nd, 48),
        **sum_buffers("SL", nd, 48),
        loc=dma((10,)),
        out=dma((5,)),
        ss=dma((SENDS,)),
        rs=dma((92 + 6 * max(0, nd.bit_length() - 4),)),
        fs=dma((8,)),
        es=dma((4, nd)),
        er=dma((4, nd)),
    )


class Links:
    def __init__(self, ss, rs, fs):
        self.ss, self.rs, self.fs = ss, rs, fs
        self.free, self.received, self.asked = list(range(SENDS)), 0, 0
        self.open, self.old, self.some = [], [], []

    def send(self, src, dst, dev):
        k, n = self.received, self.free.pop(0)
        self.received += 1
        copy = pltpu.make_async_remote_copy(
            src, dst, self.ss.at[n], self.rs.at[k], device_id=dev, device_id_type=MESH
        )
        copy.start()
        self.open.append((copy, n))
        return copy

    def retire(self, copies):
        self.old += [pair for c in copies for pair in self.open if pair[0] is c]
        while len(self.old) > 4:
            pair = self.old.pop(0)
            pair[0].wait_send()
            self.free.append(pair[1])
            self.open = [p for p in self.open if p is not pair]

    def send_if(self, flag, k, src, dst, dev):
        n = self.asked
        self.asked += 1
        copy = pltpu.make_async_remote_copy(
            src, dst, self.fs.at[n], self.rs.at[k], device_id=dev, device_id_type=MESH
        )

        @pl.when(flag)
        def _():
            copy.start()

        self.some.append((flag, copy))
        return copy

    def drain(self):
        for copy, _ in self.open:
            copy.wait_send()
        for flag, copy in self.some:
            pl.when(flag)(copy.wait_send)


def kernel(nd, nt_, T, names, *refs):
    r = dict(zip(names, refs))
    me, z = lax.axis_index("dp"), lax.axis_index("tp")
    steps = T // 8
    ch = r["w_f"].shape[0]
    blocks = list(range(nt_))

    def flip(bit):
        return me + bit - 2 * bit * ((me // bit) % 2)

    bits = (me % 2, (me // 2) % 2, (me // 4) % 2)
    order = ((1, 2), (2, 1))
    place = [bits[0] * 4 + bits[f] * 2 + bits[s] for f, s in order]
    wide = [bits[0] * 2 + bits[f] for f, s in order]
    links = Links(r["ss"], r["rs"], r["fs"])
    away = [0, 1, 3, 2] if nt_ == 4 else blocks

    def slot(k):
        o = lax.rem(k + nt_ - z, nt_)
        if nt_ != 4:
            return o
        return jnp.where(o == 2, 3, jnp.where(o == 3, 2, o))

    barrier = pltpu.get_barrier_semaphore()

    def greet_dp(o, c):
        pl.semaphore_signal(barrier, 1, device_id=(lax.rem(me + o, nd), z), device_id_type=MESH)
        return c

    def greet_tp(o, c):
        pl.semaphore_signal(barrier, 1, device_id=(me, lax.rem(z + o, nt_)), device_id_type=MESH)
        return c

    lax.fori_loop(1, nt_, greet_tp, 0)
    lax.fori_loop(1, nd, greet_dp, 0)

    WM = r["WM"]
    COT = r["DG"].at[nt_ - 1]
    loads = {}
    for k, (name, src, dst) in enumerate(
        (
            ("w_i", r["w_i"], r["RI"]),
            ("w_f", r["w_f"], r["RF"]),
            ("w_o", r["w_o"], r["RO"]),
            ("tokens", r["tokens"], r["MID"]),
            ("w_x", r["w_mix"], r["RM"]),
            ("g", r["wg"], WM.at[0, :, 0, 0:96, :]),
            ("u", r["wu"], WM.at[1, :, 0, 0:96, :]),
            ("d0", r["wd"].at[:, :, 0:384], WM.at[0, :, 0, 96:144, :]),
            ("d1", r["wd"].at[:, :, 384:768], WM.at[1, :, 0, 96:144, :]),
            ("cot", r["cot"], COT),
        )
    ):
        loads[name] = pltpu.make_async_copy(src, dst, r["loc"].at[k])
        loads[name].start()

    WI, WX, WRP, WXP, PAR = r["WI"], r["WX"], r["WRP"], r["WXP"], r["PAR"]
    rows, cols = cells((2 * ch, 2 * ch), 0), cells((2 * ch, 2 * ch), 1)
    apart = one_hot(cols == jnp.where(rows < ch, 2 * rows, 2 * (rows - ch) + 1))
    for k in ("w_i", "w_f", "w_o"):
        loads[k].wait()
    turned = jnp.concatenate(
        [
            nn(apart, r["RI"][...]).astype(BF),
            r["RF"][...],
            nn(apart, r["RO"][...]).astype(BF),
            jnp.zeros((32, 768), BF),
        ],
        axis=0,
    )
    for h in range(2):
        for p in range(8):
            WI[h, p, 0] = turned[64 * p : 64 * p + 64, 384 * h : 384 * h + 384]
    PAR[0] = jnp.zeros((8, LANES), F32)
    PAR[0, 0:1, 0:ch] = r["gap"][...]
    PAR[0, 1:2, 0:ch] = r["phase"][...]
    gains = exact(
        jnp.broadcast_to(r["gg"][...], (8, 2 * ch)), apart.astype(F32), ((1,), (1,))
    )
    PAR[0, 2:3, 0:ch] = gains[0:1, 0:ch]
    PAR[0, 3:4, 0:ch] = gains[0:1, ch : 2 * ch]

    def across(o):
        return (me, lax.rem(z + nt_ - o, nt_))

    def partner(b):
        return (flip(1 << b), z)

    class Unit:
        def __init__(self, buf, slots, portions, far=None):
            self.buf, self.slots, self.portions, self.far = buf, slots, portions, far
            self.at = place if portions == 8 else wide
            self.todo = []

        def wait(self):
            for copy in self.todo:
                copy.wait_recv()
            links.retire(self.todo)
            self.todo = []

        def hop(self, h, b, start, count):
            part = self.buf.at[h, pl.ds(start, count), pl.ds(self.slots[0], len(self.slots))]
            self.todo.append(links.send(part, part, partner(b)))

        def held(self, h, s):
            if self.far is None:
                return self.buf.at[h, self.at[h], s]
            return self.buf.at[h, pl.ds(bits[0] * 4 + bits[order[h][0]] * 2, 2), s]

        def z(self):
            for s in self.slots:
                for h in range(2):
                    own, to = self.held(h, 0), self.held(h, s)
                    if self.far is None or nt_ != 4:
                        self.todo.append(links.send(own, to, across(away[s])))
                    else:
                        k = links.received
                        links.received += 1
                        flag = z != (0 if s == 1 else 3)
                        self.todo.append(links.send_if(flag, k, own, to, across(away[s])))
                        self.first = k - h

        def forward(self):
            if nt_ != 4:
                return
            s = self.slots[0]
            who, end = (2, 3) if s == 1 else (1, 0)
            for h in range(2):
                held, to = self.held(h, self.far), self.held(h, s)
                links.send_if(z == who, self.first + h, held, to, (me, end))

        def s(self):
            self.wait()
            for h in range(2):
                f, s = order[h]
                if self.portions == 8:
                    self.hop(h, s, place[h], 1)
                else:
                    self.hop(h, f, wide[h], 1)

        def f(self):
            self.wait()
            for h in range(2):
                f, s = order[h]
                self.hop(h, f, bits[0] * 4 + bits[f] * 2, 2)

        def c(self):
            self.wait()
            n = self.portions // 2
            for h in range(2):
                self.hop(h, 0, bits[0] * n, n)

    I1, I2 = Unit(WI, blocks[1:3], 8), Unit(WI, blocks[3:], 8)
    XM = Unit(WX, blocks[1:], 4)
    M1, M2, M3 = Unit(WM, [1], 8, 3), Unit(WM, [2], 8, 3), Unit(WM, [3], 8)

    pl.semaphore_wait(barrier, nd - 1 + nt_ - 1)
    I1.z()
    par_copies = [links.send(PAR.at[0], PAR.at[s], across(away[s])) for s in blocks[1:]]

    PERM, X, GY, LOW = r["N2"], r["X"], r["GY"], r["LOW"]
    loads["tokens"].wait()
    tiles = [slice(LANES * i, LANES * i + LANES) for i in range(6)]
    for i in range(6):
        PERM[i] = r["MID"][:, tiles[i]].astype(F32)

    def take(k, c):
        for i in range(6):
            X[pl.ds(pl.multiple_of(8 * k, 8), 8), tiles[i]] = PERM[i, pl.ds(k, 8, stride=steps), :]
        return c

    lax.fori_loop(0, steps, take, 0, unroll=4)

    def whole_row(ref):
        return jnp.concatenate([ref[i : i + 1, :] for i in range(6)], axis=1)

    gain1, gain2 = whole_row(r["g1"]), whole_row(r["g2"])

    def norm_rows(src, gain, dst):
        def body(i, c):
            at = pl.ds(pl.multiple_of(i * 128, 128), 128)
            v = src[at, :]
            q = lax.rsqrt(jnp.mean(v * v, -1, keepdims=True) + 1e-06)
            dst[at, :] = (v * q * gain).astype(BF)
            return c

        lax.fori_loop(0, T // 128, body, 0)

    norm_rows(X, gain1, LOW)
    I2.z()
    for k in ("g", "u", "d0", "d1", "cot"):
        loads[k].wait()
    M3.z()

    for k in blocks:
        for g in range(5):
            WRP[k, g * 128 + 96 : g * 128 + 128, :] = jnp.zeros((32, 768), BF)
        for g in range(2):
            WXP[k, g * 128 + 96 : g * 128 + 128, :] = jnp.zeros((32, 768), BF)

    def spread_in(k):
        for g in range(5):
            for q in range(3):
                row = g * 96 + q * 32
                for h in range(2):
                    WRP[k, g * 128 + q * 32 : g * 128 + q * 32 + 32, 384 * h : 384 * h + 384] = WI[
                        h, row // 64, k, row % 64 : row % 64 + 32, :
                    ]

    def spread_mix(k):
        for p in range(4):
            row = (p // 2) * 128 + (p % 2) * 48
            for h in range(2):
                WXP[k, row : row + 48, 384 * h : 384 * h + 384] = WX[h, p, k]

    ACT, LAM, BR, BI = r["ACT"], r["LAM"], r["BR"], r["BI"]

    def project(k):
        spread_in(k)
        gap = PAR[k, 0:1, :]
        ACT[k] = nt(LOW[...], WRP[k])
        ur, ui, fg = ACT[k, :, 0:128], ACT[k, :, 128:256], ACT[k, :, 256:384]
        leak = gap * jax.nn.sigmoid(-fg)
        LAM[k] = 1.0 - leak
        BR[k] = leak * (ur * jax.nn.sigmoid(ur))
        BI[k] = leak * (ui * jax.nn.sigmoid(ui))

    loads["w_x"].wait()
    mixed_rows = nn(apart, r["RM"][...]).astype(BF)
    for h in range(2):
        for p in range(4):
            WX[h, p, 0] = mixed_rows[48 * p : 48 * p + 48, 384 * h : 384 * h + 384]
    spread_mix(0)
    I1.s()
    project(0)
    I1.f()
    M1.z()
    M2.z()
    I2.s()

    for i in range(6):
        PERM[i] = COT[:, tiles[i]].astype(F32)

    def take_cot(k, c):
        for i in range(6):
            two = [PERM[i, pl.ds(2 * k + j, 8, stride=steps), :] for j in range(2)]
            GY[pl.ds(pl.multiple_of(16 * k, 16), 16), tiles[i]] = jnp.concatenate(two, axis=0).astype(BF)
        return c

    lax.fori_loop(0, steps // 2, take_cot, 0, unroll=2)
    I1.c()
    I2.f()
    XM.z()
    for copy in par_copies:
        copy.wait_recv()
    I1.wait()
    lax.fori_loop(1, 3, lambda k, c: (project(k), c)[1], 0)
    M3.s()
    I2.c()
    I2.wait()
    project(3)
    M3.f()
    M1.forward()
    M2.forward()

    CH, ST, HR, HI = r["CH"], r["ST"], r["HR"], r["HI"]
    turn = []
    for k in blocks:
        ph = PAR[k, 1:2, :]
        turn.append((jnp.cos(ph), jnp.sin(ph)))
    turn8 = [(jnp.broadcast_to(c, (8, LANES)), jnp.broadcast_to(s, (8, LANES))) for c, s in turn]
    cos4 = jnp.concatenate([c for c, s in turn], axis=0)
    sin4 = jnp.concatenate([s for c, s in turn], axis=0)
    chunk_c, chunk_s = power(cos4, sin4, steps)
    whole_c, whole_s = power(cos4, sin4, T)
    zero8 = jnp.zeros((8, LANES), F32)
    zero4 = jnp.zeros((nt_, LANES), F32)

    def rows_of(k):
        return pl.ds(pl.multiple_of(8 * k, 8), 8)

    def ends(n, carry):
        out = []
        for k in blocks:
            hr, hi, lp = carry[k]
            c, s = turn8[k]
            lam = LAM[k, rows_of(n), :]
            nr = lam * (c * hr - s * hi) + BR[k, rows_of(n), :]
            ni = lam * (c * hi + s * hr) + BI[k, rows_of(n), :]
            out.append((nr, ni, lp * lam))
        return tuple(out)

    last = lax.fori_loop(0, steps, ends, tuple((zero8, zero8, zero8 + 1.0) for k in blocks), unroll=4)
    for k in blocks:
        CH[0, 8 * k : 8 * k + 8, :] = last[k][2]
        CH[1, 8 * k : 8 * k + 8, :] = last[k][0]
        CH[2, 8 * k : 8 * k + 8, :] = last[k][1]

    def chunk(i, c):
        return CH[i, pl.ds(c, nt_, stride=8), :]

    def chain(sr, si, sign, keep):
        for c in range(8) if sign > 0 else range(7, -1, -1):
            if keep:
                ST[0, pl.ds(c, nt_, stride=8), :] = sr
                ST[1, pl.ds(c, nt_, stride=8), :] = si
            lp = chunk(0, c)
            pr, pi = lp * chunk_c, sign * (lp * chunk_s)
            sr, si = pr * sr - pi * si + chunk(1, c), pr * si + pi * sr + chunk(2, c)
        return sr, si

    whole_lam = chunk(0, 0)
    for c in range(1, 8):
        whole_lam = whole_lam * chunk(0, c)

    def exchange(which, buf, start):
        def copy_of(o, back):
            at = lax.rem(me + nd - o, nd) if back else lax.rem(me + o, nd)
            row = at if back else me
            return pltpu.make_async_remote_copy(
                buf.at[row],
                buf.at[row],
                r["es"].at[which, o],
                r["er"].at[which, o],
                device_id=(at, z),
                device_id_type=MESH,
            )

        def go(o, c):
            copy_of(o, False).start()
            return c

        def arrive(o, c):
            copy_of(o, True).wait_recv()
            return c

        def leave(o, c):
            copy_of(o, False).wait_send()
            return c

        lax.fori_loop(1, nd, {"go": go, "arrive": arrive, "leave": leave}[start], 0)

    def post(buf, which, sr, si):
        buf[me, 0:4, :] = whole_lam
        buf[me, 4:8, :] = sr
        buf[me, 8:12, :] = si
        buf[me, 12:16, :] = zero4
        exchange(which, buf, "go")

    def carried(buf, which, sign):
        exchange(which, buf, "arrive")

        def lap(k, s):
            at = k if sign > 0 else nd - 1 - k
            reached = (at < me) if sign > 0 else (at > me)
            lp = buf[at, 0:4, :]
            pr, pi = lp * whole_c, sign * (lp * whole_s)
            nr = pr * s[0] - pi * s[1] + buf[at, 4:8, :]
            ni = pr * s[1] + pi * s[0] + buf[at, 8:12, :]
            return jnp.where(reached, nr, s[0]), jnp.where(reached, ni, s[1])

        return lax.fori_loop(0, nd, lap, (zero4, zero4))

    post(r["EX0"], 0, *chain(zero4, zero4, 1.0, False))
    XM.s()
    start = carried(r["EX0"], 0, 1.0)
    chain(start[0], start[1], 1.0, True)
    for k in blocks:
        HR[k, 0:8, :] = ST[0, 8 * k : 8 * k + 8, :]
        HI[k, 0:8, :] = ST[1, 8 * k : 8 * k + 8, :]

    def states(n, carry):
        out = []
        for k in blocks:
            hr, hi = carry[k]
            c, s = turn8[k]
            lam = LAM[k, rows_of(n), :]
            nr = lam * (c * hr - s * hi) + BR[k, rows_of(n), :]
            ni = lam * (c * hi + s * hr) + BI[k, rows_of(n), :]
            HR[k, rows_of(n + 1), :] = nr
            HI[k, rows_of(n + 1), :] = ni
            out.append((nr, ni))
        return tuple(out)

    def held(k):
        return ST[0, 8 * k : 8 * k + 8, :], ST[1, 8 * k : 8 * k + 8, :]

    lax.fori_loop(0, steps, states, tuple(held(k) for k in blocks), unroll=4)
    M3.c()
    M1.f()
    M2.f()
    XM.c()

    half = GROUP // 2
    same = one_hot(cells((LANES, LANES), 0) // half == cells((LANES, LANES), 1) // half)

    def group_mean(v):
        top = v.astype(BF)
        rest = (v - top.astype(F32)).astype(BF)
        return (nn(top, same) + nn(rest, same)) * (1.0 / GROUP)

    NR, NI = r["N2"].at[pl.ds(0, nt_)], r["N2"].at[pl.ds(nt_, nt_)]
    RS, MIX = r["RS"], r["MIX"]

    def normalise(k, c):
        hr, hi = HR[k, pl.ds(8, T), :], HI[k, pl.ds(8, T), :]
        mean = group_mean(hr + hi)
        hr, hi = hr - mean, hi - mean
        rstd = lax.rsqrt(group_mean(hr * hr + hi * hi) + 1e-05)
        RS[k] = rstd
        hr, hi = hr * rstd, hi * rstd
        NR[k] = hr
        NI[k] = hi
        gr, gi = ACT[k, :, 384:512], ACT[k, :, 512:640]
        MIX[k, :, 0:128] = (hr * PAR[k, 2:3, :] * (gr * jax.nn.sigmoid(gr))).astype(BF)
        MIX[k, :, 128:256] = (hi * PAR[k, 3:4, :] * (gi * jax.nn.sigmoid(gi))).astype(BF)
        return c

    lax.fori_loop(0, nt_, normalise, 0)
    XM.wait()
    lax.fori_loop(1, nt_, lambda k, c: (spread_mix(k), c)[1], 0)

    RES, MID = r["RES"], r["MID"]

    def mix_in(i, c):
        at = pl.ds(pl.multiple_of(i * 256, 256), 256)
        total = nn(MIX[slot(0), at, :], WXP[slot(0)])
        for k in blocks[1:]:
            total = total + nn(MIX[slot(k), at, :], WXP[slot(k)])
        RES[at, :] = X[at, :] + total
        return c

    lax.fori_loop(0, T // 256, mix_in, 0)
    norm_rows(RES, gain2, MID)

    HID, DG = r["HID"], r["DG"]

    def gate_w(k, h):
        return WM[h, :, pl.ds(k, 1), 0:96, :].reshape(768, 384)

    def down_w(k, h):
        return WM[h, :, pl.ds(k, 1), 96:144, :].reshape(384, 384)

    def swiglu(k):
        def tile(i, c):
            at = pl.ds(pl.multiple_of(i * 256, 256), 256)
            ga = nn(MID[at, :], gate_w(k, 0))
            ua = nn(MID[at, :], gate_w(k, 1))
            gh = nt(GY[at, 0:384], down_w(k, 0)) + nt(GY[at, 384:768], down_w(k, 1))
            s = jax.nn.sigmoid(ga)
            sl = ga * s
            HID[k, at, :] = (sl * ua).astype(BF)
            DG[k, at, 0:384] = (gh * ua * (s * (1.0 + ga * (1.0 - s)))).astype(BF)
            DG[k, at, 384:768] = (gh * sl).astype(BF)
            return c

        lax.fori_loop(0, T // 256, tile, 0)

    swiglu(0)
    SM = r["SM"]
    for h in range(2):
        SM[h, :, 0:96, :] = (
            tn(MID[...], DG[0, :, 384 * h : 384 * h + 384]).astype(BF).reshape(8, 96, 384)
        )
        SM[h, :, 96:144, :] = (
            tn(HID[0], GY[:, 384 * h : 384 * h + 384]).astype(BF).reshape(8, 48, 384)
        )

    class Summed:
        def __init__(self, name):
            self.bufs = [r[name + k] for k in ("", "0", "1", "2")]
            self.further, self.whole = r[name + "E"], r[name + "F"]
            self.todo = []

        def stage(self, n):
            for copy in self.todo:
                copy.wait_recv()
            links.retire(self.todo)
            self.todo = []
            S = self.bufs[0]
            for h in range(2):
                f, s = order[h]
                spans = ((0, 0, 4), (f, bits[0] * 4, 2), (s, bits[0] * 4 + bits[f] * 2, 1))
                if 1 <= n <= 3:
                    b, first, count = spans[n - 1]
                    mine = pl.ds(first + bits[b] * count, count)
                    S[h, mine] = (S[h, mine].astype(F32) + self.bufs[n][h].astype(F32)).astype(BF)
                if n == 3:
                    part = pl.ds(place[h], 1)
                    for b in range(3, nd.bit_length() - 1):
                        land = self.further.at[h, pl.ds(b - 3, 1)]
                        one = links.send(S.at[h, part], land, partner(b))
                        one.wait_recv()
                        one.wait_send()
                        links.free.append(links.open.pop()[1])
                        S[h, part] = (
                            S[h, part].astype(F32) + self.further[h, b - 3 : b - 2].astype(F32)
                        ).astype(BF)
                    self.whole[h, part] = S[h, part]
                if n < 3:
                    b, first, count = spans[n]
                    give = first + (1 - bits[b]) * count
                    self.todo.append(
                        links.send(S.at[h, pl.ds(give, count)], self.bufs[n + 1].at[h], partner(b))
                    )
                elif n < 6:
                    b, first, count = (
                        (s, place[h], 1),
                        (f, bits[0] * 4 + bits[f] * 2, 2),
                        (0, bits[0] * 4, 4),
                    )[n - 3]
                    part = self.whole.at[h, pl.ds(first, count)]
                    self.todo.append(links.send(part, part, partner(b)))

    finals = []

    def put_out(src, dst):
        copy = pltpu.make_async_copy(src, dst, r["out"].at[len(finals)])
        copy.start()
        finals.append(copy)

    ACC = r["ACC"]
    NAT, GRES = ACC.at[0], ACC.at[1]

    def back_mid(k):
        ACC[k] = nt(DG[k, :, 0:384], gate_w(k, 0)) + nt(DG[k, :, 384:768], gate_w(k, 1))

    mlp_sum, early_sum, late_sum = Summed("SM"), Summed("SE"), Summed("SL")
    mlp_sum.stage(0)
    back_mid(0)
    M1.c()
    M2.c()
    M3.wait()
    swiglu(3)
    back_mid(3)
    M1.wait()
    mlp_sum.stage(1)
    swiglu(1)
    back_mid(1)
    M2.wait()
    swiglu(2)
    back_mid(2)

    LOWR = r["MID"]

    def back_second(i, total):
        at = pl.ds(pl.multiple_of(i * 128, 128), 128)
        res, gmid = RES[at, :], ACC[slot(0), at, :]
        for k in blocks[1:]:
            gmid = gmid + ACC[slot(k), at, :]
        q2 = lax.rsqrt(jnp.mean(res * res, -1, keepdims=True) + 1e-06)
        p = gmid * gain2
        back = q2 * p - res * (q2 * q2 * q2) * jnp.mean(p * res, -1, keepdims=True)
        gres = GY[at, :].astype(F32) + back
        GRES[at, :] = gres
        LOWR[at, :] = gres.astype(BF)
        return total + jnp.sum((gmid * res * q2).reshape(16, 8, 768), 0)

    VEC = r["EX3"]
    gnorm2 = down_sum(lax.fori_loop(0, T // 128, back_second, jnp.zeros((8, 768), F32)))
    for i in range(6):
        VEC[me, 6 + i : 7 + i, :] = gnorm2[:, 128 * i : 128 * i + 128]

    G = DG
    rows, cols = cells((256, 256), 0), cells((256, 256), 1)
    lane = rows % 128
    together = one_hot((cols == 2 * lane + rows // 128) & (lane < ch))

    def back_norm(k, own):
        gact = nt(LOWR[...], WXP[k])
        rstd = RS[k]
        parts, sums, dots = [], 0.0, 0.0
        group = []
        for i, hn in enumerate((NR[k], NI[k])):
            pre = ACT[k, :, 384 + 128 * i : 512 + 128 * i]
            gain = PAR[k, 2 + i : 3 + i, :]
            ga = gact[:, 128 * i : 128 * i + 128]
            s = jax.nn.sigmoid(pre)
            sl = pre * s
            gh = ga * hn
            G[k, :, 384 + 128 * i : 512 + 128 * i] = (
                gh * gain * (s * (1.0 + pre * (1.0 - s)))
            ).astype(BF)
            if own:
                group.append(down_sum(gh * sl))
            p = ga * gain * sl
            parts.append((p, hn))
            sums = sums + p
            dots = dots + p * hn
        sums, dots = group_mean(sums), group_mean(dots)
        for buf, (p, hn) in zip((BR, BI), parts):
            buf[k] = rstd * (p - sums - hn * dots)
        if own:
            both = jnp.broadcast_to(jnp.concatenate(group, axis=1), (8, 256))
            both = exact(both, together.astype(F32), ((1,), (0,)))
            VEC[me, 14:15, :] = both[0:1, 0:128]
            VEC[me, 15:16, :] = both[0:1, 128:256]

    def back_step(n, carry, some, keep):
        n = steps - 1 - n
        out = []
        for k, (ur, ui) in zip(some, carry):
            c, s = turn8[k]
            lam = LAM[k, rows_of(n), :]
            er = BR[k, rows_of(n), :] + ur
            ei = BI[k, rows_of(n), :] + ui
            if keep:
                BR[k, rows_of(n), :] = er
                BI[k, rows_of(n), :] = ei
            out.append((lam * (c * er + s * ei), lam * (c * ei - s * er)))
        return tuple(out)

    def back_ends(some, buf, which):
        body = functools.partial(back_step, some=some, keep=False)
        first = lax.fori_loop(0, steps, body, tuple((zero8, zero8) for k in some), unroll=4)
        for k, (ur, ui) in zip(some, first):
            CH[1, 8 * k : 8 * k + 8, :] = ur
            CH[2, 8 * k : 8 * k + 8, :] = ui
        post(buf, which, *chain(zero4, zero4, -1.0, False))

    def back_states(some, buf, which):
        sr, si = carried(buf, which, -1.0)
        chain(sr, si, -1.0, True)
        body = functools.partial(back_step, some=some, keep=True)
        lax.fori_loop(0, steps, body, tuple(held(k) for k in some), unroll=4)

    def back_gates(k, own):
        c, s = turn[k]
        er, ei = BR[k], BI[k]
        hr, hi = HR[k, pl.ds(0, T), :], HI[k, pl.ds(0, T), :]
        gap = PAR[k, 0:1, :]
        gar, gai = er * hr + ei * hi, ei * hr - er * hi
        ur, ui, fg = ACT[k, :, 0:128], ACT[k, :, 128:256], ACT[k, :, 256:384]
        su, si, sf = jax.nn.sigmoid(ur), jax.nn.sigmoid(ui), jax.nn.sigmoid(-fg)
        leak = gap * sf
        gleak = er * (ur * su) + ei * (ui * si) - (c * gar + s * gai)
        G[k, :, 0:128] = (er * leak * (su * (1.0 + ur * (1.0 - su)))).astype(BF)
        G[k, :, 128:256] = (ei * leak * (si * (1.0 + ui * (1.0 - si)))).astype(BF)
        G[k, :, 256:384] = (-gleak * leak * (1.0 - sf)).astype(BF)
        if own:
            VEC[me, 12:13, :] = down_sum(gleak * sf)
            VEC[me, 13:14, :] = down_sum((1.0 - leak) * (c * gai - s * gar))

    back_norm(0, True)
    back_ends([0], r["EX1"], 1)

    SE, SL = r["SE"], r["SL"]
    gate_cols = nn(G[0, :, 384:640], together)[:, 0 : 2 * ch].astype(BF)
    mix_cols = nn(MIX[0], together)[:, 0 : 2 * ch].astype(BF)
    for h in range(2):
        at = slice(384 * h, 384 * h + 384)
        SE[h, 0:4] = tn(gate_cols, LOW[:, at]).astype(BF).reshape(4, 48, 384)
        SE[h, 4:8] = tn(mix_cols, LOWR[:, at]).astype(BF).reshape(4, 48, 384)
    early_sum.stage(0)
    mlp_sum.stage(2)
    lax.fori_loop(1, nt_, lambda k, c: (back_norm(k, False), c)[1], 0)
    early_sum.stage(1)
    back_ends(blocks[1:], r["EX2"], 2)
    back_states([0], r["EX1"], 1)
    back_gates(0, True)
    rows, cols = cells((384, 384), 0), cells((384, 384), 1)
    lane, g = rows % 128, rows // 128
    to = jnp.where(g < 2, 2 * lane + g, 2 * ch + lane)
    late_cols = nn(G[0, :, 0:384], one_hot((cols == to) & (lane < ch))).astype(BF)
    for h in range(2):
        SL[h] = tn(late_cols, LOW[:, 384 * h : 384 * h + 384]).astype(BF).reshape(8, 48, 384)
    late_sum.stage(0)
    mlp_sum.stage(3)

    back_states(blocks[1:], r["EX2"], 2)
    late_sum.stage(1)
    early_sum.stage(2)
    mlp_sum.stage(4)
    for k in blocks[1:]:
        back_gates(k, False)
    early_sum.stage(3)
    late_sum.stage(2)

    def back_in(k, c):
        NAT[...] += nn(G[slot(k), :, 0:640], WRP[slot(k)])
        return c

    NAT[...] = nn(G[slot(0), :, 0:640], WRP[slot(0)])
    lax.fori_loop(1, nt_ // 2, back_in, 0)
    late_sum.stage(3)
    lax.fori_loop(nt_ // 2, nt_, back_in, 0)
    mlp_sum.stage(5)
    early_sum.stage(4)

    def back_first(i, total):
        at = pl.ds(pl.multiple_of(i * 128, 128), 128)
        x, gin = X[at, :], NAT[at, :]
        q1 = lax.rsqrt(jnp.mean(x * x, -1, keepdims=True) + 1e-06)
        p = gin * gain1
        GRES[at, :] += q1 * p - x * (q1 * q1 * q1) * jnp.mean(p * x, -1, keepdims=True)
        return total + jnp.sum((gin * x * q1).reshape(16, 8, 768), 0)

    gnorm1 = down_sum(lax.fori_loop(0, T // 128, back_first, jnp.zeros((8, 768), F32)))
    for i in range(6):
        VEC[me, i : i + 1, :] = gnorm1[:, 128 * i : 128 * i + 128]
    exchange(3, VEC, "go")
    late_sum.stage(4)

    def put_from(buf):
        def put(k, c):
            for i in range(6):
                PERM[i, pl.ds(k, 8, stride=steps), :] = buf[pl.ds(pl.multiple_of(8 * k, 8), 8), tiles[i]]
            return c

        lax.fori_loop(0, steps, put, 0, unroll=4)

    put_from(GRES)
    for i in range(6):
        NAT[:, tiles[i]] = PERM[i]
    put_out(NAT, r["tok"])
    mlp_sum.stage(6)
    put_out(r["SMF"], r["o_mlp"])

    def down(k, c):
        j = slot(k)
        for h in range(2):
            RES[:, 384 * h : 384 * h + 384] += nn(HID[j], down_w(j, h))
        return c

    lax.fori_loop(0, nt_, down, 0)
    late_sum.stage(5)
    early_sum.stage(5)
    put_from(RES)
    for i in range(6):
        COT[:, tiles[i]] = PERM[i].astype(BF)
    put_out(COT, r["mixed"])
    late_sum.stage(6)
    put_out(r["SLF"], r["o_late"])
    early_sum.stage(6)
    put_out(r["SEF"], r["o_early"])

    exchange(3, VEC, "arrive")
    total = VEC[0]
    for k in range(1, nd):
        total = total + VEC[k]
    r["vec"][...] = total
    for which in range(4):
        exchange(which, r["EX%d" % which], "leave")
    links.drain()
    for copy in finals:
        copy.wait()


def writer(names, *refs):
    r = dict(zip(names, refs))
    sem = r["sem"]
    count = [0]

    def copy(src, dst):
        c = pltpu.make_async_copy(src, dst, sem.at[count[0]])
        count[0] += 1
        c.start()
        return c

    ins = {}
    for name, src, dst in (
        ("tok", "tok_in", "TK"),
        ("mlp", "mlp", "M"),
        ("mixed", "mixed_in", "MX"),
        ("early", "early", "E"),
        ("late", "late", "L"),
    ):
        ins[name] = copy(r[src], r[dst])
    outs = []
    ins["tok"].wait()
    outs.append(copy(r["TK"], r["tok"]))
    ins["mlp"].wait()
    for h, name in ((0, "g_g"), (1, "g_u")):
        r["GF"][h] = r["M"][h, :, 0:96, :].astype(F32)
        outs.append(copy(r["GF"].at[h], r[name]))
    ins["mixed"].wait()
    outs.append(copy(r["MX"], r["mixed"]))
    for h in range(2):
        r["DF"][:, :, 384 * h : 384 * h + 384] = r["M"][h, :, 96:144, :].astype(F32)
    outs.append(copy(r["DF"], r["g_d"]))
    for name, a, f, n, dests in (
        ("early", "E", "EF", 8, (("g_o", 0, 4), ("g_x", 4, 8))),
        ("late", "L", "LF", 6, (("g_in", 0, 4), ("g_f", 4, 6))),
    ):
        ins[name].wait()
        for h in range(2):
            r[f][:, :, 384 * h : 384 * h + 384] = r[a][h, 0:n].astype(F32)
        for dst, p, q in dests:
            outs.append(copy(r[f].at[p:q], r[dst]))
    ch = r["gap"].shape[1]
    vec = r["vec"]
    r["gn1"][...] = vec[0:6, :]
    r["gn2"][...] = vec[6:12, :]
    r["gap"][...] = vec[12:13, 0:ch]
    r["phase"][...] = vec[13:14, 0:ch]
    r["group"][...] = jnp.concatenate([vec[14:15, :], vec[15:16, 0 : 2 * ch - LANES]], axis=1)
    for c in outs:
        c.wait()


def local(nd, nt_, *args):
    (tokens, cot, g1, w_in, w_f, w_o, gap, phase, gg, w_mix, g2, wg, wu, wd) = args
    T, D = tokens.shape
    ch = w_f.shape[1]
    vmem = pl.BlockSpec(memory_space=pltpu.VMEM)
    hbm = pl.BlockSpec(memory_space=pl.ANY)
    given = dict(
        tokens=tokens,
        cot=cot,
        g1=g1.reshape(6, LANES),
        w_i=w_in.T,
        w_f=w_f.T,
        w_o=w_o.T,
        gap=gap.reshape(1, ch),
        phase=phase.reshape(1, ch),
        gg=gg.reshape(1, 2 * ch),
        w_mix=w_mix,
        g2=g2.reshape(6, LANES),
        wg=wg.reshape(8, 96, 384),
        wu=wu.reshape(8, 96, 384),
        wd=wd.reshape(8, 48, D),
    )
    small = ("g1", "g2", "gap", "phase", "gg", "vec")
    shape = jax.ShapeDtypeStruct
    raw = dict(
        mixed=shape((T, D), BF),
        tok=shape((T, D), F32),
        o_mlp=shape((2, 8, 144, 384), BF),
        o_early=shape((2, 8, 48, 384), BF),
        o_late=shape((2, 8, 48, 384), BF),
        vec=shape((16, LANES), F32),
    )
    scratch = scratch_list(nd, nt_, T)
    mixed, tok, o_mlp, o_early, o_late, vec = pl.pallas_call(
        functools.partial(kernel, nd, nt_, T, list(given) + list(raw) + list(scratch)),
        out_shape=list(raw.values()),
        in_specs=[vmem if k in small else hbm for k in given],
        out_specs=[vmem if k in small else hbm for k in raw],
        scratch_shapes=list(scratch.values()),
        compiler_params=pltpu.CompilerParams(
            collective_id=0, has_side_effects=True, vmem_limit_bytes=63 * 2**20
        ),
        name="layer",
    )(*given.values())

    got = dict(mixed_in=mixed, tok_in=tok, mlp=o_mlp, early=o_early, late=o_late, vec=vec)
    final = dict(
        mixed=shape((T, D), BF),
        tok=shape((T, D), F32),
        gn1=shape((6, LANES), F32),
        g_in=shape((4, 48, D), F32),
        g_f=shape((2, 48, D), F32),
        g_o=shape((4, 48, D), F32),
        gap=shape((1, ch), F32),
        phase=shape((1, ch), F32),
        group=shape((1, 2 * ch), F32),
        g_x=shape((4, 48, D), F32),
        gn2=shape((6, LANES), F32),
        g_g=shape((8, 96, 384), F32),
        g_u=shape((8, 96, 384), F32),
        g_d=shape((8, 48, D), F32),
    )
    held = dict(
        L=pltpu.VMEM((2, 8, 48, 384), BF),
        E=pltpu.VMEM((2, 8, 48, 384), BF),
        M=pltpu.VMEM((2, 8, 144, 384), BF),
        MX=pltpu.VMEM((T, D), BF),
        TK=pltpu.VMEM((T, D), F32),
        LF=pltpu.VMEM((6, 48, D), F32),
        EF=pltpu.VMEM((8, 48, D), F32),
        GF=pltpu.VMEM((2, 8, 96, 384), F32),
        DF=pltpu.VMEM((8, 48, D), F32),
        sem=pltpu.SemaphoreType.DMA((15,)),
    )
    blocky = ("gn1", "gn2", "gap", "phase", "group")
    outs = pl.pallas_call(
        functools.partial(writer, list(got) + list(final) + list(held)),
        out_shape=list(final.values()),
        in_specs=[vmem if k == "vec" else hbm for k in got],
        out_specs=[vmem if k in blocky else hbm for k in final],
        scratch_shapes=list(held.values()),
        compiler_params=pltpu.CompilerParams(vmem_limit_bytes=62 * 2**20),
        name="writer",
    )(*got.values())
    o = dict(zip(final, outs))
    return (
        o["mixed"],
        o["tok"],
        o["gn1"].reshape(D),
        o["g_in"].reshape(2 * ch, D).T,
        o["g_f"].reshape(ch, D).T,
        o["g_o"].reshape(2 * ch, D).T,
        o["gap"].reshape(ch),
        o["phase"].reshape(ch),
        o["group"].reshape(2 * ch),
        o["g_x"].reshape(2 * ch, D),
        o["gn2"].reshape(D),
        o["g_g"].reshape(D, 384),
        o["g_u"].reshape(D, 384),
        o["g_d"].reshape(384, D),
    )


def solution(mesh):
    in_specs = (
        P("dp", None),
        P("dp", None),
        P(),
        P(None, "tp"),
        P(None, "tp"),
        P(None, "tp"),
        P("tp"),
        P("tp"),
        P("tp"),
        P("tp", None),
        P(),
        P(None, "tp"),
        P(None, "tp"),
        P("tp", None),
    )
    out_specs = (
        P("dp", None),
        P("dp", None),
        P(),
        P(None, "tp"),
        P(None, "tp"),
        P(None, "tp"),
        P("tp"),
        P("tp"),
        P("tp"),
        P("tp", None),
        P(),
        P(None, "tp"),
        P(None, "tp"),
        P("tp", None),
    )
    body = functools.partial(local, mesh.shape["dp"], mesh.shape["tp"])
    return jax.shard_map(body, mesh=mesh, in_specs=in_specs, out_specs=out_specs, check_vma=False)
```
